128 devices in a mesh: fsdp: 16 (over y, z_hi, core), ctx: 2 (over z_lo), tp: 4 (over x).
Axes of the slice: x: 4, y: 4, z: 4 (z_hi: 2, z_lo: 2; z = z_hi * 2 + z_lo), core: 2. Of those that a mesh axis runs over, the one named last changes fastest.
Arguments:
- inputs: bfloat16 [32, 1024, 1472], P('fsdp', ('ctx', 'tp')), may hold values from -6 to 6
- cotangent: bfloat16 [32, 1024, 1472], P('fsdp', ('ctx', 'tp')), may hold values from -6 to 6
- segment_ids: int32 [32, 1024], P('fsdp'), may hold values from 0 to 8, as said below
- buckets: int32 [2047], replicated, may hold values from 0 to 31
- norm_gain_1: bfloat16 [1472], replicated, may hold values from 0.5 to 1.5
- norm_gain_2: bfloat16 [1472], replicated, may hold values from 0.5 to 1.5
- relative_bias: bfloat16 [32, 6], replicated, may hold values from -4 to 4
- query_weight: bfloat16 [1472, 384], P(None, ('fsdp', 'ctx', 'tp')), may hold values from -0.0625 to 0.0625
- key_weight: bfloat16 [1472, 384], P(None, ('fsdp', 'ctx', 'tp')), may hold values from -0.0625 to 0.0625
- value_weight: bfloat16 [1472, 384], P(None, ('fsdp', 'ctx', 'tp')), may hold values from -0.15625 to 0.15625
- output_weight: bfloat16 [384, 1472], P(('fsdp', 'ctx', 'tp')), may hold values from -1.25 to 1.25
- gate_weight: bfloat16 [1472, 3584], P(('fsdp', 'ctx'), 'tp'), may hold values from -0.15625 to 0.15625
- up_weight: bfloat16 [1472, 3584], P(('fsdp', 'ctx'), 'tp'), may hold values from -0.15625 to 0.15625
- down_weight: bfloat16 [3584, 1472], P('tp', ('fsdp', 'ctx')), may hold values from -0.09375 to 0.09375
Outputs:
- layer_output: float32 [32, 1024, 1472], P('fsdp', ('ctx', 'tp'))
- grad_inputs: float32 [32, 1024, 1472], P('fsdp', ('ctx', 'tp'))
- grad_gain_1: float32 [1472], replicated
- grad_gain_2: float32 [1472], replicated
- grad_bias: float32 [32, 6], replicated
- grad_query: float32 [1472, 384], P(None, ('fsdp', 'ctx', 'tp'))
- grad_key: float32 [1472, 384], P(None, ('fsdp', 'ctx', 'tp'))
- grad_value: float32 [1472, 384], P(None, ('fsdp', 'ctx', 'tp'))
- grad_output: float32 [384, 1472], P(('fsdp', 'ctx', 'tp'))
- grad_gate: float32 [1472, 3584], P(('fsdp', 'ctx'), 'tp')
- grad_up: float32 [1472, 3584], P(('fsdp', 'ctx'), 'tp')
- grad_down: float32 [3584, 1472], P('tp', ('fsdp', 'ctx'))
The draws below stay inside these ranges and needn't reach their ends.
Inputs may be any that keep to these rules, and one draw needn't show every extreme that they name: `segment_ids`: in each sequence the ids start at 1 and never decrease, except for a final run of one or more padding bytes with id 0; equal nonzero ids of a sequence form one document; every sequence reaches the largest id.
All inputs are finite; a program needn't handle non-finite values.
Results may differ from the reference program's by a relative error of at most 0.02.
Values may be sent and summed in bfloat16 or wider, within the bound.
A program may use at most 128 MiB of HBM per device.

```python
import functools
import jax
import jax.numpy as jnp
from jax import lax

D = 1472
FF = 3584
HEADS = 6
HEAD_DIM = 64
BUCKETS = 32
LEN = 1024
INNER = 384
BATCH = 32


def draw_segment_ids(key, part):
    first_key, second_key = jax.random.split(jax.random.fold_in(key, 7))
    places = jnp.arange(LEN, dtype=jnp.int32)[None, :]
    random_starts = jax.random.randint(first_key, (BATCH, LEN), 0, LEN // 4) == 0
    forced_starts = places % (LEN // 16) == 0
    starts = random_starts | forced_starts
    numbered = jnp.minimum(jnp.cumsum(starts.astype(jnp.int32), axis=1), 8)
    padding = jax.random.randint(second_key, (BATCH, 1), 1, LEN // 4 + 1)
    return jnp.where(places >= LEN - padding, 0, numbered).astype(jnp.int32)


def plant(result, stream_key, smallest, largest):
    extent = result.shape
    index_at = [jax.random.randint(jax.random.fold_in(stream_key, axis), (), 0, extent[axis]) for axis in range(len(extent))]
    result = result.at[tuple(index_at)].set(smallest)
    longest = extent.index(max(extent))
    index_at[longest] = (index_at[longest] + 1) % extent[longest]
    return result.at[tuple(index_at)].set(largest)


def block_scale(key, shape, cuts, smallest, top_value):
    def one(axis_at, parts):
        draws = jax.random.uniform(jax.random.fold_in(jax.random.fold_in(key, 6), axis_at), (parts,), jnp.float32, smallest / len(cuts), top_value / len(cuts))
        return jnp.repeat(jnp.exp(draws), shape[axis_at] // parts).reshape((-1,) + (1,) * (len(shape) - axis_at - 1))

    factor_of = one(*cuts[0])
    for cut in cuts[1:]:
        factor_of = factor_of * one(*cut)
    return factor_of


def noise(rng, extent, deviation, limit, cuts=(), held_as=jnp.bfloat16):
    entries = deviation * jax.random.normal(rng, extent, jnp.float32)
    if cuts:
        entries = entries * block_scale(rng, extent, cuts, -0.22, 0.18)
    return jnp.clip(entries, -limit, limit).astype(held_as)


def setup_inputs(seed: int = 0) -> dict:
    keys = jax.random.split(jax.random.key(seed), 15)
    inputs = noise(keys[0], (BATCH, LEN, D), 1.0, 6.0, ((0, 16), (1, 8)))
    cotangent = noise(keys[1], (BATCH, LEN, D), 1.0, 6.0, ((0, 16), (1, 8)))
    segment_ids = draw_segment_ids(jax.random.fold_in(keys[14], 71), 0)
    buckets = plant(jax.random.randint(keys[3], (2 * LEN - 1,), 0, BUCKETS), jax.random.fold_in(keys[3], 1), 0, BUCKETS - 1).astype(jnp.int32)
    norm_gain_1 = jnp.clip(1.0 + 0.1 * jax.random.normal(keys[4], (D,), jnp.float32), 0.5, 1.5).astype(jnp.bfloat16)
    norm_gain_2 = jnp.clip(1.0 + 0.1 * jax.random.normal(keys[5], (D,), jnp.float32), 0.5, 1.5).astype(jnp.bfloat16)
    relative_bias = noise(keys[6], (BUCKETS, HEADS), 1.0, 4.0)
    query_weight = noise(keys[7], (D, INNER), (5 * D) ** -0.5, 0.0625, ((1, 128),))
    key_weight = noise(keys[8], (D, INNER), (5 * D) ** -0.5, 0.0625, ((1, 128),))
    value_weight = noise(keys[9], (D, INNER), D ** -0.5, 0.15625, ((1, 128),))
    output_weight = noise(keys[10], (INNER, D), (INNER // 16) ** -0.5, 1.25, ((0, 128),))
    gate_weight = noise(keys[11], (D, FF), D ** -0.5, 0.15625, ((0, 32), (1, 4)))
    up_weight = noise(keys[12], (D, FF), D ** -0.5, 0.15625, ((0, 32), (1, 4)))
    down_weight = noise(keys[13], (FF, D), FF ** -0.5, 0.09375, ((0, 4), (1, 32)))
    return dict(inputs=inputs, cotangent=cotangent, segment_ids=segment_ids, buckets=buckets, norm_gain_1=norm_gain_1, norm_gain_2=norm_gain_2, relative_bias=relative_bias, query_weight=query_weight, key_weight=key_weight, value_weight=value_weight, output_weight=output_weight, gate_weight=gate_weight, up_weight=up_weight, down_weight=down_weight)


epsilon = 1e-06

@jax.custom_vjp
def low(v):
    return lax.optimization_barrier(v.astype(jnp.bfloat16)).astype(jnp.float32)

@jax.custom_vjp
def low_back(v):
    return v

def low_keep(v):
    return (low(v), None)

def low_pass(kept, grad):
    return (grad,)

def back_keep(v):
    return (v, None)

def back_low(kept, grad):
    return (low(grad),)
low.defvjp(low_keep, low_pass)
low_back.defvjp(back_keep, back_low)

def matmul(left, right):
    return jnp.dot(left, right, precision=lax.Precision.HIGHEST, preferred_element_type=jnp.float32)

def normalize(token_rows, gain):
    return token_rows * lax.rsqrt(lax.optimization_barrier(jnp.mean(token_rows * token_rows, axis=-1, keepdims=True)) + epsilon) * gain

def forward(segment_ids, buckets, inputs, gain_one, gain_two, relative_bias, query_weight, key_weight, value_weight, output_weight, gate_weight, up_weight, down_weight):
    length = segment_ids.shape[1]
    places = jnp.arange(length)
    by_offset = relative_bias[buckets]
    relative = jnp.transpose(by_offset[places[None, :] - places[:, None] + length - 1], (2, 0, 1))

    def one_sequence(sequence_pair):
        token_rows, segments = sequence_pair
        allowed = (segments[:, None] == segments[None, :]) & ((segments[None, :] != 0) | (places[:, None] == places[None, :]))
        normed = low(normalize(token_rows, gain_one))
        queries = low(low_back(matmul(normed, query_weight))).reshape(length, HEADS, HEAD_DIM)
        key_rows = low(low_back(matmul(normed, key_weight))).reshape(length, HEADS, HEAD_DIM)
        values = low(low_back(matmul(normed, value_weight))).reshape(length, HEADS, HEAD_DIM)
        scores = low_back(jnp.einsum('qhd,khd->hqk', queries, key_rows, precision=lax.Precision.HIGHEST) + relative)
        masked = jnp.where(allowed[None], scores, -1e+30)
        attention_probs = low(jax.nn.softmax(masked, axis=-1))
        attended = jnp.einsum('hqk,khd->qhd', attention_probs, values, precision=lax.Precision.HIGHEST)
        attended = low(low_back(attended.reshape(length, HEADS * HEAD_DIM)))
        middle = token_rows + low_back(matmul(attended, output_weight))
        normed_two = low(normalize(middle, gain_two))
        gate_proj = low_back(matmul(normed_two, gate_weight))
        up_proj = low_back(matmul(normed_two, up_weight))
        hidden = low(jax.nn.gelu(gate_proj, approximate=True) * up_proj)
        return middle + low_back(matmul(hidden, down_weight))
    return lax.map(jax.checkpoint(one_sequence), (inputs, segment_ids))

def reference(inputs, cotangent, segment_ids, buckets, norm_gain_1, norm_gain_2, relative_bias, query_weight, key_weight, value_weight, output_weight, gate_weight, up_weight, down_weight):
    floats = [array.astype(jnp.float32) for array in (inputs, norm_gain_1, norm_gain_2, relative_bias, query_weight, key_weight, value_weight, output_weight, gate_weight, up_weight, down_weight)]
    layer_output, pullback = jax.vjp(functools.partial(forward, segment_ids, buckets), *floats)
    grads = pullback(cotangent.astype(jnp.float32))
    return (layer_output, grads[0], grads[1], grads[2], grads[3], grads[4], grads[5], grads[6], grads[7], grads[8], grads[9], grads[10])
```

```python
import functools
import numpy as np
import jax
import jax.numpy as jnp
from jax import lax
from jax.experimental import pallas as pl
from jax.experimental.pallas import tpu as pltpu
from jax.sharding import PartitionSpec as P

D = 1472
DP = 1536
FS = 896
LEN = 1024
PIECE = 128
ROWS = 256
EPS = 1e-6
MESH = pl.DeviceIdType.MESH
BF = jnp.bfloat16
F32 = jnp.float32
NT = (((1,), (1,)), ((), ()))
NN = (((1,), (0,)), ((), ()))
TN = (((0,), (0,)), ((), ()))
GELU_C = 0.7978845608028654
WHOLE_HEAD = (0, 2, 3, 5)
SHARED_HEAD = (1, 1, 4, 4)


def dot(left, right, dims=NN):
    return lax.dot_general(left, right, dims, preferred_element_type=F32)


def block_slot(block):
    f, c = divmod(block, 2)
    y, zh, core = f // 4, (f // 2) % 2, f % 2
    z = zh * 2 + c
    return core * 16 + (y * 4 + z if core == 0 else z * 4 + y)


def make_constants():
    feat = np.zeros((DP, DP), np.float32)
    for r in range(D):
        feat[r, block_slot(r // 46) * 48 + r % 46] = 1
    stage = np.zeros((48, 64), np.float32)
    for w in range(4):
        for t in range(4):
            for i in range(3):
                stage[w * 12 + t * 3 + i, t * 16 + w * 3 + i] = 1

    def gathered(w, col):
        return block_slot(col // 12) * 48 + w * 12 + col % 12

    heads = np.zeros((DP, DP), np.float32)
    outs = np.zeros((DP, 512), np.float32)
    for j in range(4):
        hw, hs = WHOLE_HEAD[j], SHARED_HEAD[j]
        for part, (w, h) in enumerate(
            ((0, hw), (1, hw), (2, hw), (1, hs), (2, hs), (0, hs))
        ):
            for e in range(64):
                heads[gathered(w, h * 64 + e), j * 384 + part * 64 + e] = 1
        for part, h in enumerate((hw, hs)):
            for e in range(64):
                outs[gathered(3, h * 64 + e), j * 128 + part * 64 + e] = 1
    return tuple(a.astype(jnp.bfloat16) for a in (feat, stage, heads, outs))


class Place:
    def __init__(self):
        self.f = lax.axis_index("fsdp")
        self.c = lax.axis_index("ctx")
        self.t = lax.axis_index("tp")
        y = lax.div(self.f, 4)
        self.core = lax.rem(self.f, 2)
        z = lax.rem(lax.div(self.f, 2), 2) * 2 + self.c
        self.a1 = y + self.core * (z - y)
        self.a2 = z + self.core * (y - z)
        self.piece = self.c * 4 + self.t

    def at(self, da1, da2, dcore=0):
        core = lax.rem(self.core + dcore, 2)
        if dcore:
            y = self.a1 + self.core * (self.a2 - self.a1)
            z = self.a2 + self.core * (self.a1 - self.a2)
        else:
            b1 = lax.rem(self.a1 + da1, 4)
            b2 = lax.rem(self.a2 + da2, 4)
            y = b1 + core * (b2 - b1)
            z = b2 + core * (b1 - b2)
        return (y * 4 + lax.div(z, 2) * 2 + core, lax.rem(z, 2), self.t)

    def sibling(self):
        return self.at(0, 0, 1)

    def x(self, d):
        return (self.f, self.c, lax.rem(self.t + d + 4, 4))

    def group(self, dc, dt):
        return (self.f, lax.rem(self.c + dc, 2), lax.rem(self.t + dt, 4))

    def group_piece(self, dc, dt):
        return lax.rem(self.c + dc, 2) * 4 + lax.rem(self.t + dt, 4)

    def slot(self, da1=0, da2=0):
        return (
            self.core * 16 + lax.rem(self.a1 + da1, 4) * 4 + lax.rem(self.a2 + da2, 4)
        )

    def all_partners(self):
        out = [self.sibling()]
        for d in (1, 2, 3):
            out += [self.at(d, 0), self.at(0, d), self.x(d), self.group(1, d)]
        return out


GROUP = tuple((dc, dt) for dc in (0, 1) for dt in range(4) if (dc, dt) != (0, 0))


def greet(partners):
    bar = pltpu.get_barrier_semaphore()
    for p in partners:
        pl.semaphore_signal(bar, inc=1, device_id=p, device_id_type=MESH)
    pl.semaphore_wait(bar, len(partners))


def remote(src, dst, ss, rs, dev):
    return pltpu.make_async_remote_copy(
        src_ref=src, dst_ref=dst, send_sem=ss, recv_sem=rs, device_id=dev,
        device_id_type=MESH,
    )


class Gather32:
    def __init__(self, me, view, ss, rs):
        self.me, self.view, self.ss, self.rs = me, view, ss, rs
        self.sent = []

    def _send(self, slot, dev):
        k = len(self.sent)
        cp = remote(self.view(slot), self.view(slot), self.ss.at[k], self.rs.at[slot], dev)
        cp.start()
        self.sent.append(cp)

    def _arrived(self, slot):
        v = self.view(slot)
        remote(v, v, self.ss.at[0], self.rs.at[slot], self.me.sibling()).wait_recv()

    def first(self):
        me = self.me
        for d in (1, 3, 2):
            self._send(me.slot(), me.at(0, d))
        for d in (1, 3, 2):
            self._send(me.slot(), me.at(d, 0))
        self._send(me.slot(), me.sibling())

    def second(self):
        me = self.me
        for d in (1, 3, 2):
            s = me.slot(0, d)
            self._arrived(s)
            for e in (1, 3, 2):
                self._send(s, me.at(e, 0))
            self._send(s, me.sibling())

    def third(self):
        me = self.me
        for d in (0, 1, 3, 2):
            for e in (1, 3, 2):
                s = me.slot(e, d)
                self._arrived(s)
                self._send(s, me.sibling())

    def last(self):
        me = self.me
        base = (1 - me.core) * 16
        for k in range(16):
            self._arrived(base + k)

    def drain(self):
        for cp in self.sent:
            cp.wait_send()


class RingGather:
    def __init__(self, me, own, buf, ss, rs):
        self.me, self.own, self.buf, self.ss, self.rs = me, own, buf, ss, rs
        self.sent = []

    def slot(self, d):
        return lax.rem(self.me.t + d + 4, 4)

    def first(self):
        me = self.me
        for k, d in ((0, 1), (1, -1)):
            cp = remote(self.own, self.buf.at[me.t], self.ss.at[k], self.rs.at[k], me.x(d))
            cp.start()
            self.sent.append(cp)

    def arrived(self, k):
        v = self.buf.at[self.slot(-1 if k == 0 else 1)]
        remote(v, v, self.ss.at[k], self.rs.at[k], self.me.x(1)).wait_recv()

    def relay(self, k):
        rows = pl.ds(0, 128) if k == 0 else pl.ds(128, 128)
        v = self.buf.at[self.slot(-1 if k == 0 else 1), rows]
        cp = remote(v, v, self.ss.at[2 + k], self.rs.at[2 + k], self.me.x(1 if k == 0 else -1))
        cp.start()
        self.sent.append(cp)

    def opposite(self):
        for k, rows in ((0, pl.ds(0, 128)), (1, pl.ds(128, 128))):
            v = self.buf.at[self.slot(2), rows]
            remote(v, v, self.ss.at[2 + k], self.rs.at[2 + k], self.me.x(1)).wait_recv()

    def drain(self):
        for cp in self.sent:
            cp.wait_send()


class Exchange:
    def __init__(self, me, src, dst, ss, rs):
        self.me, self.src, self.dst, self.ss, self.rs = me, src, dst, ss, rs
        self.sent = []

    def start(self):
        me = self.me
        for k, (dc, dt) in enumerate(GROUP):
            cp = remote(
                self.src.at[me.group_piece(dc, dt)], self.dst.at[me.piece],
                self.ss.at[k], self.rs.at[k], me.group(dc, dt),
            )
            cp.start()
            self.sent.append(cp)
        self.dst[me.piece] = self.src[me.piece]

    def wait(self):
        me = self.me
        for k, (dc, dt) in enumerate(GROUP):
            v = self.dst.at[me.group_piece((2 - dc) % 2, (4 - dt) % 4)]
            remote(v, v, self.ss.at[k], self.rs.at[k], me.sibling()).wait_recv()

    def drain(self):
        for cp in self.sent:
            cp.wait_send()


def norm_rows(rows):
    return lax.rsqrt(jnp.sum(rows * rows, axis=1, keepdims=True) * (1.0 / D) + EPS)


def rows_of(ref, s):
    v = ref[s].astype(F32)
    v = jnp.concatenate([v, jnp.zeros((DP - D, PIECE), F32)], axis=0)
    return jnp.transpose(v)


def front_kernel(
    xt, ct, aw, fw, seg, bk, rb, g1, g2, stage, feat_h, heads_h, outs_h,
    wall_o, wf_o, cot_o, qkv_o, prob_o, att_o, mid_o, rows_o, wo_o,
    wall, wf, feat, heads, outs, sx, cot, zbuf, qkv, kv, prob, skew, cqs, wo, obuf, orecv,
    att, mid, rows2, xn,
    lsem, osem, ssx, rsx, sg, rg, sf, rf, sc, rc, sq, rq, so, ro,
):
    me = Place()
    loads = [
        pltpu.make_async_copy(a, b, lsem.at[i])
        for i, (a, b) in enumerate(((feat_h, feat), (heads_h, heads), (outs_h, outs)))
    ]
    for cp in loads:
        cp.start()
    stores = []

    def store(src, dst):
        cp = pltpu.make_async_copy(src, dst, osem.at[len(stores)])
        cp.start()
        stores.append(cp)

    greet(me.all_partners())

    xs = []
    for k, d in enumerate((1, 3, 2)):
        cp = remote(aw, sx.at[pl.ds(me.t * 16, 16)], ssx.at[k], rsx.at[k], me.x(d))
        cp.start()
        xs.append(cp)
    sx[pl.ds(pl.multiple_of(me.t * 16, 16), 16), :] = aw[...]

    for s in range(2):
        rows = rows_of(xt, s)
        xn[pl.ds(s * 128, 128), :] = (rows * norm_rows(rows) * g1[...]).astype(BF)

    for cp in xs:
        cp.wait()

    def wall_block(slot):
        return wall.at[pl.ds(pl.multiple_of(slot * 48, 48), 48), :]

    wall_block(me.slot())[...] = dot(stage[...], sx[...]).astype(BF)
    gw = Gather32(me, wall_block, sg, rg)
    gw.first()

    loads[0].wait()
    for s in range(2):
        cot[me.t, pl.ds(s * 128, 128), :] = dot(rows_of(ct, s).astype(BF), feat[...]).astype(BF)
    gw.second()
    gc = RingGather(me, cot.at[me.t], cot, sc, rc)
    gc.first()

    whole = me.t + lax.div(me.t + 1, 2)
    shared = 1 + 3 * lax.div(me.t, 2)
    half = lax.rem(me.t, 2)
    onehot = lax.broadcasted_iota(jnp.int32, (32, 2048), 0) == bk[...]
    lane = lax.broadcasted_iota(jnp.int32, (32, 128), 1)
    for n, head in ((0, whole), (1, shared)):
        column = jnp.sum(jnp.where(lane == head, rb[...], 0.0), axis=1, keepdims=True)
        line = jnp.sum(jnp.where(onehot, column, 0.0), axis=0, keepdims=True)
        skew[n] = pltpu.roll(
            jnp.broadcast_to(line, (128, 2048)), 0, 1, stride=1, stride_axis=0
        )
    ids = seg[pl.ds(me.c, 1), :].astype(F32)
    place = lax.broadcasted_iota(jnp.int32, (1, LEN), 1).astype(F32)
    ids = jnp.where(ids == 0.0, -1.0 - place, ids)
    cqs[...] = jnp.transpose(jnp.broadcast_to(ids, (128, LEN)))

    gw.third()
    gw.last()

    def wf_block(slot):
        return wf.at[:, pl.ds(pl.multiple_of(slot * 48, 48), 48), :]

    wf[:, pl.ds(pl.multiple_of(me.slot() * 48, 48), 48), :] = fw[...]
    gf = Gather32(me, wf_block, sf, rf)
    gf.first()

    loads[1].wait()
    y = jnp.concatenate(
        [dot(xn[...], wall[pl.ds(n * 512, 512), :], NT).astype(BF) for n in range(3)], axis=1
    )
    for j in range(4):
        z = dot(y, heads[:, pl.ds(j * 384, 384)]).astype(BF)
        for s in range(2):
            zbuf[s * 4 + j] = z[s * 128 : (s + 1) * 128]
    eq = Exchange(me, zbuf, qkv, sq, rq)
    eq.start()
    store(wall, wall_o)
    gf.second()
    loads[2].wait()
    wo[...] = dot(outs[...], wall[...], TN).astype(BF)
    store(wo, wo_o)
    for k in (0, 1):
        gc.arrived(k)
        gc.relay(k)

    eq.wait()
    store(qkv, qkv_o)
    for p in range(8):
        rows = pl.ds(p * 128, 128)
        for n, part in enumerate((1, 2, 3, 4)):
            kv[n, rows, :] = qkv[p, :, part * 64 : part * 64 + 64]

    def attend(n, block, p, q):
        start = pl.multiple_of(LEN - p * 128, 128)
        scores = dot(q, kv[2 * n], NT) + skew[n, :, pl.ds(start, LEN)]
        same = cqs[pl.ds(pl.multiple_of(p * 128, 128), 128), 0:1] == ids
        scores = jnp.where(same, scores, -1e30)
        e = jnp.exp(scores - jnp.max(scores, axis=1, keepdims=True))
        probs = (e * (1.0 / jnp.sum(e, axis=1, keepdims=True))).astype(BF)
        prob[block] = probs
        return dot(probs, kv[2 * n + 1]).astype(BF)

    def whole_step(p, _):
        o = attend(0, p, p, qkv[p, :, 0:64])
        obuf[p, :, 0:64] = o
        obuf[p, :, 64:128] = jnp.zeros((128, 64), BF)
        return 0

    lax.fori_loop(0, 8, whole_step, 0)
    gf.third()

    def shared_step(i, _):
        p = half * 4 + i
        obuf[p, :, 64:128] = attend(1, 8 + i, p, qkv[p, :, 320:384])
        return 0

    lax.fori_loop(0, 4, shared_step, 0)
    eo = Exchange(me, obuf, orecv, so, ro)
    eo.start()
    store(prob, prob_o)
    gc.opposite()
    store(cot, cot_o)
    eo.wait()
    for s in range(2):
        for j in range(4):
            att[pl.ds(s * 128, 128), pl.ds(j * 128, 128)] = orecv[s * 4 + j]
    store(att, att_o)
    for s in range(2):
        rows = pl.ds(s * 128, 128)
        h1 = rows_of(xt, s) + dot(att[rows, :], wo[...])
        mid[rows, :] = h1
        n2 = (h1 * norm_rows(h1) * g2[...]).astype(BF)
        rows2[rows, :] = dot(n2, feat[...]).astype(BF)
    store(mid, mid_o)
    store(rows2, rows_o)
    gf.last()
    store(wf, wf_o)
    for g in (gw, gc, gf, eq, eo):
        g.drain()
    for cp in stores:
        cp.wait()


VM = pl.BlockSpec(memory_space=pltpu.VMEM)
HB = pl.BlockSpec(memory_space=pl.ANY)
DMA = pltpu.SemaphoreType.DMA


def sds(shape, dtype=BF):
    return jax.ShapeDtypeStruct(shape, dtype)


def front(xt, ct, aw, fw, seg, bk, rb, g1, g2, stage, feat, heads, outs):
    V = pltpu.VMEM
    return pl.pallas_call(
        front_kernel,
        name="front",
        out_shape=(
            sds((DP, DP)), sds((3, DP, FS)), sds((4, ROWS, DP)), sds((8, 128, 384)),
            sds((12, 128, LEN)), sds((ROWS, 512)), sds((ROWS, DP), F32), sds((ROWS, DP)),
            sds((512, DP)),
        ),
        in_specs=[VM] * 10 + [HB] * 3,
        out_specs=[HB] * 9,
        scratch_shapes=[
            V((DP, DP), BF), V((3, DP, FS), BF), V((DP, DP), BF), V((DP, DP), BF),
            V((DP, 512), BF), V((64, DP), BF), V((4, ROWS, DP), BF), V((8, 128, 384), BF),
            V((8, 128, 384), BF), V((4, LEN, 64), BF), V((12, 128, LEN), BF),
            V((2, 128, 2048), F32), V((LEN, 128), F32), V((512, DP), BF),
            V((8, 128, 128), BF), V((8, 128, 128), BF), V((ROWS, 512), BF),
            V((ROWS, DP), F32), V((ROWS, DP), BF), V((ROWS, DP), BF),
            DMA((3,)), DMA((9,)), DMA((3,)), DMA((3,)), DMA((31,)), DMA((32,)),
            DMA((31,)), DMA((32,)), DMA((4,)), DMA((4,)), DMA((7,)), DMA((7,)),
            DMA((7,)), DMA((7,)),
        ],
        compiler_params=pltpu.CompilerParams(
            collective_id=0, has_side_effects=True, vmem_limit_bytes=60 * 2**20
        ),
    )(xt, ct, aw, fw, seg, bk, rb, g1, g2, stage, feat, heads, outs)


def prepare(
    inputs, cotangent, segment_ids, buckets, norm_gain_1, norm_gain_2, relative_bias,
    query_weight, key_weight, value_weight, output_weight, gate_weight, up_weight, down_weight,
):
    xt = jnp.transpose(inputs, (0, 2, 1))
    ct = jnp.transpose(cotangent, (0, 2, 1))
    aw = jnp.concatenate(
        [query_weight.T, key_weight.T, value_weight.T, output_weight], axis=0
    )
    aw = jnp.pad(aw, ((0, 4), (0, DP - D)))
    fw = jnp.pad(jnp.stack([gate_weight, up_weight, down_weight.T]), ((0, 0), (0, 2), (0, 0)))
    bk = jnp.concatenate([jnp.zeros((1,), jnp.int32), buckets])[None]
    rb = jnp.pad(relative_bias.astype(F32), ((0, 0), (0, 122)))
    g1, g2 = (
        jnp.pad(g.astype(F32), (0, DP - D))[None] for g in (norm_gain_1, norm_gain_2)
    )
    return xt, ct, aw, fw, segment_ids, bk, rb, g1, g2


def middle_kernel(
    rows2, cot_h, wf_h,
    fg_o, op_o, dx_o,
    wf, cot, xa, gu, hid, dpart, opart, recv, fg,
    lsem, osem, sc, rc, sd, rd,
):
    me = Place()
    stores = []

    def store(src, dst):
        cp = pltpu.make_async_copy(src, dst, osem.at[len(stores)])
        cp.start()
        stores.append(cp)

    loads = [
        pltpu.make_async_copy(a, b, lsem.at[i])
        for i, (a, b) in enumerate(
            ((wf_h.at[0], wf.at[0]), (wf_h.at[1], wf.at[1]), (cot_h, cot), (wf_h.at[2], wf.at[2]))
        )
    ]
    for cp in loads:
        cp.start()
    greet([me.x(d) for d in (1, 2, 3)])
    ring = RingGather(me, rows2, xa, sc, rc)
    ring.first()
    xa[me.t] = rows2[...]
    for cp in loads:
        cp.wait()
    sent = []

    def chunk(slot):
        base = pl.multiple_of(slot * ROWS, ROWS)
        rows = pl.ds(base, ROWS)
        x = xa[slot]
        dy = cot[slot]
        for n0, nw in ((0, 256), (256, 256), (512, 256), (768, 128)):
            cols = slice(n0, n0 + nw)
            g = dot(x, wf[0, :, cols])
            u = dot(x, wf[1, :, cols])
            dh = dot(dy, wf[2, :, cols])
            g2 = g * g
            th = jnp.tanh(GELU_C * g * (1.0 + 0.044715 * g2))
            half = 0.5 * (1.0 + th)
            gelu = g * half
            slope = half + 0.5 * g * (1.0 - th * th) * (GELU_C * (1.0 + 0.134145 * g2))
            hid[rows, cols] = (gelu * u).astype(BF)
            gu[rows, cols] = (dh * u * slope).astype(BF)
            gu[rows, FS + n0 : FS + n0 + nw] = (dh * gelu).astype(BF)
        dpart[slot] = (
            dot(gu[rows, 0:FS], wf[0], NT) + dot(gu[rows, FS : 2 * FS], wf[1], NT)
        ).astype(BF)
        opart[slot] = dot(hid[rows, :], wf[2], NT).astype(BF)

    def give(k, d):
        slot = ring.slot(d)
        cp = remote(dpart.at[slot], recv.at[k], sd.at[k], rd.at[k], me.x(d))
        cp.start()
        sent.append(cp)

    chunk(me.t)
    for k in (0, 1):
        ring.arrived(k)
        ring.relay(k)
    chunk(ring.slot(-1))
    give(0, -1)
    chunk(ring.slot(1))
    give(1, 1)
    ring.opposite()
    chunk(ring.slot(2))
    give(2, 2)
    store(opart, op_o)
    for m in range(6):
        cols = slice(m * 256, m * 256 + 256)
        both = dot(xa[:, :, cols].reshape(4 * ROWS, 256), gu[...], TN).astype(BF)
        fg[0, cols, :] = both[:, 0:FS]
        fg[1, cols, :] = both[:, FS:]
        fg[2, cols, :] = dot(cot[:, :, cols].reshape(4 * ROWS, 256), hid[...], TN).astype(BF)
        store(fg.at[:, pl.ds(m * 256, 256)], fg_o.at[:, pl.ds(m * 256, 256)])
    for k in (0, 1, 2):
        sent[k].wait_recv()
    total = dpart[me.t].astype(F32)
    for k in range(3):
        total = total + recv[k].astype(F32)
    dx_o[...] = total.astype(BF)
    for cp in sent:
        cp.wait_send()
    ring.drain()
    for cp in stores:
        cp.wait()


def middle(rows2, cot, wf):
    V = pltpu.VMEM
    return pl.pallas_call(
        middle_kernel,
        name="middle",
        out_shape=(sds((3, DP, FS)), sds((4, ROWS, DP)), sds((ROWS, DP))),
        in_specs=[VM, HB, HB],
        out_specs=[HB, HB, VM],
        scratch_shapes=[
            V((3, DP, FS), BF), V((4, ROWS, DP), BF), V((4, ROWS, DP), BF),
            V((4 * ROWS, 2 * FS), BF), V((4 * ROWS, FS), BF), V((4, ROWS, DP), BF),
            V((4, ROWS, DP), BF), V((3, ROWS, DP), BF), V((3, DP, FS), BF),
            DMA((4,)), DMA((7,)), DMA((4,)), DMA((4,)), DMA((3,)), DMA((3,)),
        ],
        compiler_params=pltpu.CompilerParams(
            collective_id=1, has_side_effects=True, vmem_limit_bytes=60 * 2**20
        ),
    )(rows2, cot, wf)


class Reduce32:
    def __init__(self, me, half, rc, r1, s1, r2, ss, rs):
        self.me, self.half, self.rc, self.r1, self.s1, self.r2 = me, half, rc, r1, s1, r2
        self.ss, self.rs = ss, rs
        self.sent = []

    def _send(self, src, dst, k, dev):
        cp = remote(src, dst, self.ss.at[k], self.rs.at[k], dev)
        cp.start()
        self.sent.append(cp)
        return cp

    def across(self, src):
        self.c = self._send(src, self.rc, 0, self.me.sibling())

    def first(self):
        me = self.me
        self.c.wait_recv()
        self.half[...] = (self.half[...].astype(F32) + self.rc[...].astype(F32)).astype(BF)
        self.one = []
        for k, d in enumerate((1, 3, 2)):
            g = pl.multiple_of(lax.rem(me.a1 + d, 4) * 192, 192)
            src = self.half.at[..., pl.ds(g, 192), :]
            self.one.append(self._send(src, self.r1.at[k], 1 + k, me.at(d, 0)))

    def second(self):
        me = self.me
        for cp in self.one:
            cp.wait_recv()
        total = self.half[..., pl.ds(pl.multiple_of(me.a1 * 192, 192), 192), :].astype(F32)
        for k in range(3):
            total = total + self.r1[k].astype(F32)
        self.s1[...] = total.astype(BF)
        self.two = []
        for k, d in enumerate((1, 3, 2)):
            g = pl.multiple_of(lax.rem(me.a2 + d, 4) * 48, 48)
            src = self.s1.at[..., pl.ds(g, 48), :]
            self.two.append(self._send(src, self.r2.at[k], 4 + k, me.at(0, d)))

    def last(self):
        me = self.me
        for cp in self.two:
            cp.wait_recv()
        total = self.s1[..., pl.ds(pl.multiple_of(me.a2 * 48, 48), 48), :].astype(F32)
        for k in range(3):
            total = total + self.r2[k].astype(F32)
        return total

    def drain(self):
        for cp in self.sent:
            cp.wait_send()


def back_kernel(
    dx2, xt, ct, g1, g2, bk, stage,
    fg_h, op_h, qkv_h, prob_h, att_h, mid_h, wall_h, wo_h, feat_h, heads_h, outs_h,
    small_o, ga_o, gf_o, lo_o, gi_o,
    perm, outs, wo, qkv, prob, att, mid, own, fhalf, dh1, xs, das, kv, acc, skew,
    dob, dor, db, dr, ro, frc, fr1, fs1, fr2, gall, arc, ar1, as1, ar2, sx, rx, sm, rm,
    lsem, so, ro_s, sdo, rdo, sdq, rdq, sf, rf, sa, ra, sx_s, rx_s, sm_s, rm_s,
):
    me = Place()
    half_rows = pl.multiple_of(me.core * 768, 768)
    other_rows = pl.multiple_of((1 - me.core) * 768, 768)
    pairs = (
        (wo_h, wo), (feat_h, perm), (mid_h, mid), (qkv_h, qkv), (prob_h, prob),
        (fg_h.at[:, pl.ds(half_rows, 768)], fhalf), (op_h.at[me.t], own),
        (att_h, att), (outs_h, outs),
    )
    loads = [pltpu.make_async_copy(a, b, lsem.at[i]) for i, (a, b) in enumerate(pairs)]
    for cp in loads:
        cp.start()
    greet(me.all_partners())
    rf32 = Reduce32(me, fhalf, frc, fr1, fs1, fr2, sf, rf)
    rf32.across(fg_h.at[:, pl.ds(other_rows, 768)])

    for cp in loads[:3]:
        cp.wait()
    gain2 = jnp.zeros((1, DP), F32)
    for s in range(2):
        rows = pl.ds(s * 128, 128)
        dxn2 = dot(dx2[rows, :], perm[...], NT)
        h1 = mid[rows, :]
        r2 = norm_rows(h1)
        n2 = h1 * r2
        gain2 = gain2 + jnp.sum(dxn2 * n2, axis=0, keepdims=True)
        e2 = dxn2 * g2[...]
        mean = jnp.sum(e2 * n2, axis=1, keepdims=True) * (1.0 / D)
        d = rows_of(ct, s) + r2 * (e2 - n2 * mean)
        dh1[rows, :] = d
        da = d.astype(BF)
        xs[pl.ds(256 + s * 128, 128), :] = da
        do = dot(da, wo[...], NT).astype(BF)
        for j in range(4):
            dob[s * 4 + j] = do[:, j * 128 : (j + 1) * 128]
    ed = Exchange(me, dob, dor, sdo, rdo)
    ed.start()
    outsends = []
    for k, d in enumerate((1, 3, 2)):
        cp = remote(
            op_h.at[lax.rem(me.t + d, 4)], ro.at[k], so.at[k], ro_s.at[k], me.x(d)
        )
        cp.start()
        outsends.append(cp)
    for cp in loads[3:]:
        cp.wait()
    for p in range(8):
        rows = pl.ds(p * 128, 128)
        for n, part in enumerate((1, 2, 3, 4)):
            kv[n, rows, :] = qkv[p, :, part * 64 : part * 64 + 64]
    acc[...] = jnp.zeros_like(acc)
    skew[...] = jnp.zeros_like(skew)
    for s in range(2):
        rows = rows_of(xt, s)
        xs[pl.ds(s * 128, 128), :] = (rows * norm_rows(rows) * g1[...]).astype(BF)
    rf32.first()
    ed.wait()

    def attend(n, block, p, q, do):
        start = pl.multiple_of(LEN - p * 128, 128)
        pb = prob[block]
        probs = pb.astype(F32)
        dp = dot(do, kv[2 * n + 1], NT)
        delta = jnp.sum(dp * probs, axis=1, keepdims=True)
        ds = (probs * (dp - delta)).astype(BF)
        cols = pl.ds(start, LEN)
        skew[n, :, cols] = skew[n, :, cols] + ds.astype(F32)
        acc[2 * n] = acc[2 * n] + dot(ds, q, TN)
        acc[2 * n + 1] = acc[2 * n + 1] + dot(pb, do, TN)
        return dot(ds, kv[2 * n]).astype(BF)

    half = lax.rem(me.t, 2)

    def whole_step(p, _):
        db[p, :, 0:64] = attend(0, p, p, qkv[p, :, 0:64], dor[p, :, 0:64])
        db[p, :, 320:384] = jnp.zeros((128, 64), BF)
        return 0

    lax.fori_loop(0, 8, whole_step, 0)
    rf32.second()

    def shared_step(i, _):
        p = half * 4 + i
        db[p, :, 320:384] = attend(1, 8 + i, p, qkv[p, :, 320:384], dor[p, :, 64:128])
        return 0

    lax.fori_loop(0, 4, shared_step, 0)
    for p in range(8):
        for n in range(4):
            db[p, :, 64 + n * 64 : 128 + n * 64] = acc[n, pl.ds(p * 128, 128), :].astype(BF)
    eq = Exchange(me, db, dr, sdq, rdq)
    eq.start()
    gf_o[...] = rf32.last()

    whole = me.t + lax.div(me.t + 1, 2)
    shared = 1 + 3 * lax.div(me.t, 2)
    onehot = lax.broadcasted_iota(jnp.int32, (32, 2048), 0) == bk[...]
    lane = lax.broadcasted_iota(jnp.int32, (32, 128), 1)
    row = lax.broadcasted_iota(jnp.int32, (128, 2048), 0)
    bias = jnp.zeros((32, 128), F32)
    for n, head in ((0, whole), (1, shared)):
        tilted = skew[n]
        for b in range(7):
            moved = pltpu.roll(tilted, 2048 - (1 << b), 1)
            tilted = jnp.where(lax.rem(lax.div(row, 1 << b), 2) == 1, moved, tilted)
        line = jnp.sum(tilted, axis=0, keepdims=True)
        column = jnp.sum(jnp.where(onehot, line, 0.0), axis=1, keepdims=True)
        bias = bias + jnp.where(lane == head, column, 0.0)

    for cp in outsends:
        cp.wait_recv()
    for s in range(2):
        rows = pl.ds(s * 128, 128)
        total = own[rows, :].astype(F32)
        for k in range(3):
            total = total + ro[k, rows, :].astype(F32)
        y = mid[rows, :] + dot(total.astype(BF), perm[...], NT)
        lo_o[s] = jnp.transpose(y)[0:D]
    reload = pltpu.make_async_copy(heads_h, perm, lsem.at[0])
    reload.start()
    das[pl.ds(256, 256), :] = dot(att[...], outs[...], NT).astype(BF)
    reload.wait()

    eq.wait()
    for s in range(2):
        d = jnp.concatenate([dr[s * 4 + j] for j in range(4)], axis=1)
        das[pl.ds(s * 128, 128), :] = dot(d, perm[...], NT).astype(BF)
    reload = pltpu.make_async_copy(wall_h, perm, lsem.at[1])
    reload.start()
    ra32 = Reduce32(me, gall.at[0], arc, ar1, as1, ar2, sa, ra)
    for n, base in ((1, other_rows), (0, half_rows)):
        for m in range(3):
            cols = pl.ds(pl.multiple_of(base + m * 256, 256), 256)
            gall[n, pl.ds(m * 256, 256), :] = dot(das[:, cols], xs[...], TN).astype(BF)
        if n == 1:
            ra32.across(gall.at[1])

    reload.wait()
    gain1 = jnp.zeros((1, DP), F32)
    for s in range(2):
        rows = pl.ds(s * 128, 128)
        dxn = dot(das[rows, :], perm[...])
        x = rows_of(xt, s)
        r1 = norm_rows(x)
        n1 = x * r1
        gain1 = gain1 + jnp.sum(dxn * n1, axis=0, keepdims=True)
        e1 = dxn * g1[...]
        mean = jnp.sum(e1 * n1, axis=1, keepdims=True) * (1.0 / D)
        gi_o[s] = jnp.transpose(dh1[rows, :] + r1 * (e1 - n1 * mean))[0:D]
    sm[...] = jnp.zeros_like(sm)
    sm[0:1, :] = gain1
    sm[1:2, :] = gain2
    sm[8:40, 0:128] = bias

    small_sent = []

    def small(stage_no, devs):
        cps = []
        for k, dev in enumerate(devs):
            i = stage_no * 3 + k
            cp = remote(sm.at[pl.ds(stage_no * 40, 40)], rm.at[i], sm_s.at[i], rm_s.at[i], dev)
            cp.start()
            cps.append(cp)
        small_sent.extend(cps)
        return cps

    def gather_small(stage_no, cps):
        total = sm[pl.ds(stage_no * 40, 40), :]
        for k, cp in enumerate(cps):
            cp.wait_recv()
            total = total + rm[stage_no * 3 + k]
        sm[pl.ds(stage_no * 40 + 40, 40), :] = total

    c = small(0, [me.x(d) for d in (1, 2, 3)])
    ra32.first()
    gather_small(0, c)
    c = small(1, [me.at(d, 0) for d in (1, 2, 3)])
    gather_small(1, c)
    c = small(2, [me.at(0, d) for d in (1, 2, 3)])
    ra32.second()
    gather_small(2, c)
    c = small(3, [me.sibling()])
    mine = ra32.last().astype(BF)
    sx[...] = dot(stage[...], mine, TN).astype(BF)
    xsend = []
    for k, d in enumerate((1, 3, 2)):
        rows = pl.ds(pl.multiple_of(lax.rem(me.t + d, 4) * 16, 16), 16)
        cp = remote(sx.at[rows], rx.at[k], sx_s.at[k], rx_s.at[k], me.x(d))
        cp.start()
        xsend.append(cp)
    gather_small(3, c)
    small_o[...] = sm[160:200, :]
    total = sx[pl.ds(pl.multiple_of(me.t * 16, 16), 16), :].astype(F32)
    for k, cp in enumerate(xsend):
        cp.wait_recv()
        total = total + rx[k].astype(F32)
    ga_o[...] = total
    for cp in outsends + xsend + small_sent:
        cp.wait_send()
    for g in (rf32, ra32, ed, eq):
        g.drain()


def back(dx2, xt, ct, g1, g2, bk, stage, *rest):
    V = pltpu.VMEM
    return pl.pallas_call(
        back_kernel,
        name="back",
        out_shape=(
            sds((40, DP), F32), sds((16, DP), F32), sds((3, 48, FS), F32),
            sds((2, D, 128), F32), sds((2, D, 128), F32),
        ),
        in_specs=[VM] * 7 + [HB] * 11,
        out_specs=[VM] * 5,
        scratch_shapes=[
            V((DP, DP), BF), V((DP, 512), BF), V((512, DP), BF),
            V((8, 128, 384), BF), V((12, 128, LEN), BF), V((ROWS, 512), BF),
            V((ROWS, DP), F32), V((ROWS, DP), BF), V((3, 768, FS), BF), V((ROWS, DP), F32),
            V((512, DP), BF), V((512, DP), BF), V((4, LEN, 64), BF), V((4, LEN, 64), F32),
            V((2, 128, 2048), F32), V((8, 128, 128), BF), V((8, 128, 128), BF),
            V((8, 128, 384), BF), V((8, 128, 384), BF), V((3, ROWS, DP), BF),
            V((3, 768, FS), BF), V((3, 3, 192, FS), BF), V((3, 192, FS), BF),
            V((3, 3, 48, FS), BF), V((2, 768, DP), BF), V((768, DP), BF),
            V((3, 192, DP), BF), V((192, DP), BF), V((3, 48, DP), BF), V((64, DP), BF),
            V((3, 16, DP), BF), V((200, DP), F32), V((10, 40, DP), F32),
            DMA((10,)), DMA((3,)), DMA((3,)), DMA((7,)), DMA((7,)), DMA((7,)), DMA((7,)),
            DMA((7,)), DMA((7,)), DMA((7,)), DMA((7,)), DMA((3,)), DMA((3,)), DMA((10,)),
            DMA((10,)),
        ],
        compiler_params=pltpu.CompilerParams(
            collective_id=2, has_side_effects=True, vmem_limit_bytes=64 * 2**20 - 2**19
        ),
    )(dx2, xt, ct, g1, g2, bk, stage, *rest)


def per_device(*args):
    feat, stage, heads, outs = make_constants()
    xt, ct, aw, fw, seg, bk, rb, g1, g2 = prepare(*args)
    wall, wf, cot, qkv, prob, att, mid, rows2, wo = front(
        xt, ct, aw, fw, seg, bk, rb, g1, g2, stage, feat, heads, outs
    )
    fg, op, dx2 = middle(rows2, cot, wf)
    small, ga, gf, lo, gi = back(
        dx2, xt, ct, g1, g2, bk, stage,
        fg, op, qkv, prob, att, mid, wall, wo, feat, heads, outs,
    )
    return (
        jnp.transpose(lo, (0, 2, 1)),
        jnp.transpose(gi, (0, 2, 1)),
        small[0, :D],
        small[1, :D],
        small[8:40, :6],
        ga[0:3, :D].T,
        ga[3:6, :D].T,
        ga[6:9, :D].T,
        ga[9:12, :D],
        gf[0, :46],
        gf[1, :46],
        gf[2, :46].T,
    )


def solution(mesh):
    every = ("fsdp", "ctx", "tp")
    rows = P("fsdp", ("ctx", "tp"), None)
    wide = P(("fsdp", "ctx"), "tp")
    attn = (P(None, every), P(None, every), P(None, every), P(every, None))
    ffn = (wide, wide, P("tp", ("fsdp", "ctx")))
    return jax.shard_map(
        per_device,
        mesh=mesh,
        in_specs=(rows, rows, P("fsdp", None), P(), P(), P(), P()) + attn + ffn,
        out_specs=(rows, rows, P(), P(), P()) + attn + ffn,
        check_vma=False,
    )
```

```python
import functools
import numpy as np
import jax
import jax.numpy as jnp
from jax import lax
from jax.experimental import pallas as pl
from jax.experimental.pallas import tpu as pltpu
from jax.sharding import PartitionSpec as P

D = 1472
DP = 1536
FS = 896
LEN = 1024
PIECE = 128
ROWS = 256
EPS = 1e-6
MESH = pl.DeviceIdType.MESH
BF = jnp.bfloat16
F32 = jnp.float32
NT = (((1,), (1,)), ((), ()))
NN = (((1,), (0,)), ((), ()))
TN = (((0,), (0,)), ((), ()))
GELU_C = 0.7978845608028654
WHOLE_HEAD = (0, 2, 3, 5)
SHARED_HEAD = (1, 1, 4, 4)


def dot(left, right, dims=NN):
    return lax.dot_general(left, right, dims, preferred_element_type=F32)


def block_slot(block):
    f, c = divmod(block, 2)
    y, zh, core = f // 4, (f // 2) % 2, f % 2
    z = zh * 2 + c
    return core * 16 + (y * 4 + z if core == 0 else z * 4 + y)


def make_constants():
    feat = np.zeros((DP, DP), np.float32)
    for r in range(D):
        feat[r, block_slot(r // 46) * 48 + r % 46] = 1
    stage = np.zeros((48, 64), np.float32)
    for w in range(4):
        for t in range(4):
            for i in range(3):
                stage[w * 12 + t * 3 + i, t * 16 + w * 3 + i] = 1

    def gathered(w, col):
        return block_slot(col // 12) * 48 + w * 12 + col % 12

    heads = np.zeros((DP, DP), np.float32)
    outs = np.zeros((DP, 512), np.float32)
    for j in range(4):
        hw, hs = WHOLE_HEAD[j], SHARED_HEAD[j]
        for part, (w, h) in enumerate(
            ((0, hw), (1, hw), (2, hw), (1, hs), (2, hs), (0, hs))
        ):
            for e in range(64):
                heads[gathered(w, h * 64 + e), j * 384 + part * 64 + e] = 1
        for part, h in enumerate((hw, hs)):
            for e in range(64):
                outs[gathered(3, h * 64 + e), j * 128 + part * 64 + e] = 1
    return tuple(a.astype(jnp.bfloat16) for a in (stage, feat, heads, outs.T))


class Place:
    def __init__(self):
        self.f = lax.axis_index("fsdp")
        self.c = lax.axis_index("ctx")
        self.t = lax.axis_index("tp")
        y = lax.div(self.f, 4)
        self.core = lax.rem(self.f, 2)
        z = lax.rem(lax.div(self.f, 2), 2) * 2 + self.c
        self.a1 = y + self.core * (z - y)
        self.a2 = z + self.core * (y - z)
        self.piece = self.c * 4 + self.t

    def at(self, da1, da2, dcore=0):
        core = lax.rem(self.core + dcore, 2)
        if dcore:
            y = self.a1 + self.core * (self.a2 - self.a1)
            z = self.a2 + self.core * (self.a1 - self.a2)
        else:
            b1 = lax.rem(self.a1 + da1, 4)
            b2 = lax.rem(self.a2 + da2, 4)
            y = b1 + core * (b2 - b1)
            z = b2 + core * (b1 - b2)
        return (y * 4 + lax.div(z, 2) * 2 + core, lax.rem(z, 2), self.t)

    def sibling(self):
        return self.at(0, 0, 1)

    def x(self, d):
        return (self.f, self.c, lax.rem(self.t + d + 4, 4))

    def group(self, dc, dt):
        return (self.f, lax.rem(self.c + dc, 2), lax.rem(self.t + dt, 4))

    def group_piece(self, dc, dt):
        return lax.rem(self.c + dc, 2) * 4 + lax.rem(self.t + dt, 4)

    def slot(self, da1=0, da2=0):
        return (
            self.core * 16 + lax.rem(self.a1 + da1, 4) * 4 + lax.rem(self.a2 + da2, 4)
        )

    def all_partners(self):
        out = [self.sibling()]
        for d in (1, 2, 3):
            out += [self.at(d, 0), self.at(0, d), self.x(d), self.group(1, d)]
        return out


GROUP = tuple((dc, dt) for dc in (0, 1) for dt in range(4) if (dc, dt) != (0, 0))


def greet(partners):
    bar = pltpu.get_barrier_semaphore()
    for p in partners:
        pl.semaphore_signal(bar, inc=1, device_id=p, device_id_type=MESH)
    pl.semaphore_wait(bar, len(partners))


def remote(src, dst, ss, rs, dev, tag=None):
    return pltpu.make_async_remote_copy(
        src_ref=src, dst_ref=dst, send_sem=ss, recv_sem=rs, device_id=dev,
        device_id_type=MESH,
    )


class Gather32:
    tag = None

    def __init__(self, me, view, ss, rs):
        self.me, self.view, self.ss, self.rs = me, view, ss, rs
        self.sent = []

    def _send(self, slot, dev):
        k = len(self.sent)
        cp = remote(self.view(slot), self.view(slot), self.ss.at[k], self.rs.at[slot], dev, self.tag)
        cp.start()
        self.sent.append(cp)

    def _arrived(self, slot):
        v = self.view(slot)
        remote(v, v, self.ss.at[0], self.rs.at[slot], self.me.sibling(), self.tag).wait_recv()

    def first(self):
        me = self.me
        for d in (1, 3, 2):
            self._send(me.slot(), me.at(0, d))
        for d in (1, 3, 2):
            self._send(me.slot(), me.at(d, 0))
        self._send(me.slot(), me.sibling())

    def second(self):
        me = self.me
        for d in (1, 3, 2):
            s = me.slot(0, d)
            self._arrived(s)
            for e in (1, 3, 2):
                self._send(s, me.at(e, 0))
            self._send(s, me.sibling())

    def third(self):
        me = self.me
        for d in (0, 1, 3, 2):
            for e in (1, 3, 2):
                s = me.slot(e, d)
                self._arrived(s)
                self._send(s, me.sibling())

    def last(self):
        me = self.me
        base = (1 - me.core) * 16
        for k in range(16):
            self._arrived(base + k)

    def drain(self):
        for cp in self.sent:
            cp.wait_send()


class RingGather:
    tag = None

    def __init__(self, me, buf, ss, rs):
        self.me, self.buf, self.ss, self.rs = me, buf, ss, rs
        self.sent = []

    def slot(self, d):
        return lax.rem(self.me.t + d + 4, 4)

    def _send(self, v, k, d):
        cp = remote(v, v, self.ss.at[k], self.rs.at[k], self.me.x(d), self.tag)
        cp.start()
        self.sent.append(cp)

    def _arrived(self, v, k):
        remote(v, v, self.ss.at[k], self.rs.at[k], self.me.x(1), self.tag).wait_recv()

    def first(self):
        own = self.buf(self.me.t, 0, ROWS)
        self._send(own, 0, 1)
        self._send(own, 1, -1)

    def arrived(self, k):
        self._arrived(self.buf(self.slot(2 * k - 1), 0, ROWS), k)

    def relay(self, k):
        self._send(self.buf(self.slot(2 * k - 1), k * 128, 128), 2 + k, 1 - 2 * k)

    def opposite(self):
        for k in (0, 1):
            self._arrived(self.buf(self.slot(2), k * 128, 128), 2 + k)

    def drain(self):
        for cp in self.sent:
            cp.wait_send()


class Exchange:
    tag = None

    def __init__(self, me, src, dst, ss, rs):
        self.me, self.src, self.dst, self.ss, self.rs = me, src, dst, ss, rs
        self.sent = []

    def start(self):
        me = self.me
        for k, (dc, dt) in enumerate(GROUP):
            cp = remote(
                self.src.at[me.group_piece(dc, dt)], self.dst.at[me.piece],
                self.ss.at[k], self.rs.at[k], me.group(dc, dt), self.tag,
            )
            cp.start()
            self.sent.append(cp)
        self.dst[me.piece] = self.src[me.piece]

    def wait(self):
        me = self.me
        for k, (dc, dt) in enumerate(GROUP):
            v = self.dst.at[me.group_piece((2 - dc) % 2, (4 - dt) % 4)]
            remote(v, v, self.ss.at[k], self.rs.at[k], me.sibling(), self.tag).wait_recv()

    def drain(self):
        for cp in self.sent:
            cp.wait_send()


def norm_rows(rows):
    return lax.rsqrt(jnp.sum(rows * rows, axis=1, keepdims=True) * (1.0 / D) + EPS)


def rows_of(ref, s):
    v = ref[s].astype(F32)
    v = jnp.concatenate([v, jnp.zeros((DP - D, PIECE), F32)], axis=0)
    return jnp.transpose(v)


class Reduce32:
    tag = None

    def __init__(self, me, mine, theirs, landing, ss, rs, free):
        self.me, self.mine, self.theirs, self.landing = me, mine, theirs, landing
        self.ss, self.rs, self.free = ss, rs, free
        self.sent, self.crossing = [], []
        self.pair = 1 - lax.div(me.a1, 2)
        mate = me.a1 + 1 - 2 * lax.rem(me.a1, 2)
        self.order = (self.pair * 2, self.pair * 2 + 1, mate, me.a1)

    def _send(self, src, dst, k, dev):
        cp = remote(src, dst, self.ss.at[k], self.rs.at[k], dev, self.tag)
        cp.start()
        self.sent.append(cp)
        return cp

    def across(self, group):
        cp = self._send(
            self.theirs(group * 192, 192), self.landing(group * 192, 192), group,
            self.me.sibling(),
        )
        self.crossing.append(cp)

    def release(self):
        for cp in self.crossing:
            cp.wait_send()
            self.sent.remove(cp)
        for d in (1, 2, 3):
            for dev in (self.me.at(d, 0), self.me.at(0, d)):
                pl.semaphore_signal(self.free, inc=1, device_id=dev, device_id_type=MESH)

    def first(self):
        me = self.me
        pl.semaphore_wait(self.free, 6)
        self.one = []
        for group in self.order:
            m, there = self.mine(group * 192, 192), self.landing(group * 192, 192)
            remote(
                m, there, self.ss.at[group], self.rs.at[group], me.sibling(), self.tag
            ).wait_recv()
            m[...] = (m[...].astype(F32) + there[...].astype(F32)).astype(BF)
            if len(self.one) < 3:
                d = lax.rem(group - me.a1 + 4, 4)
                dst = self.theirs((d - 1) * 192, 192)
                self.one.append(self._send(m, dst, 3 + d, me.at(d, 0)))

    def second(self):
        me = self.me
        m = self.mine(me.a1 * 192, 192)
        for k in range(3):
            v = self.theirs(k * 192, 192)
            remote(v, v, self.ss.at[4 + k], self.rs.at[4 + k], me.sibling(), self.tag).wait_recv()
        total = m[...].astype(F32)
        for k in range(3):
            total = total + self.theirs(k * 192, 192)[...].astype(F32)
        m[...] = total.astype(BF)
        self.two = []
        for k, d in enumerate((1, 3, 2)):
            src = self.mine(me.a1 * 192 + lax.rem(me.a2 + d, 4) * 48, 48)
            self.two.append(self._send(src, self.theirs(576 + k * 48, 48), 7 + k, me.at(0, d)))

    def last(self):
        me = self.me
        for cp in self.two:
            cp.wait_recv()
        total = self.mine(me.a1 * 192 + me.a2 * 48, 48)[...].astype(F32)
        for k in range(3):
            total = total + self.theirs(576 + k * 48, 48)[...].astype(F32)
        return total

    def drain(self):
        for cp in self.sent:
            cp.wait_send()


def layer_kernel(
    xt, ct, wq, wk, wv, wo_in, wg, wu, wd, seg, bk_in, rb, g1_in, g2_in, stage,
    feat_h, heads_h, outs_h,
    small_o, ga_o, gf_o, lo_o, gi_o, wall_o,
    pool, feat, r1, own, wf, hgu, zbuf, qkv, dr, kv, acc, prob, skew, cqs, wo, obuf, orecv, dor,
    att, mid, xs, das, sx, rx, sm, rm, aw, g1, g2, bk,
    lsem, ssx, rsx, sg, rg, sf, rf, sc, rc, sq, rq, so, ro, sxr, rxr, sd, rd, st, rt,
    sdo, rdo, sdq, rdq, srf, rrf, sra, rra, sxs, rxs, sms, rms, credit,
):
    me = Place()
    core, t = me.core, me.t
    WALL, RECV, OUT, OUTS = 1024, 2048, 2816, 2816

    def local(src, dst, i):
        cp = pltpu.make_async_copy(src, dst, lsem.at[i])
        cp.start()
        return cp

    load_feat = local(feat_h, feat, 0)
    aw[...] = jnp.zeros_like(aw)
    shard = [w[...].astype(F32) for w in (wq, wk, wv, wo_in)] + [jnp.zeros((4, D), F32)]
    aw[:, 0:D] = jnp.concatenate(shard, axis=0).astype(BF)
    greet(me.all_partners())
    load_heads = local(heads_h, r1, 1)
    load_outs = local(outs_h, pool.at[pl.ds(OUTS, 512)], 2)

    xsend = []
    for k, d in enumerate((1, 3, 2)):
        cp = remote(
            aw, sx.at[pl.ds(pl.multiple_of(t * 16, 16), 16)], ssx.at[k], rsx.at[k], me.x(d), "xst"
        )
        cp.start()
        xsend.append(cp)
    sx[pl.ds(pl.multiple_of(t * 16, 16), 16), :] = aw[...]

    for g, g_in in ((g1, g1_in), (g2, g2_in)):
        g[...] = jnp.zeros_like(g)
        g[:, 0:D] = g_in[...].astype(F32).reshape(1, D)
    bk[...] = jnp.zeros_like(bk)
    bk[:, 1:2048] = bk_in[...].reshape(1, 2047)
    for s in range(2):
        rows = rows_of(xt, s)
        xs[pl.ds(s * 128, 128), :] = (rows * norm_rows(rows) * g1[...]).astype(BF)
    for cp in xsend:
        cp.wait()

    def wall_block(slot):
        return pool.at[pl.ds(pl.multiple_of(WALL + slot * 48, 16), 48), :]

    wall_block(me.slot())[...] = dot(stage[...], sx[...]).astype(BF)
    gw = Gather32(me, wall_block, sg, rg)
    gw.first()

    def chunk_rows(base, slot):
        return pl.ds(pl.multiple_of(base + slot * ROWS, ROWS), ROWS)

    load_feat.wait()
    for s in range(2):
        pool[pl.ds(pl.multiple_of(t * ROWS + s * 128, 128), 128), :] = dot(
            rows_of(ct, s).astype(BF), feat[...]
        ).astype(BF)
    gw.second()
    gc = RingGather(
        me, lambda i, r, n: pool.at[pl.ds(pl.multiple_of(i * ROWS + r, 128), n)], sc, rc
    )
    gc.first()

    whole = t + lax.div(t + 1, 2)
    shared = 1 + 3 * lax.div(t, 2)
    half = lax.rem(t, 2)
    onehot = lax.broadcasted_iota(jnp.int32, (32, 2048), 0) == bk[...]
    lane = lax.broadcasted_iota(jnp.int32, (32, 128), 1)
    by_bucket = jnp.concatenate(
        [jnp.transpose(jnp.pad(rb[...].astype(F32), ((0, 122), (0, 96))))], axis=0
    )[0:32]
    for n, head in ((0, whole), (1, shared)):
        column = jnp.sum(jnp.where(lane == head, by_bucket, 0.0), axis=1, keepdims=True)
        line = jnp.sum(jnp.where(onehot, column, 0.0), axis=0, keepdims=True)
        skew[n] = pltpu.roll(
            jnp.broadcast_to(line, (128, 2048)), 0, 1, stride=1, stride_axis=0
        )
    ids = seg[pl.ds(me.c, 1), :].astype(F32)
    place = lax.broadcasted_iota(jnp.int32, (1, LEN), 1).astype(F32)
    ids = jnp.where(ids == 0.0, -1.0 - place, ids)
    cqs[...] = jnp.transpose(jnp.broadcast_to(ids, (128, LEN)))

    gw.third()
    gw.last()

    def wf_rows(row, n):
        return wf.at[:, pl.ds(pl.multiple_of(row, 16), n), :]

    def wf_block(slot):
        return wf_rows(slot * 48, 48)

    for n, w in enumerate((wg, wu, wd)):
        wf[n, pl.ds(pl.multiple_of(me.slot() * 48, 16), 48), :] = jnp.concatenate(
            [w[...].astype(F32), jnp.zeros((2, FS), F32)], axis=0
        ).astype(BF)
    gf = Gather32(me, wf_block, sf, rf)
    gf.first()

    load_heads.wait()
    y = jnp.concatenate(
        [
            dot(xs[0:256, :], pool[pl.ds(WALL + n * 512, 512), :], NT).astype(BF)
            for n in range(3)
        ],
        axis=1,
    )
    for j in range(4):
        z = dot(y, r1[:, pl.ds(j * 384, 384)]).astype(BF)
        for s in range(2):
            zbuf[s * 4 + j] = z[s * 128 : (s + 1) * 128]
    eq = Exchange(me, zbuf, qkv, sq, rq)
    eq.start()
    store_wall = local(pool.at[pl.ds(WALL, DP)], wall_o, 3)
    gf.second()
    load_outs.wait()
    wo[...] = dot(pool[pl.ds(OUTS, 512), :], pool[pl.ds(WALL, DP), :]).astype(BF)
    for k in (0, 1):
        gc.arrived(k)
        gc.relay(k)

    eq.wait()
    for p in range(8):
        rows = pl.ds(p * 128, 128)
        for n, part in enumerate((1, 2, 3, 4)):
            kv[n, rows, :] = qkv[p, :, part * 64 : part * 64 + 64]

    def attend(n, block, p, q):
        start = pl.multiple_of(LEN - p * 128, 128)
        scores = dot(q, kv[2 * n], NT) + skew[n, :, pl.ds(start, LEN)]
        same = cqs[pl.ds(pl.multiple_of(p * 128, 128), 128), 0:1] == ids
        scores = jnp.where(same, scores, -1e30)
        e = jnp.exp(scores - jnp.max(scores, axis=1, keepdims=True))
        probs = (e * (1.0 / jnp.sum(e, axis=1, keepdims=True))).astype(BF)
        prob[block] = probs
        return dot(probs, kv[2 * n + 1]).astype(BF)

    def whole_step(p, _):
        o = attend(0, p, p, qkv[p, :, 0:64])
        obuf[p, :, 0:64] = o
        obuf[p, :, 64:128] = jnp.zeros((128, 64), BF)
        return 0

    lax.fori_loop(0, 8, whole_step, 0)
    gf.third()

    def shared_step(i, _):
        p = half * 4 + i
        obuf[p, :, 64:128] = attend(1, 8 + i, p, qkv[p, :, 320:384])
        return 0

    lax.fori_loop(0, 4, shared_step, 0)
    gw.drain()
    store_wall.wait()
    eo = Exchange(me, obuf, orecv, so, ro)
    eo.start()
    eo.wait()
    for s in range(2):
        for j in range(4):
            att[pl.ds(s * 128, 128), pl.ds(j * 128, 128)] = orecv[s * 4 + j]

    def xa_rows(i, r, n):
        return pool.at[pl.ds(pl.multiple_of(1024 + i * ROWS + r, 128), n)]

    for s in range(2):
        rows = pl.ds(s * 128, 128)
        h1 = rows_of(xt, s) + dot(att[rows, :], wo[...])
        mid[rows, :] = h1
        n2 = (h1 * norm_rows(h1) * g2[...]).astype(BF)
        xa_rows(t, s * 128, 128)[...] = dot(n2, feat[...]).astype(BF)
    ring = RingGather(me, xa_rows, sxr, rxr)
    ring.first()
    das[pl.ds(256, 256), :] = dot(att[...], pool[pl.ds(OUTS, 512), :]).astype(BF)
    gc.opposite()
    gf.last()
    gf.drain()

    gives = []

    def chunk(slot, dpart, opart):
        rows = chunk_rows(0, slot)
        x = pool[chunk_rows(1024, slot), :]
        dy = pool[rows, :]
        for n0, nw in ((0, 256), (256, 256), (512, 256), (768, 128)):
            cols = slice(n0, n0 + nw)
            g = dot(x, wf[0, :, cols])
            u = dot(x, wf[1, :, cols])
            dh = dot(dy, wf[2, :, cols])
            sq_g = g * g
            th = jnp.tanh(GELU_C * g * (1.0 + 0.044715 * sq_g))
            up = 0.5 * (1.0 + th)
            gelu = g * up
            slope = up + 0.5 * g * (1.0 - th * th) * (GELU_C * (1.0 + 0.134145 * sq_g))
            hgu[0, rows, cols] = (gelu * u).astype(BF)
            hgu[1, rows, cols] = (dh * u * slope).astype(BF)
            hgu[2, rows, cols] = (dh * gelu).astype(BF)
        dpart[...] = (dot(hgu[1, rows, :], wf[0], NT) + dot(hgu[2, rows, :], wf[1], NT)).astype(BF)
        opart[...] = dot(hgu[0, rows, :], wf[2], NT).astype(BF)

    def give(k, d):
        cp = remote(
            r1.at[pl.ds(k * ROWS, ROWS)], pool.at[pl.ds(RECV + k * ROWS, ROWS)],
            sd.at[k], rd.at[k], me.x(d), "give",
        )
        cp.start()
        gives.append(cp)

    chunk(t, own.at[0], own.at[1])
    for k in (0, 1):
        ring.arrived(k)
        ring.relay(k)
    chunk(ring.slot(-1), r1.at[pl.ds(0, ROWS)], r1.at[pl.ds(768, ROWS)])
    give(0, -1)
    chunk(ring.slot(1), r1.at[pl.ds(256, ROWS)], r1.at[pl.ds(1024, ROWS)])
    give(1, 1)
    ring.opposite()
    chunk(ring.slot(2), r1.at[pl.ds(512, ROWS)], own.at[2])
    give(2, 2)

    for m in range(6):
        cols = slice(m * 256, m * 256 + 256)
        x = pool[1024:2048, cols]
        wf[0, cols, :] = dot(x, hgu[1], TN).astype(BF)
        wf[1, cols, :] = dot(x, hgu[2], TN).astype(BF)
        wf[2, cols, :] = dot(pool[0:1024, cols], hgu[0], TN).astype(BF)
    pl.semaphore_signal(credit.at[0], inc=1, device_id=me.sibling(), device_id_type=MESH)
    mine_row, their_row = core * 768, (1 - core) * 768
    rf32 = Reduce32(
        me, lambda r, n: wf_rows(mine_row + r, n), lambda r, n: wf_rows(their_row + r, n),
        lambda r, n: hgu.at[:, pl.ds(pl.multiple_of(r, 16), n), :], srf, rrf, credit.at[1],
    )
    pl.semaphore_wait(credit.at[0], 1)
    for group in rf32.order:
        rf32.across(group)

    for g in (gc, ring, eo):
        g.drain()
    for cp in gives:
        cp.wait_recv()
    gain2 = jnp.zeros((1, DP), F32)
    for s in range(2):
        rows = pl.ds(s * 128, 128)
        total = own[0, rows, :].astype(F32)
        for k in range(3):
            total = total + pool[pl.ds(RECV + k * ROWS + s * 128, 128), :].astype(F32)
        dxn2 = dot(total.astype(BF), feat[...], NT)
        h1 = mid[rows, :]
        r2 = norm_rows(h1)
        n2 = h1 * r2
        gain2 = gain2 + jnp.sum(dxn2 * n2, axis=0, keepdims=True)
        e2 = dxn2 * g2[...]
        mean = jnp.sum(e2 * n2, axis=1, keepdims=True) * (1.0 / D)
        d = rows_of(ct, s) + r2 * (e2 - n2 * mean)
        gi_o[s] = jnp.transpose(d)[0:D]
        da = d.astype(BF)
        xs[pl.ds(256 + s * 128, 128), :] = da
        do = dot(da, wo[...], NT).astype(BF)
        for j in range(4):
            obuf[s * 4 + j] = do[:, j * 128 : (j + 1) * 128]
    pl.semaphore_signal(credit.at[2], inc=1, device_id=me.sibling(), device_id_type=MESH)
    ed = Exchange(me, obuf, dor, sdo, rdo)
    ed.start()
    outsends = []

    def send_out(k, d, src):
        dst = pool.at[pl.ds(OUT + k * ROWS, ROWS)]
        cp = remote(src, dst, st.at[k], rt.at[k], me.x(d), "out")
        cp.start()
        outsends.append(cp)

    send_out(0, -1, r1.at[pl.ds(768, ROWS)])
    send_out(1, 1, r1.at[pl.ds(1024, ROWS)])
    acc[...] = jnp.zeros_like(acc)
    skew[...] = jnp.zeros_like(skew)
    eq.drain()
    rf32.release()
    rf32.first()
    ed.wait()

    def attend_back(n, block, p, q, do):
        start = pl.multiple_of(LEN - p * 128, 128)
        pb = prob[block]
        probs = pb.astype(F32)
        dp = dot(do, kv[2 * n + 1], NT)
        delta = jnp.sum(dp * probs, axis=1, keepdims=True)
        ds = (probs * (dp - delta)).astype(BF)
        cols = pl.ds(start, LEN)
        skew[n, :, cols] = skew[n, :, cols] + ds.astype(F32)
        acc[2 * n] = acc[2 * n] + dot(ds, q, TN)
        acc[2 * n + 1] = acc[2 * n + 1] + dot(pb, do, TN)
        return dot(ds, kv[2 * n]).astype(BF)

    def whole_back(p, _):
        zbuf[p, :, 0:64] = attend_back(0, p, p, qkv[p, :, 0:64], dor[p, :, 0:64])
        zbuf[p, :, 320:384] = jnp.zeros((128, 64), BF)
        return 0

    lax.fori_loop(0, 8, whole_back, 0)

    def shared_back(i, _):
        p = half * 4 + i
        zbuf[p, :, 320:384] = attend_back(1, 8 + i, p, qkv[p, :, 320:384], dor[p, :, 64:128])
        return 0

    lax.fori_loop(0, 4, shared_back, 0)
    for p in range(8):
        for n in range(4):
            zbuf[p, :, 64 + n * 64 : 128 + n * 64] = acc[n, pl.ds(p * 128, 128), :].astype(BF)
    ez = Exchange(me, zbuf, dr, sdq, rdq)
    ez.start()
    for cp in gives + outsends:
        cp.wait_send()
    load_heads = local(heads_h, r1, 1)
    rf32.second()

    row = lax.broadcasted_iota(jnp.int32, (128, 2048), 0)
    bias = jnp.zeros((32, 128), F32)
    for n, head in ((0, whole), (1, shared)):
        tilted = skew[n]
        for b in range(7):
            moved = pltpu.roll(tilted, 2048 - (1 << b), 1)
            tilted = jnp.where(lax.rem(lax.div(row, 1 << b), 2) == 1, moved, tilted)
        line = jnp.sum(tilted, axis=0, keepdims=True)
        column = jnp.sum(jnp.where(onehot, line, 0.0), axis=1, keepdims=True)
        bias = bias + jnp.where(lane == head, column, 0.0)
    bias_rows = jnp.transpose(jnp.concatenate([bias, jnp.zeros((96, 128), F32)], axis=0))

    load_heads.wait()
    ez.wait()
    for s in range(2):
        d = jnp.concatenate([dr[s * 4 + j] for j in range(4)], axis=1)
        das[pl.ds(s * 128, 128), :] = dot(d, r1[...], NT).astype(BF)
    load_wall = local(wall_o, r1, 3)
    send_out(2, 2, own.at[2])
    ra32 = Reduce32(
        me,
        lambda r, n: pool.at[pl.ds(pl.multiple_of(mine_row + r, 16), n), :],
        lambda r, n: pool.at[pl.ds(pl.multiple_of(their_row + r, 16), n), :],
        lambda r, n: pool.at[pl.ds(pl.multiple_of(RECV + r, 16), n), :],
        sra, rra, credit.at[3],
    )
    pl.semaphore_wait(credit.at[2], 1)
    for base, out in ((their_row, True), (mine_row, False)):
        for n in range(2):
            pair = lax.rem(ra32.pair + n, 2)
            rows = pl.ds(pl.multiple_of(base + pair * 384, 128), 384)
            pool[rows, :] = dot(das[:, rows], xs[...], TN).astype(BF)
            if out:
                for group in ra32.order[2 * n : 2 * n + 2]:
                    ra32.across(group)
    ra32.release()

    load_wall.wait()
    gain1 = jnp.zeros((1, DP), F32)
    for s in range(2):
        rows = pl.ds(s * 128, 128)
        dxn = dot(das[rows, :], r1[...])
        x = rows_of(xt, s)
        r1x = norm_rows(x)
        n1 = x * r1x
        gain1 = gain1 + jnp.sum(dxn * n1, axis=0, keepdims=True)
        e1 = dxn * g1[...]
        mean = jnp.sum(e1 * n1, axis=1, keepdims=True) * (1.0 / D)
        gi_o[s] = gi_o[s] + jnp.transpose(r1x * (e1 - n1 * mean))[0:D]
    sm[0, 0:1, :] = gain1
    sm[0, 1:2, :] = gain2
    sm[0, 2:8, :] = jnp.zeros((6, DP), F32)
    sm[0, 2:8, 0:128] = bias_rows[0:6]

    small_sent = []

    def small(n, devs):
        cps = []
        for k, dev in enumerate(devs):
            i = n * 3 + k
            cp = remote(sm.at[n], rm.at[i], sms.at[i], rms.at[i], dev, "small")
            cp.start()
            cps.append(cp)
        small_sent.extend(cps)
        return cps

    def gather_small(n, cps):
        total = sm[n]
        for k, cp in enumerate(cps):
            cp.wait_recv()
            total = total + rm[n * 3 + k]
        sm[n + 1] = total

    c = small(0, [me.x(d) for d in (1, 2, 3)])
    ra32.first()
    gather_small(0, c)
    c = small(1, [me.at(d, 0) for d in (1, 2, 3)])
    gf_o[...] = rf32.last()
    ra32.second()
    gather_small(1, c)
    c = small(2, [me.at(0, d) for d in (1, 2, 3)])

    for cp in outsends:
        cp.wait_recv()
    for s in range(2):
        rows = pl.ds(s * 128, 128)
        total = own[1, rows, :].astype(F32)
        for k in range(3):
            total = total + pool[pl.ds(OUT + k * ROWS + s * 128, 128), :].astype(F32)
        lo_o[s] = jnp.transpose(mid[rows, :] + dot(total.astype(BF), feat[...], NT))[0:D]

    mine = ra32.last().astype(BF)
    sx[...] = dot(stage[...], mine, TN).astype(BF)
    gather_small(2, c)
    c = small(3, [me.sibling()])
    last = []
    for k, d in enumerate((1, 3, 2)):
        rows = pl.ds(pl.multiple_of(lax.rem(t + d, 4) * 16, 16), 16)
        cp = remote(sx.at[rows], rx.at[k], sxs.at[k], rxs.at[k], me.x(d), "sx")
        cp.start()
        last.append(cp)
    gather_small(3, c)
    small_o[...] = sm[4]
    total = sx[pl.ds(pl.multiple_of(t * 16, 16), 16), :].astype(F32)
    for k, cp in enumerate(last):
        cp.wait_recv()
        total = total + rx[k].astype(F32)
    ga_o[...] = total
    outsends[2].wait_send()
    for cp in last + small_sent:
        cp.wait_send()
    for g in (rf32, ra32, ed, ez):
        g.drain()


VM = pl.BlockSpec(memory_space=pltpu.VMEM)
HB = pl.BlockSpec(memory_space=pl.ANY)
DMA = pltpu.SemaphoreType.DMA


def sds(shape, dtype=BF):
    return jax.ShapeDtypeStruct(shape, dtype)


def layer(*args):
    V = pltpu.VMEM
    return pl.pallas_call(
        layer_kernel,
        name="layer",
        out_shape=(
            sds((8, DP), F32), sds((16, DP), F32), sds((3, 48, FS), F32),
            sds((2, D, 128), F32), sds((2, D, 128), F32), sds((DP, DP)),
        ),
        in_specs=[VM] * 15 + [HB] * 3,
        out_specs=[VM] * 5 + [HB],
        scratch_shapes=[
            V((14 * ROWS, DP), BF), V((DP, DP), BF), V((DP, DP), BF), V((3, ROWS, DP), BF),
            V((3, DP, FS), BF), V((3, 4 * ROWS, FS), BF), V((8, 128, 384), BF),
            V((8, 128, 384), BF), V((8, 128, 384), BF), V((4, LEN, 64), BF), V((4, LEN, 64), F32),
            V((12, 128, LEN), BF), V((2, 128, 2048), F32), V((LEN, 128), F32), V((512, DP), BF),
            V((8, 128, 128), BF), V((8, 128, 128), BF), V((8, 128, 128), BF), V((ROWS, 512), BF),
            V((ROWS, DP), F32), V((512, DP), BF), V((512, DP), BF), V((64, DP), BF),
            V((3, 16, DP), BF), V((5, 8, DP), F32), V((10, 8, DP), F32), V((16, DP), BF),
            V((1, DP), F32), V((1, DP), F32), V((1, 2048), jnp.int32),
            DMA((4,)), DMA((3,)), DMA((3,)), DMA((31,)), DMA((32,)), DMA((31,)), DMA((32,)),
            DMA((4,)), DMA((4,)), DMA((7,)), DMA((7,)), DMA((7,)), DMA((7,)), DMA((4,)),
            DMA((4,)), DMA((3,)), DMA((3,)), DMA((3,)), DMA((3,)), DMA((7,)), DMA((7,)),
            DMA((7,)), DMA((7,)), DMA((10,)), DMA((10,)), DMA((10,)), DMA((10,)), DMA((3,)),
            DMA((3,)), DMA((10,)), DMA((10,)), pltpu.SemaphoreType.REGULAR((4,)),
        ],
        compiler_params=pltpu.CompilerParams(
            collective_id=0, has_side_effects=True, vmem_limit_bytes=64 * 2**20 - 2**17
        ),
    )(*args)


def finish_kernel(small, ga, gf, lo_h, gi_h, lo_o, gi_o, s1, s2, sb, q, k, v, o, g, u, d, sem):
    copies = [
        pltpu.make_async_copy(a, b, sem.at[i])
        for i, (a, b) in enumerate(((lo_h, lo_o), (gi_h, gi_o)))
    ]
    for cp in copies:
        cp.start()
    s1[...] = small[0:1, 0:D].reshape(D)
    s2[...] = small[1:2, 0:D].reshape(D)
    sb[...] = small[2:8, 0:32]
    for n, ref in enumerate((q, k, v, o)):
        ref[...] = ga[3 * n : 3 * n + 3, 0:D]
    for n, ref in enumerate((g, u, d)):
        ref[...] = gf[n, 0:46]
    for cp in copies:
        cp.wait()


def finish(*args):
    return pl.pallas_call(
        finish_kernel,
        name="finish",
        out_shape=(
            (sds((2, D, 128), F32),) * 2 + (sds((D,), F32),) * 2 + (sds((6, 32), F32),)
            + (sds((3, D), F32),) * 4 + (sds((46, FS), F32),) * 3
        ),
        in_specs=[VM] * 3 + [HB] * 2,
        out_specs=[HB] * 2 + [VM] * 10,
        scratch_shapes=[DMA((2,))],
    )(*args)


def per_device(
    inputs, cotangent, segment_ids, buckets, norm_gain_1, norm_gain_2, relative_bias,
    query_weight, key_weight, value_weight, output_weight, gate_weight, up_weight, down_weight,
):
    stored = layer(
        jnp.transpose(inputs, (0, 2, 1)), jnp.transpose(cotangent, (0, 2, 1)),
        query_weight.T, key_weight.T, value_weight.T, output_weight,
        gate_weight, up_weight, down_weight.T,
        segment_ids, buckets, relative_bias.T, norm_gain_1, norm_gain_2, *make_constants(),
    )
    lo, gi, gain1, gain2, bias, q, k, v, o, gate, up, down = finish(*stored[:5])
    return (
        jnp.transpose(lo, (0, 2, 1)), jnp.transpose(gi, (0, 2, 1)), gain1, gain2, bias.T,
        q.T, k.T, v.T, o, gate, up, down.T,
    )


def solution(mesh):
    every = ("fsdp", "ctx", "tp")
    rows = P("fsdp", ("ctx", "tp"), None)
    wide = P(("fsdp", "ctx"), "tp")
    attn = (P(None, every), P(None, every), P(None, every), P(every, None))
    ffn = (wide, wide, P("tp", ("fsdp", "ctx")))
    return jax.shard_map(
        per_device,
        mesh=mesh,
        in_specs=(rows, rows, P("fsdp", None), P(), P(), P(), P()) + attn + ffn,
        out_specs=(rows, rows, P(), P(), P()) + attn + ffn,
        check_vma=False,
    )
```

```python
import functools
import numpy as np
import jax
import jax.numpy as jnp
from jax import lax
from jax.experimental import pallas as pl
from jax.experimental.pallas import tpu as pltpu
from jax.sharding import PartitionSpec as P

D = 1472
DP = 1536
FS = 896
LEN = 1024
PIECE = 128
ROWS = 256
EPS = 1e-6
MESH = pl.DeviceIdType.MESH
BF = jnp.bfloat16
F32 = jnp.float32
NT = (((1,), (1,)), ((), ()))
NN = (((1,), (0,)), ((), ()))
TN = (((0,), (0,)), ((), ()))
GELU_C = 0.7978845608028654
WHOLE_HEAD = (0, 2, 3, 5)
SHARED_HEAD = (1, 1, 4, 4)


def dot(left, right, dims=NN):
    return lax.dot_general(left, right, dims, preferred_element_type=F32)


def block_slot(block):
    f, c = divmod(block, 2)
    y, zh, core = f // 4, (f // 2) % 2, f % 2
    z = zh * 2 + c
    return core * 16 + (y * 4 + z if core == 0 else z * 4 + y)


def make_constants():
    feat = np.zeros((DP, DP), np.float32)
    for r in range(D):
        feat[r, block_slot(r // 46) * 48 + r % 46] = 1
    stage = np.zeros((48, 64), np.float32)
    for w in range(4):
        for t in range(4):
            for i in range(3):
                stage[w * 12 + t * 3 + i, t * 16 + w * 3 + i] = 1

    def gathered(w, col):
        return block_slot(col // 12) * 48 + w * 12 + col % 12

    heads = np.zeros((DP, DP), np.float32)
    outs = np.zeros((DP, 512), np.float32)
    for j in range(4):
        hw, hs = WHOLE_HEAD[j], SHARED_HEAD[j]
        for part, (w, h) in enumerate(
            ((0, hw), (1, hw), (2, hw), (1, hs), (2, hs), (0, hs))
        ):
            for e in range(64):
                heads[gathered(w, h * 64 + e), j * 384 + part * 64 + e] = 1
        for part, h in enumerate((hw, hs)):
            for e in range(64):
                outs[gathered(3, h * 64 + e), j * 128 + part * 64 + e] = 1
    return tuple(a.astype(jnp.bfloat16) for a in (stage, feat, heads, outs.T))


class Place:
    def __init__(self):
        self.f = lax.axis_index("fsdp")
        self.c = lax.axis_index("ctx")
        self.t = lax.axis_index("tp")
        y = lax.div(self.f, 4)
        self.core = lax.rem(self.f, 2)
        z = lax.rem(lax.div(self.f, 2), 2) * 2 + self.c
        self.a1 = y + self.core * (z - y)
        self.a2 = z + self.core * (y - z)
        self.piece = self.c * 4 + self.t

    def at(self, da1, da2, dcore=0):
        core = lax.rem(self.core + dcore, 2)
        if dcore:
            y = self.a1 + self.core * (self.a2 - self.a1)
            z = self.a2 + self.core * (self.a1 - self.a2)
        else:
            b1 = lax.rem(self.a1 + da1, 4)
            b2 = lax.rem(self.a2 + da2, 4)
            y = b1 + core * (b2 - b1)
            z = b2 + core * (b1 - b2)
        return (y * 4 + lax.div(z, 2) * 2 + core, lax.rem(z, 2), self.t)

    def sibling(self):
        return self.at(0, 0, 1)

    def x(self, d):
        return (self.f, self.c, lax.rem(self.t + d + 4, 4))

    def group(self, dc, dt):
        return (self.f, lax.rem(self.c + dc, 2), lax.rem(self.t + dt, 4))

    def group_piece(self, dc, dt):
        return lax.rem(self.c + dc, 2) * 4 + lax.rem(self.t + dt, 4)

    def slot(self, da1=0, da2=0):
        return (
            self.core * 16 + lax.rem(self.a1 + da1, 4) * 4 + lax.rem(self.a2 + da2, 4)
        )

    def all_partners(self):
        out = [self.sibling()]
        for d in (1, 2, 3):
            out += [self.at(d, 0), self.at(0, d), self.x(d), self.group(1, d)]
        return out


GROUP = tuple((dc, dt) for dc in (0, 1) for dt in range(4) if (dc, dt) != (0, 0))


def greet(partners):
    bar = pltpu.get_barrier_semaphore()
    for p in partners:
        pl.semaphore_signal(bar, inc=1, device_id=p, device_id_type=MESH)
    pl.semaphore_wait(bar, len(partners))


def remote(src, dst, ss, rs, dev, tag=None):
    return pltpu.make_async_remote_copy(
        src_ref=src, dst_ref=dst, send_sem=ss, recv_sem=rs, device_id=dev,
        device_id_type=MESH,
    )


class Gather32:
    tag = None

    def __init__(self, me, view, ss, rs):
        self.me, self.view, self.ss, self.rs = me, view, ss, rs
        self.sent = []

    def _send(self, slot, dev):
        k = len(self.sent)
        cp = remote(self.view(slot), self.view(slot), self.ss.at[k], self.rs.at[slot], dev, self.tag)
        cp.start()
        self.sent.append(cp)

    def _arrived(self, slot):
        v = self.view(slot)
        remote(v, v, self.ss.at[0], self.rs.at[slot], self.me.sibling(), self.tag).wait_recv()

    def first(self):
        me = self.me
        for d in (1, 3, 2):
            self._send(me.slot(), me.at(0, d))
        for d in (1, 3, 2):
            self._send(me.slot(), me.at(d, 0))
        self._send(me.slot(), me.sibling())

    def second(self):
        me = self.me
        for d in (1, 3, 2):
            s = me.slot(0, d)
            self._arrived(s)
            for e in (1, 3, 2):
                self._send(s, me.at(e, 0))
            self._send(s, me.sibling())

    def third(self):
        me = self.me
        for d in (0, 1, 3, 2):
            for e in (1, 3, 2):
                s = me.slot(e, d)
                self._arrived(s)
                self._send(s, me.sibling())

    def last(self):
        me = self.me
        base = (1 - me.core) * 16
        for k in range(16):
            self._arrived(base + k)

    def drain(self):
        for cp in self.sent:
            cp.wait_send()


class RingGather:
    tag = None

    def __init__(self, me, buf, ss, rs):
        self.me, self.buf, self.ss, self.rs = me, buf, ss, rs
        self.sent = []

    def slot(self, d):
        return lax.rem(self.me.t + d + 4, 4)

    def _send(self, v, k, d):
        cp = remote(v, v, self.ss.at[k], self.rs.at[k], self.me.x(d), self.tag)
        cp.start()
        self.sent.append(cp)

    def _arrived(self, v, k):
        remote(v, v, self.ss.at[k], self.rs.at[k], self.me.x(1), self.tag).wait_recv()

    def first(self):
        own = self.buf(self.me.t, 0, ROWS)
        self._send(own, 0, 1)
        self._send(own, 1, -1)

    def arrived(self, k):
        self._arrived(self.buf(self.slot(2 * k - 1), 0, ROWS), k)

    def relay(self, k):
        self._send(self.buf(self.slot(2 * k - 1), k * 128, 128), 2 + k, 1 - 2 * k)

    def opposite(self):
        for k in (0, 1):
            self._arrived(self.buf(self.slot(2), k * 128, 128), 2 + k)

    def drain(self):
        for cp in self.sent:
            cp.wait_send()


class Exchange:
    tag = None

    def __init__(self, me, src, dst, ss, rs):
        self.me, self.src, self.dst, self.ss, self.rs = me, src, dst, ss, rs
        self.sent = []

    def start(self):
        me = self.me
        for k, (dc, dt) in enumerate(GROUP):
            cp = remote(
                self.src.at[me.group_piece(dc, dt)], self.dst.at[me.piece],
                self.ss.at[k], self.rs.at[k], me.group(dc, dt), self.tag,
            )
            cp.start()
            self.sent.append(cp)
        self.dst[me.piece] = self.src[me.piece]

    def wait(self):
        me = self.me
        for k, (dc, dt) in enumerate(GROUP):
            v = self.dst.at[me.group_piece((2 - dc) % 2, (4 - dt) % 4)]
            remote(v, v, self.ss.at[k], self.rs.at[k], me.sibling(), self.tag).wait_recv()

    def drain(self):
        for cp in self.sent:
            cp.wait_send()


def norm_rows(rows):
    return lax.rsqrt(jnp.sum(rows * rows, axis=1, keepdims=True) * (1.0 / D) + EPS)


def rows_of(ref, s):
    v = ref[s].astype(F32)
    v = jnp.concatenate([v, jnp.zeros((DP - D, PIECE), F32)], axis=0)
    return jnp.transpose(v)


class Spread:
    ROUNDS = (0, 3, 1, 2)

    def __init__(self, me, src, dst, ss, rs):
        self.me, self.src, self.dst, self.ss, self.rs = me, src, dst, ss, rs
        self.sent = []

    def start(self):
        me = self.me
        for n, d in enumerate(self.ROUNDS):
            for k, (dc, dt) in enumerate(GROUP):
                place = lax.rem(me.t + dt + d, 4)
                cp = remote(
                    self.src.at[lax.rem(me.c + dc, 2) * 4 + place],
                    self.dst.at[place, me.piece],
                    self.ss.at[n * 7 + k], self.rs.at[n * 7 + k], me.group(dc, dt), "spread",
                )
                cp.start()
                self.sent.append(cp)
            place = lax.rem(me.t + d, 4)
            self.dst[place, me.piece] = self.src[me.c * 4 + place]

    def wait(self, n):
        me = self.me
        place = lax.rem(me.t + self.ROUNDS[n], 4)
        for k, (dc, dt) in enumerate(GROUP):
            v = self.dst.at[place, me.group_piece((2 - dc) % 2, (4 - dt) % 4)]
            remote(
                v, v, self.ss.at[n * 7 + k], self.rs.at[n * 7 + k], me.sibling(), "spread"
            ).wait_recv()

    def drain(self):
        for cp in self.sent:
            cp.wait_send()


class Collect:
    def __init__(self, me, src, dst, ss, rs):
        self.me, self.src, self.dst, self.ss, self.rs = me, src, dst, ss, rs
        self.sent = []

    def start(self, n):
        me = self.me
        place = lax.rem(me.t + Spread.ROUNDS[n], 4)
        piece = me.c * 4 + place
        for k, (dc, dt) in enumerate(GROUP):
            cp = remote(
                self.src(n, place, me.group_piece(dc, dt)), self.dst.at[piece, me.t],
                self.ss.at[n * 7 + k], self.rs.at[n * 7 + k], me.group(dc, dt), "collect",
            )
            cp.start()
            self.sent.append(cp)
        self.dst[piece, me.t] = self.src(n, place, me.piece)[...]

    def wait(self):
        me = self.me
        for n in range(4):
            for k, (dc, dt) in enumerate(GROUP):
                c = lax.rem(me.c + dc, 2)
                maker = lax.rem(me.t + 4 - dt, 4)
                v = self.dst.at[c * 4 + lax.rem(maker + Spread.ROUNDS[n], 4), maker]
                remote(
                    v, v, self.ss.at[n * 7 + k], self.rs.at[n * 7 + k], me.sibling(), "collect"
                ).wait_recv()

    def drain(self):
        for cp in self.sent:
            cp.wait_send()


class RingReduce:
    def __init__(self, me, left, right, opposite, landing, ss, rs, tag):
        self.me, self.left, self.right, self.opposite = me, left, right, opposite
        self.landing, self.ss, self.rs, self.tag = landing, ss, rs, tag
        self.sent = []

    def _send(self, src, row, k, d):
        cp = remote(
            src, self.landing(row, 128), self.ss.at[k], self.rs.at[k], self.me.x(d), self.tag
        )
        cp.start()
        self.sent.append(cp)

    def _arrived(self, row, k):
        v = self.landing(row, 128)
        remote(v, v, self.ss.at[k], self.rs.at[k], self.me.x(1), self.tag).wait_recv()

    def over(self):
        self._send(self.opposite(0, 128), 512, 0, 1)
        self._send(self.opposite(128, 128), 640, 1, -1)

    def to_right(self):
        self._send(self.right(128, 128), 128, 2, 1)

    def to_left(self):
        self._send(self.left(0, 128), 256, 3, -1)

    def relay(self):
        for k, view, r, row, d in ((0, self.right, 0, 0, 1), (1, self.left, 128, 384, -1)):
            self._arrived(512 + 128 * k, k)
            v = view(r, 128)
            passed = self.landing(512 + 128 * k, 128)[...]
            v[...] = (v[...].astype(F32) + passed.astype(F32)).astype(BF)
            self._send(v, row, 4 + k, d)

    def wait(self):
        for row, k in ((128, 2), (256, 3), (0, 4), (384, 5)):
            self._arrived(row, k)

    def total(self, own, s):
        return (
            own.astype(F32)
            + self.landing(s * 128, 128)[...].astype(F32)
            + self.landing(256 + s * 128, 128)[...].astype(F32)
        )

    def drain(self):
        for cp in self.sent:
            cp.wait_send()


class Reduce32:
    tag = None

    def __init__(self, me, mine, theirs, landing, ss, rs, free):
        self.me, self.mine, self.theirs, self.landing = me, mine, theirs, landing
        self.ss, self.rs, self.free = ss, rs, free
        self.sent, self.crossing, self.arrays = [], [], []
        self.pair = 1 - lax.div(me.a1, 2)
        mate = me.a1 + 1 - 2 * lax.rem(me.a1, 2)
        self.order = (self.pair * 2, self.pair * 2 + 1, mate, me.a1)

    def _send(self, src, dst, k, dev):
        cp = remote(src, dst, self.ss.at[k], self.rs.at[k], dev, self.tag)
        cp.start()
        self.sent.append(cp)
        return cp

    def across(self, group):
        cp = self._send(
            self.theirs(group * 192, 192), self.landing(group * 192, 192), group,
            self.me.sibling(),
        )
        self.crossing.append(cp)

    def across_array(self, n, src, dst):
        self.arrays.append(self._send(src, dst, n, self.me.sibling()))
        self.crossing.append(self.arrays[-1])

    def release(self):
        for cp in self.crossing:
            cp.wait_send()
            self.sent.remove(cp)
        for d in (1, 2, 3):
            for dev in (self.me.at(d, 0), self.me.at(0, d)):
                pl.semaphore_signal(self.free, inc=1, device_id=dev, device_id_type=MESH)

    def first(self):
        me = self.me
        pl.semaphore_wait(self.free, 6)
        self.one = []
        for cp in self.arrays:
            cp.wait_recv()
        for group in self.order:
            m, there = self.mine(group * 192, 192), self.landing(group * 192, 192)
            if not self.arrays:
                remote(
                    m, there, self.ss.at[group], self.rs.at[group], me.sibling(), self.tag
                ).wait_recv()
            m[...] = (m[...].astype(F32) + there[...].astype(F32)).astype(BF)
            if len(self.one) < 3:
                d = lax.rem(group - me.a1 + 4, 4)
                dst = self.theirs((d - 1) * 192, 192)
                self.one.append(self._send(m, dst, 3 + d, me.at(d, 0)))

    def second(self):
        me = self.me
        m = self.mine(me.a1 * 192, 192)
        for k in range(3):
            v = self.theirs(k * 192, 192)
            remote(v, v, self.ss.at[4 + k], self.rs.at[4 + k], me.sibling(), self.tag).wait_recv()
        total = m[...].astype(F32)
        for k in range(3):
            total = total + self.theirs(k * 192, 192)[...].astype(F32)
        m[...] = total.astype(BF)
        self.two = []
        for k, d in enumerate((1, 3, 2)):
            src = self.mine(me.a1 * 192 + lax.rem(me.a2 + d, 4) * 48, 48)
            self.two.append(self._send(src, self.theirs(576 + k * 48, 48), 7 + k, me.at(0, d)))

    def last(self):
        me = self.me
        for cp in self.two:
            cp.wait_recv()
        total = self.mine(me.a1 * 192 + me.a2 * 48, 48)[...].astype(F32)
        for k in range(3):
            total = total + self.theirs(576 + k * 48, 48)[...].astype(F32)
        return total

    def drain(self):
        for cp in self.sent:
            cp.wait_send()


def layer_kernel(
    xt, ct, wq, wk, wv, wo_in, wg, wu, wd, seg, bk_in, rb, g1_in, g2_in, stage,
    feat_h, heads_h, outs_h,
    small_o, ga_o, gf_o, lo_o, gi_o, wall_o,
    pool, feat, r1, own, wf, hgu, zbuf, qkv, dr, kv, acc, prob, skew, cqs, wo, wop,
    obuf, spread_in, collect_in, xs, das, sx, rx, sm, rm, aw,
    g1, g2, g2p, bk,
    lsem, ssx, rsx, sg, rg, sf, rf, sc, rc, sxr, rxr, sq, rq, so, ro, sd, rd, st, rt,
    sdo, rdo, sdq, rdq, srf, rrf, sra, rra, sxs, rxs, sms, rms, credit,
):
    me = Place()
    core, t = me.core, me.t
    WALL, RECV, OUT = 2048, 2048, 2816

    def local(src, dst, i):
        cp = pltpu.make_async_copy(src, dst, lsem.at[i])
        cp.start()
        return cp

    load_feat = local(feat_h, feat, 0)
    aw[...] = jnp.zeros_like(aw)
    shard = [w[...].astype(F32) for w in (wq, wk, wv, wo_in)] + [jnp.zeros((4, D), F32)]
    aw[:, 0:D] = jnp.concatenate(shard, axis=0).astype(BF)
    greet(me.all_partners())
    load_heads = local(heads_h, r1, 1)
    load_outs = local(outs_h, das, 2)

    xsend = []
    for k, d in enumerate((1, 3, 2)):
        cp = remote(
            aw, sx.at[pl.ds(pl.multiple_of(t * 16, 16), 16)], ssx.at[k], rsx.at[k], me.x(d), "xst"
        )
        cp.start()
        xsend.append(cp)
    sx[pl.ds(pl.multiple_of(t * 16, 16), 16), :] = aw[...]

    for g, g_in in ((g1, g1_in), (g2, g2_in)):
        g[...] = jnp.zeros_like(g)
        g[:, 0:D] = g_in[...].astype(F32).reshape(1, D)
    bk[...] = jnp.zeros_like(bk)
    bk[:, 1:2048] = bk_in[...].reshape(1, 2047)
    for s in range(2):
        rows = rows_of(xt, s)
        xs[pl.ds(s * 128, 128), :] = (rows * norm_rows(rows) * g1[...]).astype(BF)
    for cp in xsend:
        cp.wait()

    def wall_block(slot):
        return pool.at[pl.ds(pl.multiple_of(WALL + slot * 48, 16), 48), :]

    wall_block(me.slot())[...] = dot(stage[...], sx[...]).astype(BF)
    gw = Gather32(me, wall_block, sg, rg)
    gw.first()

    def part_rows(base):
        return lambda i, r, n: pool.at[pl.ds(pl.multiple_of(base + i * ROWS + r, 128), n)]

    gx = RingGather(me, part_rows(1024), sxr, rxr)
    gc = RingGather(me, part_rows(0), sc, rc)
    load_feat.wait()
    for ref, part in ((xt, part_rows(1024)), (ct, part_rows(0))):
        for s in range(2):
            part(t, s * 128, 128)[...] = dot(rows_of(ref, s).astype(BF), feat[...]).astype(BF)
        if ref is xt:
            gx.first()
    gw.second()

    def chunk_rows(base, slot):
        return pl.ds(pl.multiple_of(base + slot * ROWS, ROWS), ROWS)

    whole = t + lax.div(t + 1, 2)
    shared = 1 + 3 * lax.div(t, 2)
    half = lax.rem(t, 2)
    onehot = lax.broadcasted_iota(jnp.int32, (32, 2048), 0) == bk[...]
    lane = lax.broadcasted_iota(jnp.int32, (32, 128), 1)
    by_bucket = jnp.concatenate(
        [jnp.transpose(jnp.pad(rb[...].astype(F32), ((0, 122), (0, 96))))], axis=0
    )[0:32]
    for n, head in ((0, whole), (1, shared)):
        column = jnp.sum(jnp.where(lane == head, by_bucket, 0.0), axis=1, keepdims=True)
        line = jnp.sum(jnp.where(onehot, column, 0.0), axis=0, keepdims=True)
        skew[n] = pltpu.roll(
            jnp.broadcast_to(line, (128, 2048)), 0, 1, stride=1, stride_axis=0
        )
    ids = seg[pl.ds(me.c, 1), :].astype(F32)
    place = lax.broadcasted_iota(jnp.int32, (1, LEN), 1).astype(F32)
    ids = jnp.where(ids == 0.0, -1.0 - place, ids)
    for p in range(8):
        cqs[p : p + 1, :] = ids[:, p * 128 : (p + 1) * 128]

    gw.third()
    gw.last()

    def wf_rows(row, n):
        return wf.at[:, pl.ds(pl.multiple_of(row, 16), n), :]

    def wf_block(slot):
        return wf_rows(slot * 48, 48)

    for n, w in enumerate((wg, wu, wd)):
        wf[n, pl.ds(pl.multiple_of(me.slot() * 48, 16), 48), :] = jnp.concatenate(
            [w[...].astype(F32), jnp.zeros((2, FS), F32)], axis=0
        ).astype(BF)
    gf = Gather32(me, wf_block, sf, rf)
    gf.first()
    for k in (0, 1):
        gx.arrived(k)
        gx.relay(k)

    load_heads.wait()
    y = jnp.concatenate(
        [
            dot(xs[0:256, :], pool[pl.ds(WALL + n * 512, 512), :], NT).astype(BF)
            for n in range(3)
        ],
        axis=1,
    )
    for j in range(4):
        z = dot(y, r1[:, pl.ds(j * 384, 384)]).astype(BF)
        for s in range(2):
            zbuf[s * 4 + j] = z[s * 128 : (s + 1) * 128]
    eq = Exchange(me, zbuf, qkv, sq, rq)
    eq.start()
    store_wall = local(pool.at[pl.ds(WALL, DP)], wall_o, 3)
    gf.second()
    load_outs.wait()
    wo[...] = dot(das[...], pool[pl.ds(WALL, DP), :]).astype(BF)
    wop[...] = dot(wo[...], feat[...]).astype(BF)
    gain = jnp.broadcast_to(g2[...], (16, DP)).astype(BF)
    g2p[...] = dot(gain, feat[...])[0:1]
    eq.wait()
    gc.first()
    for p in range(8):
        rows = pl.ds(p * 128, 128)
        for n, part in enumerate((1, 2, 3, 4)):
            kv[n, rows, :] = qkv[p, :, part * 64 : part * 64 + 64]

    def attend(n, block, p, q):
        start = pl.multiple_of(LEN - p * 128, 128)
        scores = dot(q, kv[2 * n], NT) + skew[n, :, pl.ds(start, LEN)]
        same = jnp.transpose(jnp.broadcast_to(cqs[pl.ds(p, 1), :], (128, 128)))[:, 0:1] == ids
        scores = jnp.where(same, scores, -1e30)
        e = jnp.exp(scores - jnp.max(scores, axis=1, keepdims=True))
        probs = (e * (1.0 / jnp.sum(e, axis=1, keepdims=True))).astype(BF)
        prob[block] = probs
        return dot(probs, kv[2 * n + 1]).astype(BF)

    def whole_step(p, _):
        o = attend(0, p, p, qkv[p, :, 0:64])
        obuf[p, :, 0:64] = o
        obuf[p, :, 64:128] = jnp.zeros((128, 64), BF)
        return 0

    lax.fori_loop(0, 8, whole_step, 0)
    gf.third()

    def shared_step(i, _):
        p = half * 4 + i
        obuf[p, :, 64:128] = attend(1, 8 + i, p, qkv[p, :, 320:384])
        return 0

    lax.fori_loop(0, 4, shared_step, 0)
    gw.drain()
    store_wall.wait()
    spread = Spread(me, obuf, spread_in, so, ro)
    spread.start()
    gx.opposite()
    gx.drain()
    gf.last()
    gf.drain()

    def collect_out(n, place, target):
        return spread_in.at[place, target] if n else obuf.at[target]

    collect = Collect(me, collect_out, collect_in, sdo, rdo)

    def attended(slot, s):
        return jnp.concatenate([spread_in[slot, s * 4 + j] for j in range(4)], axis=1)

    gain_back = jnp.where(g2p[...] > 0.0, 1.0 / jnp.maximum(g2p[...], 0.25), 0.0)

    def chunk(n, dpart, opart):
        slot = lax.rem(t + Spread.ROUNDS[n], 4)
        spread.wait(n)
        rows = chunk_rows(0, slot)
        xrows = chunk_rows(1024, slot)
        h1 = pool[xrows, :].astype(F32) + dot(
            jnp.concatenate([attended(slot, s) for s in range(2)], axis=0), wop[...]
        )
        r2 = norm_rows(h1)
        pool[xrows, :] = (h1 * r2 * g2p[...]).astype(BF)
        x = pool[xrows, :]
        dy = pool[rows, :]
        for n0, nw in ((0, 256), (256, 256), (512, 256), (768, 128)):
            cols = slice(n0, n0 + nw)
            g = dot(x, wf[0, :, cols])
            u = dot(x, wf[1, :, cols])
            dh = dot(dy, wf[2, :, cols])
            sq_g = g * g
            th = jnp.tanh(GELU_C * g * (1.0 + 0.044715 * sq_g))
            up = 0.5 * (1.0 + th)
            gelu = g * up
            slope = up + 0.5 * g * (1.0 - th * th) * (GELU_C * (1.0 + 0.134145 * sq_g))
            hgu[2, rows, cols] = (gelu * u).astype(BF)
            hgu[0, rows, cols] = (dh * u * slope).astype(BF)
            hgu[1, rows, cols] = (dh * gelu).astype(BF)
        dx = dot(hgu[0, rows, :], wf[0], NT) + dot(hgu[1, rows, :], wf[1], NT)
        dpart[...] = dx.astype(BF)
        x = pool[xrows, :].astype(F32)
        mean = jnp.sum(dx * x, axis=1, keepdims=True) * (1.0 / D)
        d = r2 * (dx * g2p[...] - x * (gain_back * mean))
        if n == 0:
            d = d + pool[rows, :].astype(F32)
        do = dot(d.astype(BF), wop[...], NT).astype(BF)
        if n == 0:
            spread.drain()
        for s in range(2):
            for j in range(4):
                block = do[s * 128 : (s + 1) * 128, j * 128 : (j + 1) * 128]
                collect_out(n, slot, s * 4 + j)[...] = block
        collect.start(n)
        opart[...] = dot(hgu[2, rows, :], wf[2], NT).astype(BF)

    def rows_at(ref, base):
        return lambda r, n: ref.at[pl.ds(base + r, n)]

    sum_dx = RingReduce(
        me, rows_at(r1, 0), rows_at(r1, 256), rows_at(r1, 512), rows_at(pool, RECV),
        sd, rd, "dx",
    )
    chunk(0, own.at[0], own.at[1])
    for k in (0, 1):
        gc.arrived(k)
        gc.relay(k)
    chunk(1, r1.at[pl.ds(0, ROWS)], r1.at[pl.ds(768, ROWS)])
    sum_dx.to_left()
    chunk(2, r1.at[pl.ds(256, ROWS)], r1.at[pl.ds(1024, ROWS)])
    sum_dx.to_right()
    gc.opposite()
    chunk(3, r1.at[pl.ds(512, ROWS)], own.at[2])
    sum_dx.over()
    gc.drain()

    mine_row, their_row = core * 768, (1 - core) * 768
    rf32 = Reduce32(
        me, lambda r, n: wf_rows(mine_row + r, n), lambda r, n: wf_rows(their_row + r, n),
        lambda r, n: hgu.at[:, pl.ds(pl.multiple_of(r, 16), n), :], srf, rrf, credit.at[1],
    )
    for i, base in ((2, 0), (0, 1024), (1, 1024)):
        for m in range(6):
            cols = slice(m * 256, m * 256 + 256)
            wf[i, cols, :] = dot(pool[base : base + 1024, cols], hgu[i], TN).astype(BF)
        pl.semaphore_signal(credit.at[0], inc=1, device_id=me.sibling(), device_id_type=MESH)
        pl.semaphore_wait(credit.at[0], 1)
        rf32.across_array(
            i, wf.at[i, pl.ds(pl.multiple_of(their_row, 16), 768)], hgu.at[i, pl.ds(0, 768)]
        )

    acc[...] = jnp.zeros_like(acc)
    skew[...] = jnp.zeros_like(skew)
    eq.drain()
    sum_dx.relay()
    pool[1536:2048, :] = r1[768:1280, :]
    sum_out = RingReduce(
        me, rows_at(pool, 1536), rows_at(pool, 1792), lambda r, n: own.at[2, pl.ds(r, n)],
        rows_at(pool, OUT), st, rt, "out",
    )
    sum_out.over()
    collect.wait()
    for p in range(8):
        do = collect_in[p, 0].astype(F32)
        for k in (1, 2, 3):
            do = do + collect_in[p, k].astype(F32)
        collect_in[p, 0] = do.astype(BF)

    def attend_back(n, block, p, q, do):
        start = pl.multiple_of(LEN - p * 128, 128)
        pb = prob[block]
        probs = pb.astype(F32)
        dp = dot(do, kv[2 * n + 1], NT)
        delta = jnp.sum(dp * probs, axis=1, keepdims=True)
        ds = (probs * (dp - delta)).astype(BF)
        cols = pl.ds(start, LEN)
        skew[n, :, cols] = skew[n, :, cols] + ds.astype(F32)
        acc[2 * n] = acc[2 * n] + dot(q, ds, TN)
        acc[2 * n + 1] = acc[2 * n + 1] + dot(do, pb, TN)
        return dot(ds, kv[2 * n]).astype(BF)

    def whole_back(p, _):
        zbuf[p, :, 0:64] = attend_back(0, p, p, qkv[p, :, 0:64], collect_in[p, 0, :, 0:64])
        zbuf[p, :, 320:384] = jnp.zeros((128, 64), BF)
        return 0

    lax.fori_loop(0, 8, whole_back, 0)
    rf32.release()
    rf32.first()

    def shared_back(i, _):
        p = half * 4 + i
        zbuf[p, :, 320:384] = attend_back(1, 8 + i, p, qkv[p, :, 320:384], collect_in[p, 0, :, 64:128])
        return 0

    lax.fori_loop(0, 4, shared_back, 0)
    for n in range(4):
        grad = jnp.transpose(acc[n]).astype(BF)
        for p in range(8):
            zbuf[p, :, 64 + n * 64 : 128 + n * 64] = grad[p * 128 : (p + 1) * 128]
    ez = Exchange(me, zbuf, dr, sdq, rdq)
    ez.start()

    sum_dx.wait()
    sum_dx.drain()
    load_heads = local(heads_h, r1, 1)
    att = jnp.concatenate([attended(t, s) for s in range(2)], axis=0)
    das[pl.ds(256, 256), :] = dot(att, das[...]).astype(BF)
    gain2 = jnp.zeros((1, DP), F32)
    for s in range(2):
        rows = pl.ds(s * 128, 128)
        dxn2 = dot(sum_dx.total(own[0, rows, :], s).astype(BF), feat[...], NT)
        h1 = rows_of(xt, s) + dot(attended(t, s), wo[...])
        lo_o[s] = jnp.transpose(h1)[0:D]
        r2 = norm_rows(h1)
        n2 = h1 * r2
        gain2 = gain2 + jnp.sum(dxn2 * n2, axis=0, keepdims=True)
        e2 = dxn2 * g2[...]
        mean = jnp.sum(e2 * n2, axis=1, keepdims=True) * (1.0 / D)
        d = rows_of(ct, s) + r2 * (e2 - n2 * mean)
        gi_o[s] = jnp.transpose(d)[0:D]
        xs[pl.ds(256 + s * 128, 128), :] = d.astype(BF)
    pl.semaphore_signal(credit.at[2], inc=1, device_id=me.sibling(), device_id_type=MESH)

    row = lax.broadcasted_iota(jnp.int32, (128, 2048), 0)
    bias = jnp.zeros((32, 128), F32)
    for n, head in ((0, whole), (1, shared)):
        tilted = skew[n]
        for b in range(7):
            moved = pltpu.roll(tilted, 2048 - (1 << b), 1)
            tilted = jnp.where(lax.rem(lax.div(row, 1 << b), 2) == 1, moved, tilted)
        line = jnp.sum(tilted, axis=0, keepdims=True)
        column = jnp.sum(jnp.where(onehot, line, 0.0), axis=1, keepdims=True)
        bias = bias + jnp.where(lane == head, column, 0.0)
    bias_rows = jnp.transpose(jnp.concatenate([bias, jnp.zeros((96, 128), F32)], axis=0))

    load_heads.wait()
    ez.wait()
    for s in range(2):
        d = jnp.concatenate([dr[s * 4 + j] for j in range(4)], axis=1)
        das[pl.ds(s * 128, 128), :] = dot(d, r1[...], NT).astype(BF)
    load_wall = local(wall_o, r1, 3)
    sum_out.relay()
    sum_out.to_right()
    sum_out.to_left()
    ra32 = Reduce32(
        me,
        lambda r, n: pool.at[pl.ds(pl.multiple_of(mine_row + r, 16), n), :],
        lambda r, n: pool.at[pl.ds(pl.multiple_of(their_row + r, 16), n), :],
        lambda r, n: pool.at[pl.ds(pl.multiple_of(RECV + r, 16), n), :],
        sra, rra, credit.at[3],
    )
    pl.semaphore_wait(credit.at[2], 1)
    for base, out in ((their_row, True), (mine_row, False)):
        for n in range(2):
            pair = lax.rem(ra32.pair + n, 2)
            rows = pl.ds(pl.multiple_of(base + pair * 384, 128), 384)
            pool[rows, :] = dot(das[:, rows], xs[...], TN).astype(BF)
            if out:
                for group in ra32.order[2 * n : 2 * n + 2]:
                    ra32.across(group)
    ra32.release()

    load_wall.wait()
    gain1 = jnp.zeros((1, DP), F32)
    for s in range(2):
        rows = pl.ds(s * 128, 128)
        dxn = dot(das[rows, :], r1[...])
        x = rows_of(xt, s)
        r1x = norm_rows(x)
        n1 = x * r1x
        gain1 = gain1 + jnp.sum(dxn * n1, axis=0, keepdims=True)
        e1 = dxn * g1[...]
        mean = jnp.sum(e1 * n1, axis=1, keepdims=True) * (1.0 / D)
        gi_o[s] = gi_o[s] + jnp.transpose(r1x * (e1 - n1 * mean))[0:D]
    sm[0, 0:1, :] = gain1
    sm[0, 1:2, :] = gain2
    sm[0, 2:8, :] = jnp.zeros((6, DP), F32)
    sm[0, 2:8, 0:128] = bias_rows[0:6]

    small_sent = []

    def small(n, devs):
        cps = []
        for k, dev in enumerate(devs):
            i = n * 3 + k
            cp = remote(sm.at[n], rm.at[i], sms.at[i], rms.at[i], dev, "small")
            cp.start()
            cps.append(cp)
        small_sent.extend(cps)
        return cps

    def gather_small(n, cps):
        total = sm[n]
        for k, cp in enumerate(cps):
            cp.wait_recv()
            total = total + rm[n * 3 + k]
        sm[n + 1] = total

    c = small(0, [me.x(d) for d in (1, 2, 3)])
    ra32.first()
    gather_small(0, c)
    c = small(1, [me.at(d, 0) for d in (1, 2, 3)])
    rf32.second()
    ra32.second()
    gather_small(1, c)
    c = small(2, [me.at(0, d) for d in (1, 2, 3)])
    gf_o[...] = rf32.last()

    sum_out.wait()
    for s in range(2):
        rows = pl.ds(s * 128, 128)
        total = sum_out.total(own[1, rows, :], s).astype(BF)
        lo_o[s] = lo_o[s] + jnp.transpose(dot(total, feat[...], NT))[0:D]

    mine = ra32.last().astype(BF)
    sx[...] = dot(stage[...], mine, TN).astype(BF)
    gather_small(2, c)
    c = small(3, [me.sibling()])
    last = []
    for k, d in enumerate((1, 3, 2)):
        rows = pl.ds(pl.multiple_of(lax.rem(t + d, 4) * 16, 16), 16)
        cp = remote(sx.at[rows], rx.at[k], sxs.at[k], rxs.at[k], me.x(d), "sx")
        cp.start()
        last.append(cp)
    gather_small(3, c)
    small_o[...] = sm[4]
    total = sx[pl.ds(pl.multiple_of(t * 16, 16), 16), :].astype(F32)
    for k, cp in enumerate(last):
        cp.wait_recv()
        total = total + rx[k].astype(F32)
    ga_o[...] = total
    for cp in last + small_sent:
        cp.wait_send()
    for g in (rf32, ra32, ez, collect, sum_out):
        g.drain()


VM = pl.BlockSpec(memory_space=pltpu.VMEM)
HB = pl.BlockSpec(memory_space=pl.ANY)
DMA = pltpu.SemaphoreType.DMA


def sds(shape, dtype=BF):
    return jax.ShapeDtypeStruct(shape, dtype)


def layer(*args):
    V = pltpu.VMEM
    return pl.pallas_call(
        layer_kernel,
        name="layer",
        out_shape=(
            sds((8, DP), F32), sds((16, DP), F32), sds((3, 48, FS), F32),
            sds((2, D, 128), F32), sds((2, D, 128), F32), sds((DP, DP)),
        ),
        in_specs=[VM] * 15 + [HB] * 3,
        out_specs=[VM] * 5 + [HB],
        scratch_shapes=[
            V((14 * ROWS, DP), BF), V((DP, DP), BF), V((DP, DP), BF), V((3, ROWS, DP), BF),
            V((3, DP, FS), BF), V((3, 4 * ROWS, FS), BF), V((8, 128, 384), BF),
            V((8, 128, 384), BF), V((8, 128, 384), BF), V((4, LEN, 64), BF), V((4, 64, LEN), F32),
            V((12, 128, LEN), BF), V((2, 128, 2048), F32), V((8, 128), F32), V((512, DP), BF),
            V((512, DP), BF), V((8, 128, 128), BF), V((4, 8, 128, 128), BF),
            V((8, 4, 128, 128), BF), V((512, DP), BF), V((512, DP), BF), V((64, DP), BF),
            V((3, 16, DP), BF), V((5, 8, DP), F32), V((10, 8, DP), F32), V((16, DP), BF),
            V((1, DP), F32), V((1, DP), F32), V((1, DP), F32), V((1, 2048), jnp.int32),
            DMA((4,)), DMA((3,)), DMA((3,)), DMA((31,)), DMA((32,)), DMA((31,)), DMA((32,)),
            DMA((4,)), DMA((4,)), DMA((4,)), DMA((4,)), DMA((7,)), DMA((7,)), DMA((28,)),
            DMA((28,)), DMA((6,)), DMA((6,)), DMA((6,)), DMA((6,)), DMA((28,)), DMA((28,)),
            DMA((7,)), DMA((7,)), DMA((10,)), DMA((10,)), DMA((10,)), DMA((10,)), DMA((3,)),
            DMA((3,)), DMA((10,)), DMA((10,)), pltpu.SemaphoreType.REGULAR((4,)),
        ],
        compiler_params=pltpu.CompilerParams(
            collective_id=0, has_side_effects=True, vmem_limit_bytes=64 * 2**20 - 2**17
        ),
    )(*args)


def finish_kernel(small, ga, gf, lo_h, gi_h, lo_o, gi_o, s1, s2, sb, q, k, v, o, g, u, d, sem):
    copies = [
        pltpu.make_async_copy(a, b, sem.at[i])
        for i, (a, b) in enumerate(((lo_h, lo_o), (gi_h, gi_o)))
    ]
    for cp in copies:
        cp.start()
    s1[...] = small[0:1, 0:D].reshape(D)
    s2[...] = small[1:2, 0:D].reshape(D)
    sb[...] = small[2:8, 0:32]
    for n, ref in enumerate((q, k, v, o)):
        ref[...] = ga[3 * n : 3 * n + 3, 0:D]
    for n, ref in enumerate((g, u, d)):
        ref[...] = gf[n, 0:46]
    for cp in copies:
        cp.wait()


def finish(*args):
    return pl.pallas_call(
        finish_kernel,
        name="finish",
        out_shape=(
            (sds((2, D, 128), F32),) * 2 + (sds((D,), F32),) * 2 + (sds((6, 32), F32),)
            + (sds((3, D), F32),) * 4 + (sds((46, FS), F32),) * 3
        ),
        in_specs=[VM] * 5,
        out_specs=[HB] * 2 + [VM] * 10,
        scratch_shapes=[DMA((2,))],
    )(*args)


def per_device(
    inputs, cotangent, segment_ids, buckets, norm_gain_1, norm_gain_2, relative_bias,
    query_weight, key_weight, value_weight, output_weight, gate_weight, up_weight, down_weight,
):
    stored = layer(
        jnp.transpose(inputs, (0, 2, 1)), jnp.transpose(cotangent, (0, 2, 1)),
        query_weight.T, key_weight.T, value_weight.T, output_weight,
        gate_weight, up_weight, down_weight.T,
        segment_ids, buckets, relative_bias.T, norm_gain_1, norm_gain_2, *make_constants(),
    )
    lo, gi, gain1, gain2, bias, q, k, v, o, gate, up, down = finish(*stored[:5])
    return (
        jnp.transpose(lo, (0, 2, 1)), jnp.transpose(gi, (0, 2, 1)), gain1, gain2, bias.T,
        q.T, k.T, v.T, o, gate, up, down.T,
    )


def solution(mesh):
    every = ("fsdp", "ctx", "tp")
    rows = P("fsdp", ("ctx", "tp"), None)
    wide = P(("fsdp", "ctx"), "tp")
    attn = (P(None, every), P(None, every), P(None, every), P(every, None))
    ffn = (wide, wide, P("tp", ("fsdp", "ctx")))
    return jax.shard_map(
        per_device,
        mesh=mesh,
        in_specs=(rows, rows, P("fsdp", None), P(), P(), P(), P()) + attn + ffn,
        out_specs=(rows, rows, P(), P(), P()) + attn + ffn,
        check_vma=False,
    )
```

```python
import functools
import numpy as np
import jax
import jax.numpy as jnp
from jax import lax
from jax.experimental import pallas as pl
from jax.experimental.pallas import tpu as pltpu
from jax.sharding import PartitionSpec as P

D = 1472
DP = 1536
FS = 896
LEN = 1024
PIECE = 128
ROWS = 256
EPS = 1e-6
MESH = pl.DeviceIdType.MESH
BF = jnp.bfloat16
F32 = jnp.float32
NT = (((1,), (1,)), ((), ()))
NN = (((1,), (0,)), ((), ()))
TN = (((0,), (0,)), ((), ()))
GELU_C = 0.7978845608028654
WHOLE_HEAD = (0, 2, 3, 5)
SHARED_HEAD = (1, 1, 4, 4)


def dot(left, right, dims=NN):
    return lax.dot_general(left, right, dims, preferred_element_type=F32)


def block_slot(block):
    f, c = divmod(block, 2)
    y, zh, core = f // 4, (f // 2) % 2, f % 2
    z = zh * 2 + c
    return core * 16 + (y * 4 + z if core == 0 else z * 4 + y)


def make_constants():
    feat = np.zeros((DP, DP), np.float32)
    for r in range(D):
        feat[r, block_slot(r // 46) * 48 + r % 46] = 1
    stage = np.zeros((48, 64), np.float32)
    for w in range(4):
        for t in range(4):
            for i in range(3):
                stage[w * 12 + t * 3 + i, t * 16 + w * 3 + i] = 1

    def gathered(w, col):
        return block_slot(col // 12) * 48 + w * 12 + col % 12

    heads = np.zeros((DP, DP), np.float32)
    outs = np.zeros((DP, 512), np.float32)
    for j in range(4):
        hw, hs = WHOLE_HEAD[j], SHARED_HEAD[j]
        for part, (w, h) in enumerate(
            ((0, hw), (1, hw), (2, hw), (1, hs), (2, hs), (0, hs))
        ):
            for e in range(64):
                heads[gathered(w, h * 64 + e), j * 384 + part * 64 + e] = 1
        for part, h in enumerate((hw, hs)):
            for e in range(64):
                outs[gathered(3, h * 64 + e), j * 128 + part * 64 + e] = 1
    return tuple(a.astype(jnp.bfloat16) for a in (stage, feat, heads, outs.T))


class Place:
    def __init__(self):
        self.f = lax.axis_index("fsdp")
        self.c = lax.axis_index("ctx")
        self.t = lax.axis_index("tp")
        y = lax.div(self.f, 4)
        self.core = lax.rem(self.f, 2)
        z = lax.rem(lax.div(self.f, 2), 2) * 2 + self.c
        self.a1 = y + self.core * (z - y)
        self.a2 = z + self.core * (y - z)
        self.piece = self.c * 4 + self.t

    def at(self, da1, da2, dcore=0):
        core = lax.rem(self.core + dcore, 2)
        if dcore:
            y = self.a1 + self.core * (self.a2 - self.a1)
            z = self.a2 + self.core * (self.a1 - self.a2)
        else:
            b1 = lax.rem(self.a1 + da1, 4)
            b2 = lax.rem(self.a2 + da2, 4)
            y = b1 + core * (b2 - b1)
            z = b2 + core * (b1 - b2)
        return (y * 4 + lax.div(z, 2) * 2 + core, lax.rem(z, 2), self.t)

    def sibling(self):
        return self.at(0, 0, 1)

    def x(self, d):
        return (self.f, self.c, lax.rem(self.t + d + 4, 4))

    def group(self, dc, dt):
        return (self.f, lax.rem(self.c + dc, 2), lax.rem(self.t + dt, 4))

    def group_piece(self, dc, dt):
        return lax.rem(self.c + dc, 2) * 4 + lax.rem(self.t + dt, 4)

    def slot(self, da1=0, da2=0):
        return (
            self.core * 16 + lax.rem(self.a1 + da1, 4) * 4 + lax.rem(self.a2 + da2, 4)
        )

    def all_partners(self):
        out = [self.sibling()]
        for d in (1, 2, 3):
            out += [self.at(d, 0), self.at(0, d), self.x(d), self.group(1, d)]
        return out


GROUP = tuple((dc, dt) for dc in (0, 1) for dt in range(4) if (dc, dt) != (0, 0))


def greet(partners, meanwhile):
    bar = pltpu.get_barrier_semaphore()
    for p in partners:
        pl.semaphore_signal(bar, inc=1, device_id=p, device_id_type=MESH)
    meanwhile()
    pl.semaphore_wait(bar, len(partners))


def remote(src, dst, ss, rs, dev, tag=None):
    return pltpu.make_async_remote_copy(
        src_ref=src, dst_ref=dst, send_sem=ss, recv_sem=rs, device_id=dev,
        device_id_type=MESH,
    )


class Gather32:
    tag = None

    def __init__(self, me, view, ss, rs, relay=False):
        self.me, self.view, self.ss, self.rs = me, view, ss, rs
        self.relay, self.reach = relay, (1, 3) if relay else (1, 3, 2)
        self.sent = []

    def _send(self, slot, dev):
        k = len(self.sent)
        cp = remote(self.view(slot), self.view(slot), self.ss.at[k], self.rs.at[slot], dev, self.tag)
        cp.start()
        self.sent.append(cp)

    def _arrived(self, slot):
        v = self.view(slot)
        remote(v, v, self.ss.at[0], self.rs.at[slot], self.me.sibling(), self.tag).wait_recv()

    def first(self):
        me = self.me
        for d in (1, 3, 2):
            self._send(me.slot(), me.at(0, d))
        for d in self.reach:
            self._send(me.slot(), me.at(d, 0))
        self._send(me.slot(), me.sibling())

    def second(self):
        me = self.me
        for d in (1, 3, 2):
            s = me.slot(0, d)
            self._arrived(s)
            for e in self.reach:
                self._send(s, me.at(e, 0))
            self._send(s, me.sibling())

    def third(self):
        me = self.me
        for d in range(4):
            for e in (1, 3):
                s = me.slot(e, d)
                self._arrived(s)
                if self.relay and (d < 2) == (e == 3):
                    self._send(s, me.at(4 - e, 0))
                self._send(s, me.sibling())

    def fourth(self):
        me = self.me
        for d in range(4):
            s = me.slot(2, d)
            self._arrived(s)
            self._send(s, me.sibling())

    def last(self):
        me = self.me
        base = (1 - me.core) * 16
        for k in range(16):
            self._arrived(base + k)

    def drain(self):
        for cp in self.sent:
            cp.wait_send()


class RingGather:
    tag = None

    def __init__(self, me, buf, ss, rs):
        self.me, self.buf, self.ss, self.rs = me, buf, ss, rs
        self.sent = []

    def slot(self, d):
        return lax.rem(self.me.t + d + 4, 4)

    def _send(self, v, k, d):
        cp = remote(v, v, self.ss.at[k], self.rs.at[k], self.me.x(d), self.tag)
        cp.start()
        self.sent.append(cp)

    def _arrived(self, v, k):
        remote(v, v, self.ss.at[k], self.rs.at[k], self.me.x(1), self.tag).wait_recv()

    def first(self):
        own = self.buf(self.me.t, 0, ROWS)
        self._send(own, 0, 1)
        self._send(own, 1, -1)

    def arrived(self, k):
        self._arrived(self.buf(self.slot(2 * k - 1), 0, ROWS), k)

    def relay(self, k):
        self._send(self.buf(self.slot(2 * k - 1), k * 128, 128), 2 + k, 1 - 2 * k)

    def opposite(self):
        for k in (0, 1):
            self._arrived(self.buf(self.slot(2), k * 128, 128), 2 + k)

    def drain(self):
        for cp in self.sent:
            cp.wait_send()


class Exchange:
    tag = None
    LANES = ((0, 256), (256, 128))

    def __init__(self, me, src, dst, ss, rs):
        self.me, self.src, self.dst, self.ss, self.rs = me, src, dst, ss, rs
        self.sent = []

    def start(self, part):
        me = self.me
        lanes = pl.ds(*self.LANES[part])
        for k, (dc, dt) in enumerate(GROUP):
            cp = remote(
                self.src.at[me.group_piece(dc, dt), :, lanes], self.dst.at[me.piece, :, lanes],
                self.ss.at[part * 7 + k], self.rs.at[part * 7 + k], me.group(dc, dt), self.tag,
            )
            cp.start()
            self.sent.append(cp)
        self.dst[me.piece, :, lanes] = self.src[me.piece, :, lanes]

    def wait(self, part):
        me = self.me
        lanes = pl.ds(*self.LANES[part])
        for k, (dc, dt) in enumerate(GROUP):
            v = self.dst.at[me.group_piece((2 - dc) % 2, (4 - dt) % 4), :, lanes]
            remote(
                v, v, self.ss.at[part * 7 + k], self.rs.at[part * 7 + k], me.sibling(), self.tag
            ).wait_recv()

    def drain(self):
        for cp in self.sent:
            cp.wait_send()


def norm_rows(rows):
    return lax.rsqrt(jnp.sum(rows * rows, axis=1, keepdims=True) * (1.0 / D) + EPS)


def rows_of(ref, s):
    v = ref[s].astype(F32)
    v = jnp.concatenate([v, jnp.zeros((DP - D, PIECE), F32)], axis=0)
    return jnp.transpose(v)


class Spread:
    ROUNDS = (0, 3, 1, 2)

    def __init__(self, me, src, dst, ss, rs):
        self.me, self.src, self.dst, self.ss, self.rs = me, src, dst, ss, rs
        self.sent = []

    def start(self):
        me = self.me
        for n, d in enumerate(self.ROUNDS):
            for k, (dc, dt) in enumerate(GROUP):
                place = lax.rem(me.t + dt + d, 4)
                cp = remote(
                    self.src.at[lax.rem(me.c + dc, 2) * 4 + place],
                    self.dst.at[place, me.piece],
                    self.ss.at[n * 7 + k], self.rs.at[n * 7 + k], me.group(dc, dt), "spread",
                )
                cp.start()
                self.sent.append(cp)
            place = lax.rem(me.t + d, 4)
            self.dst[place, me.piece] = self.src[me.c * 4 + place]

    def wait(self, n):
        me = self.me
        place = lax.rem(me.t + self.ROUNDS[n], 4)
        for k, (dc, dt) in enumerate(GROUP):
            v = self.dst.at[place, me.group_piece((2 - dc) % 2, (4 - dt) % 4)]
            remote(
                v, v, self.ss.at[n * 7 + k], self.rs.at[n * 7 + k], me.sibling(), "spread"
            ).wait_recv()

    def drain(self):
        for cp in self.sent:
            cp.wait_send()


class Collect:
    def __init__(self, me, src, dst, ss, rs):
        self.me, self.src, self.dst, self.ss, self.rs = me, src, dst, ss, rs
        self.sent = []

    def start(self, n):
        me = self.me
        place = lax.rem(me.t + Spread.ROUNDS[n], 4)
        piece = me.c * 4 + place
        for k, (dc, dt) in enumerate(GROUP):
            cp = remote(
                self.src(n, place, me.group_piece(dc, dt)), self.dst.at[piece, me.t],
                self.ss.at[n * 7 + k], self.rs.at[n * 7 + k], me.group(dc, dt), "collect",
            )
            cp.start()
            self.sent.append(cp)
        self.dst[piece, me.t] = self.src(n, place, me.piece)[...]

    def wait(self):
        me = self.me
        for n in range(4):
            for k, (dc, dt) in enumerate(GROUP):
                c = lax.rem(me.c + dc, 2)
                maker = lax.rem(me.t + 4 - dt, 4)
                v = self.dst.at[c * 4 + lax.rem(maker + Spread.ROUNDS[n], 4), maker]
                remote(
                    v, v, self.ss.at[n * 7 + k], self.rs.at[n * 7 + k], me.sibling(), "collect"
                ).wait_recv()

    def drain(self):
        for cp in self.sent:
            cp.wait_send()


class RingReduce:
    def __init__(self, me, left, right, opposite, landing, ss, rs, tag):
        self.me, self.left, self.right, self.opposite = me, left, right, opposite
        self.landing, self.ss, self.rs, self.tag = landing, ss, rs, tag
        self.sent = []

    def _send(self, src, row, k, d):
        cp = remote(
            src, self.landing(row, 128), self.ss.at[k], self.rs.at[k], self.me.x(d), self.tag
        )
        cp.start()
        self.sent.append(cp)

    def _arrived(self, row, k):
        v = self.landing(row, 128)
        remote(v, v, self.ss.at[k], self.rs.at[k], self.me.x(1), self.tag).wait_recv()

    def over(self):
        self._send(self.opposite(0, 128), 512, 0, 1)
        self._send(self.opposite(128, 128), 640, 1, -1)

    def to_right(self):
        self._send(self.right(128, 128), 128, 2, 1)

    def to_left(self):
        self._send(self.left(0, 128), 256, 3, -1)

    def relay(self):
        for k, view, r, row, d in ((0, self.right, 0, 0, 1), (1, self.left, 128, 384, -1)):
            self._arrived(512 + 128 * k, k)
            v = view(r, 128)
            passed = self.landing(512 + 128 * k, 128)[...]
            v[...] = (v[...].astype(F32) + passed.astype(F32)).astype(BF)
            self._send(v, row, 4 + k, d)

    def wait(self):
        for row, k in ((128, 2), (256, 3), (0, 4), (384, 5)):
            self._arrived(row, k)

    def total(self, own, s):
        return (
            own.astype(F32)
            + self.landing(s * 128, 128)[...].astype(F32)
            + self.landing(256 + s * 128, 128)[...].astype(F32)
        )

    def drain(self):
        for cp in self.sent:
            cp.wait_send()


class Reduce32:
    tag = None

    def __init__(self, me, mine, theirs, landing, ss, rs, free, relay=False):
        self.relay = relay
        self.me, self.mine, self.theirs, self.landing = me, mine, theirs, landing
        self.ss, self.rs, self.free = ss, rs, free
        self.sent, self.crossing, self.arrays = [], [], []
        self.pair = 1 - lax.div(me.a1, 2)
        mate = me.a1 + 1 - 2 * lax.rem(me.a1, 2)
        self.order = (self.pair * 2, self.pair * 2 + 1, mate, me.a1)

    def _send(self, src, dst, k, dev):
        cp = remote(src, dst, self.ss.at[k], self.rs.at[k], dev, self.tag)
        cp.start()
        self.sent.append(cp)
        return cp

    def across(self, group):
        cp = self._send(
            self.theirs(group * 192, 192), self.landing(group * 192, 192), group,
            self.me.sibling(),
        )
        self.crossing.append(cp)

    def across_array(self, n, src, dst):
        self.arrays.append(self._send(src, dst, n, self.me.sibling()))
        self.crossing.append(self.arrays[-1])

    def release(self):
        for cp in self.crossing:
            cp.wait_send()
            self.sent.remove(cp)
        for d in (1, 2, 3):
            for dev in (self.me.at(d, 0), self.me.at(0, d)):
                pl.semaphore_signal(self.free, inc=1, device_id=dev, device_id_type=MESH)

    def first(self):
        me = self.me
        pl.semaphore_wait(self.free, 6)
        self.one = []
        for cp in self.arrays:
            cp.wait_recv()
        for group in self.order:
            m, there = self.mine(group * 192, 192), self.landing(group * 192, 192)
            if not self.arrays:
                remote(
                    m, there, self.ss.at[group], self.rs.at[group], me.sibling(), self.tag
                ).wait_recv()
            m[...] = (m[...].astype(F32) + there[...].astype(F32)).astype(BF)
            if not self.relay and len(self.one) < 3:
                d = lax.rem(group - me.a1 + 4, 4)
                dst = self.theirs((d - 1) * 192, 192)
                self.one.append(self._send(m, dst, 3 + d, me.at(d, 0)))
        if self.relay:
            up, down = (lax.rem(me.a1 + d, 4) * 192 for d in (1, 3))
            over = lax.rem(me.a1 + 2, 4) * 192
            for src, row, k, d in (
                (over, 384, 4, 1), (over + 96, 480, 5, 3), (up + 96, 96, 6, 1), (down, 192, 7, 3),
            ):
                self._send(self.mine(src, 96), self.theirs(row, 96), k, me.at(d, 0))

    def _half_arrived(self, row, k):
        v = self.theirs(row, 96)
        remote(v, v, self.ss.at[k], self.rs.at[k], self.me.sibling(), self.tag).wait_recv()

    def pass_on(self):
        me = self.me
        for n, d, half, row in ((0, 1, 0, 0), (1, 3, 96, 288)):
            self._half_arrived(384 + 96 * n, 4 + n)
            m = self.mine(lax.rem(me.a1 + d, 4) * 192 + half, 96)
            passed = self.theirs(384 + 96 * n, 96)[...]
            m[...] = (m[...].astype(F32) + passed.astype(F32)).astype(BF)
            self._send(m, self.theirs(row, 96), 8 + n, me.at(d, 0))

    def second(self):
        me = self.me
        m = self.mine(me.a1 * 192, 192)
        if self.relay:
            for row, k in ((96, 6), (192, 7), (0, 8), (288, 9)):
                self._half_arrived(row, k)
        else:
            for k in range(3):
                v = self.theirs(k * 192, 192)
                remote(
                    v, v, self.ss.at[4 + k], self.rs.at[4 + k], me.sibling(), self.tag
                ).wait_recv()
        total = m[...].astype(F32)
        for k in range(2 if self.relay else 3):
            total = total + self.theirs(k * 192, 192)[...].astype(F32)
        m[...] = total.astype(BF)
        self.two = []
        for k, d in enumerate((1, 3, 2)):
            src = self.mine(me.a1 * 192 + lax.rem(me.a2 + d, 4) * 48, 48)
            self.two.append(self._send(src, self.theirs(576 + k * 48, 48), 10 + k, me.at(0, d)))

    def last(self):
        me = self.me
        for cp in self.two:
            cp.wait_recv()
        total = self.mine(me.a1 * 192 + me.a2 * 48, 48)[...].astype(F32)
        for k in range(3):
            total = total + self.theirs(576 + k * 48, 48)[...].astype(F32)
        return total

    def drain(self):
        for cp in self.sent:
            cp.wait_send()


def layer_kernel(
    wq, wk, wv, wo_in, wg, wu, wd, seg, bk_in, rb, g1_in, g2_in, stage,
    xt_h, ct_h, feat_h, heads_h, outs_h,
    small_o, ga_o, gf_o, lo_h, gi_h, wall_o,
    xt, ct, lo_o, gi_o,
    pool, feat, r1, own, wf, hgu, zbuf, qkv, dr, kv, acc, prob, skew, cqs, wo, wop,
    obuf, spread_in, collect_in, xs, das, sx, rx, sm, rm, aw,
    g1, g2, g2p, bk,
    lsem, ssx, rsx, sg, rg, sf, rf, sc, rc, sxr, rxr, sq, rq, so, ro, sd, rd, st, rt,
    sdo, rdo, sdq, rdq, srf, rrf, sra, rra, sxs, rxs, sms, rms, credit,
):
    me = Place()
    core, t = me.core, me.t
    WALL, RECV, OUT = 2048, 2048, 2816

    def local(src, dst, i):
        cp = pltpu.make_async_copy(src, dst, lsem.at[i])
        cp.start()
        return cp

    load_xt = local(xt_h, xt, 4)
    load_feat = local(feat_h, feat, 0)
    load_ct = local(ct_h, ct, 5)

    def pack():
        aw[...] = jnp.zeros_like(aw)
        shard = [w[...].astype(F32) for w in (wq, wk, wv, wo_in)] + [jnp.zeros((4, D), F32)]
        aw[:, 0:D] = jnp.concatenate(shard, axis=0).astype(BF)
        for g, g_in in ((g1, g1_in), (g2, g2_in)):
            g[...] = jnp.zeros_like(g)
            g[:, 0:D] = g_in[...].astype(F32).reshape(1, D)
        bk[...] = jnp.zeros_like(bk)
        bk[:, 1:2048] = bk_in[...].reshape(1, 2047)

    greet(me.all_partners(), pack)
    load_heads = local(heads_h, r1, 1)
    load_outs = local(outs_h, das, 2)

    xsend = []
    for k, d in enumerate((1, 3, 2)):
        cp = remote(
            aw, sx.at[pl.ds(pl.multiple_of(t * 16, 16), 16)], ssx.at[k], rsx.at[k], me.x(d), "xst"
        )
        cp.start()
        xsend.append(cp)
    sx[pl.ds(pl.multiple_of(t * 16, 16), 16), :] = aw[...]

    load_xt.wait()
    for s in range(2):
        rows = rows_of(xt, s)
        xs[pl.ds(s * 128, 128), :] = (rows * norm_rows(rows) * g1[...]).astype(BF)
    for cp in xsend:
        cp.wait()

    def wall_block(slot):
        return pool.at[pl.ds(pl.multiple_of(WALL + slot * 48, 16), 48), :]

    wall_block(me.slot())[...] = dot(stage[...], sx[...]).astype(BF)
    gw = Gather32(me, wall_block, sg, rg)
    gw.first()

    def part_rows(base):
        return lambda i, r, n: pool.at[pl.ds(pl.multiple_of(base + i * ROWS + r, 128), n)]

    gx = RingGather(me, part_rows(1024), sxr, rxr)
    gc = RingGather(me, part_rows(0), sc, rc)
    load_feat.wait()
    load_ct.wait()
    for ref, part in ((xt, part_rows(1024)), (ct, part_rows(0))):
        for s in range(2):
            part(t, s * 128, 128)[...] = dot(rows_of(ref, s).astype(BF), feat[...]).astype(BF)
        if ref is xt:
            gx.first()
    gw.second()

    def chunk_rows(base, slot):
        return pl.ds(pl.multiple_of(base + slot * ROWS, ROWS), ROWS)

    def wf_rows(row, n):
        return wf.at[:, pl.ds(pl.multiple_of(row, 16), n), :]

    def wf_block(slot):
        return wf_rows(slot * 48, 48)

    for n, w in enumerate((wg, wu, wd)):
        wf[n, pl.ds(pl.multiple_of(me.slot() * 48, 16), 48), :] = jnp.concatenate(
            [w[...].astype(F32), jnp.zeros((2, FS), F32)], axis=0
        ).astype(BF)
    gf = Gather32(me, wf_block, sf, rf, True)
    gf.first()

    whole = t + lax.div(t + 1, 2)
    shared = 1 + 3 * lax.div(t, 2)
    half = lax.rem(t, 2)
    onehot = lax.broadcasted_iota(jnp.int32, (32, 2048), 0) == bk[...]
    lane = lax.broadcasted_iota(jnp.int32, (32, 128), 1)
    by_bucket = jnp.concatenate(
        [jnp.transpose(jnp.pad(rb[...].astype(F32), ((0, 122), (0, 96))))], axis=0
    )[0:32]
    for n, head in ((0, whole), (1, shared)):
        column = jnp.sum(jnp.where(lane == head, by_bucket, 0.0), axis=1, keepdims=True)
        line = jnp.sum(jnp.where(onehot, column, 0.0), axis=0, keepdims=True)
        skew[n] = pltpu.roll(
            jnp.broadcast_to(line, (128, 2048)), 0, 1, stride=1, stride_axis=0
        )
    ids = seg[pl.ds(me.c, 1), :].astype(F32)
    place = lax.broadcasted_iota(jnp.int32, (1, LEN), 1).astype(F32)
    ids = jnp.where(ids == 0.0, -1.0 - place, ids)
    for p in range(8):
        cqs[p : p + 1, :] = ids[:, p * 128 : (p + 1) * 128]

    gw.third()
    for k in (0, 1):
        gx.arrived(k)
        gx.relay(k)
    gw.fourth()
    gw.last()

    gf.second()

    load_heads.wait()
    y = jnp.concatenate(
        [
            dot(xs[0:256, :], pool[pl.ds(WALL + n * 512, 512), :], NT).astype(BF)
            for n in range(3)
        ],
        axis=1,
    )
    for j in range(4):
        z = dot(y, r1[:, pl.ds(j * 384, 384)]).astype(BF)
        for s in range(2):
            zbuf[s * 4 + j] = z[s * 128 : (s + 1) * 128]
    eq = Exchange(me, zbuf, qkv, sq, rq)
    eq.start(0)
    eq.start(1)
    store_wall = local(pool.at[pl.ds(WALL, DP)], wall_o, 3)
    load_outs.wait()
    wo[...] = dot(das[...], pool[pl.ds(WALL, DP), :]).astype(BF)
    wop[...] = dot(wo[...], feat[...]).astype(BF)
    gain = jnp.broadcast_to(g2[...], (16, DP)).astype(BF)
    g2p[...] = dot(gain, feat[...])[0:1]
    def unpack(parts):
        for p in range(8):
            for n in parts:
                kv[n, pl.ds(p * 128, 128), :] = qkv[p, :, 64 + n * 64 : 128 + n * 64]

    eq.wait(0)
    gc.first()
    unpack((0, 1, 2))

    def attend(n, block, p, q):
        start = pl.multiple_of(LEN - p * 128, 128)
        scores = dot(q, kv[2 * n], NT) + skew[n, :, pl.ds(start, LEN)]
        same = jnp.transpose(jnp.broadcast_to(cqs[pl.ds(p, 1), :], (128, 128)))[:, 0:1] == ids
        scores = jnp.where(same, scores, -1e30)
        e = jnp.exp(scores - jnp.max(scores, axis=1, keepdims=True))
        probs = (e * (1.0 / jnp.sum(e, axis=1, keepdims=True))).astype(BF)
        prob[block] = probs
        return dot(probs, kv[2 * n + 1]).astype(BF)

    def whole_step(p, _):
        o = attend(0, p, p, qkv[p, :, 0:64])
        obuf[p, :, 0:64] = o
        obuf[p, :, 64:128] = jnp.zeros((128, 64), BF)
        return 0

    lax.fori_loop(0, 8, whole_step, 0)
    eq.wait(1)
    unpack((3,))
    gf.third()

    def shared_step(i, _):
        p = half * 4 + i
        obuf[p, :, 64:128] = attend(1, 8 + i, p, qkv[p, :, 320:384])
        return 0

    lax.fori_loop(0, 4, shared_step, 0)
    gw.drain()
    store_wall.wait()
    spread = Spread(me, obuf, spread_in, so, ro)
    spread.start()
    gf.fourth()
    gx.opposite()
    gx.drain()
    gf.last()
    gf.drain()

    def collect_out(n, place, target):
        return spread_in.at[place, target] if n else obuf.at[target]

    collect = Collect(me, collect_out, collect_in, sdo, rdo)

    def attended(slot, s):
        return jnp.concatenate([spread_in[slot, s * 4 + j] for j in range(4)], axis=1)

    gain_back = jnp.where(g2p[...] > 0.0, 1.0 / jnp.maximum(g2p[...], 0.25), 0.0)

    def chunk(n, dpart, opart):
        slot = lax.rem(t + Spread.ROUNDS[n], 4)
        spread.wait(n)
        rows = chunk_rows(0, slot)
        xrows = chunk_rows(1024, slot)
        h1 = pool[xrows, :].astype(F32) + dot(
            jnp.concatenate([attended(slot, s) for s in range(2)], axis=0), wop[...]
        )
        r2 = norm_rows(h1)
        pool[xrows, :] = (h1 * r2 * g2p[...]).astype(BF)
        x = pool[xrows, :]
        dy = pool[rows, :]
        for n0, nw in ((0, 256), (256, 256), (512, 256), (768, 128)):
            cols = slice(n0, n0 + nw)
            g = dot(x, wf[0, :, cols])
            u = dot(x, wf[1, :, cols])
            dh = dot(dy, wf[2, :, cols])
            sq_g = g * g
            th = jnp.tanh(GELU_C * g * (1.0 + 0.044715 * sq_g))
            up = 0.5 * (1.0 + th)
            gelu = g * up
            slope = up + 0.5 * g * (1.0 - th * th) * (GELU_C * (1.0 + 0.134145 * sq_g))
            hgu[2, rows, cols] = (gelu * u).astype(BF)
            hgu[0, rows, cols] = (dh * u * slope).astype(BF)
            hgu[1, rows, cols] = (dh * gelu).astype(BF)
        dx = dot(hgu[0, rows, :], wf[0], NT) + dot(hgu[1, rows, :], wf[1], NT)
        dpart[...] = dx.astype(BF)
        x = pool[xrows, :].astype(F32)
        mean = jnp.sum(dx * x, axis=1, keepdims=True) * (1.0 / D)
        d = r2 * (dx * g2p[...] - x * (gain_back * mean))
        if n == 0:
            d = d + pool[rows, :].astype(F32)
        do = dot(d.astype(BF), wop[...], NT).astype(BF)
        if n == 0:
            spread.drain()
        for s in range(2):
            for j in range(4):
                block = do[s * 128 : (s + 1) * 128, j * 128 : (j + 1) * 128]
                collect_out(n, slot, s * 4 + j)[...] = block
        collect.start(n)
        opart[...] = dot(hgu[2, rows, :], wf[2], NT).astype(BF)

    def rows_at(ref, base):
        return lambda r, n: ref.at[pl.ds(base + r, n)]

    sum_dx = RingReduce(
        me, rows_at(r1, 0), rows_at(r1, 256), rows_at(r1, 512), rows_at(pool, RECV),
        sd, rd, "dx",
    )
    chunk(0, own.at[0], own.at[1])
    for k in (0, 1):
        gc.arrived(k)
        gc.relay(k)
    chunk(1, r1.at[pl.ds(0, ROWS)], r1.at[pl.ds(768, ROWS)])
    sum_dx.to_left()
    chunk(2, r1.at[pl.ds(256, ROWS)], r1.at[pl.ds(1024, ROWS)])
    sum_dx.to_right()
    gc.opposite()
    chunk(3, r1.at[pl.ds(512, ROWS)], own.at[2])
    sum_dx.over()
    gc.drain()

    mine_row, their_row = core * 768, (1 - core) * 768
    rf32 = Reduce32(
        me, lambda r, n: wf_rows(mine_row + r, n), lambda r, n: wf_rows(their_row + r, n),
        lambda r, n: hgu.at[:, pl.ds(pl.multiple_of(r, 16), n), :], srf, rrf, credit.at[1],
        True,
    )
    for n, ws in ((0, (2,)), (1, (0, 1))):
        for m in range(6):
            cols = slice(m * 256, m * 256 + 256)
            term = jnp.concatenate([hgu[i] for i in ws], axis=1)
            grad = dot(pool[n * 1024 : n * 1024 + 1024, cols], term, TN).astype(BF)
            for k, i in enumerate(ws):
                wf[i, cols, :] = grad[:, k * FS : k * FS + FS]
        pl.semaphore_signal(credit.at[0], inc=1, device_id=me.sibling(), device_id_type=MESH)
        pl.semaphore_wait(credit.at[0], 1)
        for i in ws:
            rf32.across_array(
                i, wf.at[i, pl.ds(pl.multiple_of(their_row, 16), 768)], hgu.at[i, pl.ds(0, 768)]
            )

    acc[...] = jnp.zeros_like(acc)
    skew[...] = jnp.zeros_like(skew)
    eq.drain()
    sum_dx.relay()
    pool[1536:2048, :] = r1[768:1280, :]
    sum_out = RingReduce(
        me, rows_at(pool, 1536), rows_at(pool, 1792), lambda r, n: own.at[2, pl.ds(r, n)],
        rows_at(pool, OUT), st, rt, "out",
    )
    collect.wait()
    for p in range(8):
        do = collect_in[p, 0].astype(F32)
        for k in (1, 2, 3):
            do = do + collect_in[p, k].astype(F32)
        collect_in[p, 0] = do.astype(BF)

    def attend_back(n, block, p, q, do):
        start = pl.multiple_of(LEN - p * 128, 128)
        pb = prob[block]
        probs = pb.astype(F32)
        dp = dot(do, kv[2 * n + 1], NT)
        delta = jnp.sum(dp * probs, axis=1, keepdims=True)
        ds = (probs * (dp - delta)).astype(BF)
        cols = pl.ds(start, LEN)
        skew[n, :, cols] = skew[n, :, cols] + ds.astype(F32)
        acc[2 * n] = acc[2 * n] + dot(q, ds, TN)
        acc[2 * n + 1] = acc[2 * n + 1] + dot(do, pb, TN)
        return dot(ds, kv[2 * n]).astype(BF)

    def whole_back(p, _):
        zbuf[p, :, 0:64] = attend_back(0, p, p, qkv[p, :, 0:64], collect_in[p, 0, :, 0:64])
        return 0

    def shared_back(i, _):
        p = half * 4 + i
        zbuf[p, :, 320:384] = attend_back(1, 8 + i, p, qkv[p, :, 320:384], collect_in[p, 0, :, 64:128])
        return 0

    def key_grads(n):
        grad = jnp.transpose(acc[n]).astype(BF)
        for p in range(8):
            zbuf[p, :, 64 + n * 64 : 128 + n * 64] = grad[p * 128 : (p + 1) * 128]

    zbuf[:, :, 320:384] = jnp.zeros((8, 128, 64), BF)
    lax.fori_loop(0, 4, shared_back, 0)
    key_grads(2)
    key_grads(3)
    ez = Exchange(me, zbuf, dr, sdq, rdq)
    ez.start(1)
    lax.fori_loop(0, 4, whole_back, 0)
    rf32.release()
    rf32.first()
    lax.fori_loop(4, 8, whole_back, 0)
    key_grads(0)
    key_grads(1)
    ez.start(0)

    sum_dx.wait()
    sum_dx.drain()
    load_heads = local(heads_h, r1, 1)
    att = jnp.concatenate([attended(t, s) for s in range(2)], axis=0)
    das[pl.ds(256, 256), :] = dot(att, das[...]).astype(BF)
    gain2 = jnp.zeros((1, DP), F32)
    for s in range(2):
        rows = pl.ds(s * 128, 128)
        dxn2 = dot(sum_dx.total(own[0, rows, :], s).astype(BF), feat[...], NT)
        h1 = rows_of(xt, s) + dot(attended(t, s), wo[...])
        lo_o[s] = jnp.transpose(h1)[0:D]
        r2 = norm_rows(h1)
        n2 = h1 * r2
        gain2 = gain2 + jnp.sum(dxn2 * n2, axis=0, keepdims=True)
        e2 = dxn2 * g2[...]
        mean = jnp.sum(e2 * n2, axis=1, keepdims=True) * (1.0 / D)
        d = rows_of(ct, s) + r2 * (e2 - n2 * mean)
        gi_o[s] = jnp.transpose(d)[0:D]
        xs[pl.ds(256 + s * 128, 128), :] = d.astype(BF)
    pl.semaphore_signal(credit.at[2], inc=1, device_id=me.sibling(), device_id_type=MESH)

    row = lax.broadcasted_iota(jnp.int32, (128, 2048), 0)
    bias = jnp.zeros((32, 128), F32)
    for n, head in ((0, whole), (1, shared)):
        tilted = skew[n]
        for b in range(7):
            moved = pltpu.roll(tilted, 2048 - (1 << b), 1)
            tilted = jnp.where(lax.rem(lax.div(row, 1 << b), 2) == 1, moved, tilted)
        line = jnp.sum(tilted, axis=0, keepdims=True)
        column = jnp.sum(jnp.where(onehot, line, 0.0), axis=1, keepdims=True)
        bias = bias + jnp.where(lane == head, column, 0.0)
    bias_rows = jnp.transpose(jnp.concatenate([bias, jnp.zeros((96, 128), F32)], axis=0))

    load_heads.wait()
    rf32.pass_on()
    ez.wait(0)
    ez.wait(1)
    for s in range(2):
        d = jnp.concatenate([dr[s * 4 + j] for j in range(4)], axis=1)
        das[pl.ds(s * 128, 128), :] = dot(d, r1[...], NT).astype(BF)
    load_wall = local(wall_o, r1, 3)
    sum_out.over()
    ra32 = Reduce32(
        me,
        lambda r, n: pool.at[pl.ds(pl.multiple_of(mine_row + r, 16), n), :],
        lambda r, n: pool.at[pl.ds(pl.multiple_of(their_row + r, 16), n), :],
        lambda r, n: pool.at[pl.ds(pl.multiple_of(RECV + r, 16), n), :],
        sra, rra, credit.at[3],
    )
    pl.semaphore_wait(credit.at[2], 1)
    for base, out in ((their_row, True), (mine_row, False)):
        for n in range(2):
            pair = lax.rem(ra32.pair + n, 2)
            rows = pl.ds(pl.multiple_of(base + pair * 384, 128), 384)
            pool[rows, :] = dot(das[:, rows], xs[...], TN).astype(BF)
            if out:
                for group in ra32.order[2 * n : 2 * n + 2]:
                    ra32.across(group)
    ra32.release()
    sum_out.to_right()
    sum_out.to_left()

    load_wall.wait()
    gain1 = jnp.zeros((1, DP), F32)
    for s in range(2):
        rows = pl.ds(s * 128, 128)
        dxn = dot(das[rows, :], r1[...])
        x = rows_of(xt, s)
        r1x = norm_rows(x)
        n1 = x * r1x
        gain1 = gain1 + jnp.sum(dxn * n1, axis=0, keepdims=True)
        e1 = dxn * g1[...]
        mean = jnp.sum(e1 * n1, axis=1, keepdims=True) * (1.0 / D)
        gi_o[s] = gi_o[s] + jnp.transpose(r1x * (e1 - n1 * mean))[0:D]
    store_gi = local(gi_o, gi_h, 5)
    sm[0, 0:1, :] = gain1
    sm[0, 1:2, :] = gain2
    sm[0, 2:8, :] = jnp.zeros((6, DP), F32)
    sm[0, 2:8, 0:128] = bias_rows[0:6]

    small_sent = []

    def small(n, devs):
        cps = []
        for k, dev in enumerate(devs):
            i = n * 3 + k
            cp = remote(sm.at[n], rm.at[i], sms.at[i], rms.at[i], dev, "small")
            cp.start()
            cps.append(cp)
        small_sent.extend(cps)
        return cps

    def gather_small(n, cps):
        total = sm[n]
        for k, cp in enumerate(cps):
            cp.wait_recv()
            total = total + rm[n * 3 + k]
        sm[n + 1] = total

    c = small(0, [me.x(d) for d in (1, 2, 3)])
    ra32.first()
    sum_out.relay()
    gather_small(0, c)
    c = small(1, [me.at(d, 0) for d in (1, 2, 3)])
    rf32.second()
    ra32.second()
    gather_small(1, c)
    c = small(2, [me.at(0, d) for d in (1, 2, 3)])
    gf_o[...] = rf32.last()

    sum_out.wait()
    for s in range(2):
        rows = pl.ds(s * 128, 128)
        total = sum_out.total(own[1, rows, :], s).astype(BF)
        lo_o[s] = lo_o[s] + jnp.transpose(dot(total, feat[...], NT))[0:D]
    store_lo = local(lo_o, lo_h, 4)

    mine = ra32.last().astype(BF)
    sx[...] = dot(stage[...], mine, TN).astype(BF)
    gather_small(2, c)
    c = small(3, [me.sibling()])
    last = []
    for k, d in enumerate((1, 3, 2)):
        rows = pl.ds(pl.multiple_of(lax.rem(t + d, 4) * 16, 16), 16)
        cp = remote(sx.at[rows], rx.at[k], sxs.at[k], rxs.at[k], me.x(d), "sx")
        cp.start()
        last.append(cp)
    gather_small(3, c)
    small_o[...] = sm[4]
    total = sx[pl.ds(pl.multiple_of(t * 16, 16), 16), :].astype(F32)
    for k, cp in enumerate(last):
        cp.wait_recv()
        total = total + rx[k].astype(F32)
    ga_o[...] = total
    for cp in last + small_sent:
        cp.wait_send()
    store_lo.wait()
    store_gi.wait()
    for g in (rf32, ra32, ez, collect, sum_out):
        g.drain()


VM = pl.BlockSpec(memory_space=pltpu.VMEM)
HB = pl.BlockSpec(memory_space=pl.ANY)
DMA = pltpu.SemaphoreType.DMA


def sds(shape, dtype=BF):
    return jax.ShapeDtypeStruct(shape, dtype)


def layer(*args):
    V = pltpu.VMEM
    return pl.pallas_call(
        layer_kernel,
        name="layer",
        out_shape=(
            sds((8, DP), F32), sds((16, DP), F32), sds((3, 48, FS), F32),
            sds((2, D, 128), F32), sds((2, D, 128), F32), sds((DP, DP)),
        ),
        in_specs=[VM] * 13 + [HB] * 5,
        out_specs=[VM] * 3 + [HB] * 3,
        scratch_shapes=[
            V((2, D, 128), BF), V((2, D, 128), BF), V((2, D, 128), F32), V((2, D, 128), F32),
            V((14 * ROWS, DP), BF), V((DP, DP), BF), V((DP, DP), BF), V((3, ROWS, DP), BF),
            V((3, DP, FS), BF), V((3, 4 * ROWS, FS), BF), V((8, 128, 384), BF),
            V((8, 128, 384), BF), V((8, 128, 384), BF), V((4, LEN, 64), BF), V((4, 64, LEN), F32),
            V((12, 128, LEN), BF), V((2, 128, 2048), F32), V((8, 128), F32), V((512, DP), BF),
            V((512, DP), BF), V((8, 128, 128), BF), V((4, 8, 128, 128), BF),
            V((8, 4, 128, 128), BF), V((512, DP), BF), V((512, DP), BF), V((64, DP), BF),
            V((3, 16, DP), BF), V((5, 8, DP), F32), V((10, 8, DP), F32), V((16, DP), BF),
            V((1, DP), F32), V((1, DP), F32), V((1, DP), F32), V((1, 2048), jnp.int32),
            DMA((6,)), DMA((3,)), DMA((3,)), DMA((31,)), DMA((32,)), DMA((31,)), DMA((32,)),
            DMA((4,)), DMA((4,)), DMA((4,)), DMA((4,)), DMA((14,)), DMA((14,)), DMA((28,)),
            DMA((28,)), DMA((6,)), DMA((6,)), DMA((6,)), DMA((6,)), DMA((28,)), DMA((28,)),
            DMA((14,)), DMA((14,)), DMA((13,)), DMA((13,)), DMA((13,)), DMA((13,)), DMA((3,)),
            DMA((3,)), DMA((10,)), DMA((10,)), pltpu.SemaphoreType.REGULAR((4,)),
        ],
        compiler_params=pltpu.CompilerParams(
            collective_id=0, has_side_effects=True, vmem_limit_bytes=64 * 2**20 - 2**17
        ),
    )(*args)


def finish_kernel(
    small, ga, gf, lo_h, gi_h, lo_o, gi_o, s1, s2, sb, q, k, v, o, g, u, d, hold, sem_in, sem_out
):
    steps = [(n, s, r) for n in range(2) for s in range(2) for r in range(4)]

    def into(i):
        n, s, r = steps[i]
        src = (lo_h, gi_h)[n].at[s, pl.ds(r * 368, 368)]
        return pltpu.make_async_copy(src, hold.at[i], sem_in.at[i])

    def out(i):
        n, s, r = steps[i]
        dst = (lo_o, gi_o)[n].at[s, pl.ds(r * 368, 368)]
        return pltpu.make_async_copy(hold.at[i], dst, sem_out.at[i])

    for i in range(16):
        into(i).start()
    for i in range(16):
        into(i).wait()
        out(i).start()
    s1[...] = small[0:1, 0:D].reshape(D)
    s2[...] = small[1:2, 0:D].reshape(D)
    sb[...] = small[2:8, 0:32]
    for n, ref in enumerate((q, k, v, o)):
        ref[...] = ga[3 * n : 3 * n + 3, 0:D]
    for n, ref in enumerate((g, u, d)):
        ref[...] = gf[n, 0:46]
    for i in range(16):
        out(i).wait()


def finish(*args):
    return pl.pallas_call(
        finish_kernel,
        name="finish",
        out_shape=(
            (sds((2, D, 128), F32),) * 2 + (sds((D,), F32),) * 2 + (sds((6, 32), F32),)
            + (sds((3, D), F32),) * 4 + (sds((46, FS), F32),) * 3
        ),
        in_specs=[VM] * 3 + [HB] * 2,
        out_specs=[HB] * 2 + [VM] * 10,
        scratch_shapes=[pltpu.VMEM((16, 368, 128), F32), DMA((16,)), DMA((16,))],
        compiler_params=pltpu.CompilerParams(vmem_limit_bytes=60 * 2**20),
    )(*args)


def per_device(
    inputs, cotangent, segment_ids, buckets, norm_gain_1, norm_gain_2, relative_bias,
    query_weight, key_weight, value_weight, output_weight, gate_weight, up_weight, down_weight,
):
    stage, feat, heads, outs = make_constants()
    stored = layer(
        query_weight.T, key_weight.T, value_weight.T, output_weight,
        gate_weight, up_weight, down_weight.T,
        segment_ids, buckets, relative_bias.T, norm_gain_1, norm_gain_2, stage,
        jnp.transpose(inputs, (0, 2, 1)), jnp.transpose(cotangent, (0, 2, 1)), feat, heads, outs,
    )
    lo, gi, gain1, gain2, bias, q, k, v, o, gate, up, down = finish(*stored[:5])
    return (
        jnp.transpose(lo, (0, 2, 1)), jnp.transpose(gi, (0, 2, 1)), gain1, gain2, bias.T,
        q.T, k.T, v.T, o, gate, up, down.T,
    )


def solution(mesh):
    every = ("fsdp", "ctx", "tp")
    rows = P("fsdp", ("ctx", "tp"), None)
    wide = P(("fsdp", "ctx"), "tp")
    attn = (P(None, every), P(None, every), P(None, every), P(every, None))
    ffn = (wide, wide, P("tp", ("fsdp", "ctx")))
    return jax.shard_map(
        per_device,
        mesh=mesh,
        in_specs=(rows, rows, P("fsdp", None), P(), P(), P(), P()) + attn + ffn,
        out_specs=(rows, rows, P(), P(), P()) + attn + ffn,
        check_vma=False,
    )
```

```python
import functools
import numpy as np
import jax
import jax.numpy as jnp
from jax import lax
from jax.experimental import pallas as pl
from jax.experimental.pallas import tpu as pltpu
from jax.sharding import PartitionSpec as P

D = 1472
DP = 1536
FS = 896
LEN = 1024
PIECE = 128
ROWS = 256
EPS = 1e-6
MESH = pl.DeviceIdType.MESH
BF = jnp.bfloat16
F32 = jnp.float32
NT = (((1,), (1,)), ((), ()))
NN = (((1,), (0,)), ((), ()))
TN = (((0,), (0,)), ((), ()))
GELU_C = 0.7978845608028654
WHOLE_HEAD = (0, 2, 3, 5)
SHARED_HEAD = (1, 1, 4, 4)


def dot(left, right, dims=NN):
    return lax.dot_general(left, right, dims, preferred_element_type=F32)


def block_slot(block):
    f, c = divmod(block, 2)
    y, zh, core = f // 4, (f // 2) % 2, f % 2
    z = zh * 2 + c
    return core * 16 + (y * 4 + z if core == 0 else z * 4 + y)


def make_constants():
    feat = np.zeros((DP, DP), np.float32)
    for r in range(D):
        feat[r, block_slot(r // 46) * 48 + r % 46] = 1
    stage = np.zeros((48, 64), np.float32)
    for w in range(4):
        for t in range(4):
            for i in range(3):
                stage[w * 12 + t * 3 + i, t * 16 + w * 3 + i] = 1

    def gathered(w, col):
        return block_slot(col // 12) * 48 + w * 12 + col % 12

    heads = np.zeros((DP, DP), np.float32)
    outs = np.zeros((DP, 512), np.float32)
    for j in range(4):
        hw, hs = WHOLE_HEAD[j], SHARED_HEAD[j]
        for part, (w, h) in enumerate(
            ((0, hw), (1, hw), (2, hw), (1, hs), (2, hs), (0, hs))
        ):
            for e in range(64):
                heads[gathered(w, h * 64 + e), j * 384 + part * 64 + e] = 1
        for part, h in enumerate((hw, hs)):
            for e in range(64):
                outs[gathered(3, h * 64 + e), j * 128 + part * 64 + e] = 1
    return tuple(a.astype(jnp.bfloat16) for a in (stage, feat, heads, outs.T))


class Place:
    def __init__(self):
        self.f = lax.axis_index("fsdp")
        self.c = lax.axis_index("ctx")
        self.t = lax.axis_index("tp")
        y = lax.div(self.f, 4)
        self.core = lax.rem(self.f, 2)
        z = lax.rem(lax.div(self.f, 2), 2) * 2 + self.c
        self.a1 = y + self.core * (z - y)
        self.a2 = z + self.core * (y - z)
        self.piece = self.c * 4 + self.t

    def at(self, da1, da2, dcore=0):
        core = lax.rem(self.core + dcore, 2)
        if dcore:
            y = self.a1 + self.core * (self.a2 - self.a1)
            z = self.a2 + self.core * (self.a1 - self.a2)
        else:
            b1 = lax.rem(self.a1 + da1, 4)
            b2 = lax.rem(self.a2 + da2, 4)
            y = b1 + core * (b2 - b1)
            z = b2 + core * (b1 - b2)
        return (y * 4 + lax.div(z, 2) * 2 + core, lax.rem(z, 2), self.t)

    def sibling(self):
        return self.at(0, 0, 1)

    def x(self, d):
        return (self.f, self.c, lax.rem(self.t + d + 4, 4))

    def group(self, dc, dt):
        return (self.f, lax.rem(self.c + dc, 2), lax.rem(self.t + dt, 4))

    def group_piece(self, dc, dt):
        return lax.rem(self.c + dc, 2) * 4 + lax.rem(self.t + dt, 4)

    def slot(self, da1=0, da2=0):
        return (
            self.core * 16 + lax.rem(self.a1 + da1, 4) * 4 + lax.rem(self.a2 + da2, 4)
        )

    def all_partners(self):
        out = [self.sibling()]
        for d in (1, 2, 3):
            out += [self.at(d, 0), self.at(0, d), self.x(d), self.group(1, d)]
        return out


GROUP = tuple((dc, dt) for dc in (0, 1) for dt in range(4) if (dc, dt) != (0, 0))


def greet(partners, meanwhile):
    bar = pltpu.get_barrier_semaphore()
    for p in partners:
        pl.semaphore_signal(bar, inc=1, device_id=p, device_id_type=MESH)
    meanwhile()
    pl.semaphore_wait(bar, len(partners))


def remote(src, dst, ss, rs, dev, tag=None):
    return pltpu.make_async_remote_copy(
        src_ref=src, dst_ref=dst, send_sem=ss, recv_sem=rs, device_id=dev,
        device_id_type=MESH,
    )


class Gather32:
    tag = None

    def __init__(self, me, view, ss, rs, relay=False):
        self.me, self.view, self.ss, self.rs = me, view, ss, rs
        self.relay, self.reach = relay, (1, 3) if relay else (1, 3, 2)
        self.sent = []

    def _send(self, slot, dev):
        k = len(self.sent)
        cp = remote(self.view(slot), self.view(slot), self.ss.at[k], self.rs.at[slot], dev, self.tag)
        cp.start()
        self.sent.append(cp)

    def _arrived(self, slot):
        v = self.view(slot)
        remote(v, v, self.ss.at[0], self.rs.at[slot], self.me.sibling(), self.tag).wait_recv()

    def first(self):
        me = self.me
        for d in (1, 3, 2):
            self._send(me.slot(), me.at(0, d))
        for d in self.reach:
            self._send(me.slot(), me.at(d, 0))
        self._send(me.slot(), me.sibling())

    def second(self):
        me = self.me
        for d in (1, 3, 2):
            s = me.slot(0, d)
            self._arrived(s)
            for e in self.reach:
                self._send(s, me.at(e, 0))
            self._send(s, me.sibling())

    def third(self):
        me = self.me
        for d in range(4):
            for e in (1, 3):
                s = me.slot(e, d)
                self._arrived(s)
                if self.relay and (d < 2) == (e == 3):
                    self._send(s, me.at(4 - e, 0))
                self._send(s, me.sibling())

    def fourth(self):
        me = self.me
        for d in range(4):
            s = me.slot(2, d)
            self._arrived(s)
            self._send(s, me.sibling())

    def last(self):
        me = self.me
        base = (1 - me.core) * 16
        for k in range(16):
            self._arrived(base + k)

    def drain(self):
        for cp in self.sent:
            cp.wait_send()


class RingGather:
    tag = None

    def __init__(self, me, buf, ss, rs):
        self.me, self.buf, self.ss, self.rs = me, buf, ss, rs
        self.sent = []

    def slot(self, d):
        return lax.rem(self.me.t + d + 4, 4)

    def _send(self, v, k, d):
        cp = remote(v, v, self.ss.at[k], self.rs.at[k], self.me.x(d), self.tag)
        cp.start()
        self.sent.append(cp)

    def _arrived(self, v, k):
        remote(v, v, self.ss.at[k], self.rs.at[k], self.me.x(1), self.tag).wait_recv()

    def first(self):
        own = self.buf(self.me.t, 0, ROWS)
        self._send(own, 0, 1)
        self._send(own, 1, -1)

    def arrived(self, k):
        self._arrived(self.buf(self.slot(2 * k - 1), 0, ROWS), k)

    def relay(self, k):
        self._send(self.buf(self.slot(2 * k - 1), k * 128, 128), 2 + k, 1 - 2 * k)

    def opposite(self):
        for k in (0, 1):
            self._arrived(self.buf(self.slot(2), k * 128, 128), 2 + k)

    def drain(self):
        for cp in self.sent:
            cp.wait_send()


class Exchange:
    tag = None
    LANES = ((0, 256), (256, 128))

    def __init__(self, me, src, dst, ss, rs):
        self.me, self.src, self.dst, self.ss, self.rs = me, src, dst, ss, rs
        self.sent = []

    def start(self, part):
        me = self.me
        lanes = pl.ds(*self.LANES[part])
        for k, (dc, dt) in enumerate(GROUP):
            cp = remote(
                self.src.at[me.group_piece(dc, dt), :, lanes], self.dst.at[me.piece, :, lanes],
                self.ss.at[part * 7 + k], self.rs.at[part * 7 + k], me.group(dc, dt), self.tag,
            )
            cp.start()
            self.sent.append(cp)
        self.dst[me.piece, :, lanes] = self.src[me.piece, :, lanes]

    def wait(self, part):
        me = self.me
        lanes = pl.ds(*self.LANES[part])
        for k, (dc, dt) in enumerate(GROUP):
            v = self.dst.at[me.group_piece((2 - dc) % 2, (4 - dt) % 4), :, lanes]
            remote(
                v, v, self.ss.at[part * 7 + k], self.rs.at[part * 7 + k], me.sibling(), self.tag
            ).wait_recv()

    def drain(self):
        for cp in self.sent:
            cp.wait_send()


def norm_rows(rows):
    return lax.rsqrt(jnp.sum(rows * rows, axis=1, keepdims=True) * (1.0 / D) + EPS)


def rows_of(ref, s):
    v = ref[s].astype(F32)
    v = jnp.concatenate([v, jnp.zeros((DP - D, PIECE), F32)], axis=0)
    return jnp.transpose(v)


class Spread:
    ROUNDS = (0, 3, 1, 2)

    def __init__(self, me, src, dst, ss, rs):
        self.me, self.src, self.dst, self.ss, self.rs = me, src, dst, ss, rs
        self.sent = []

    def start(self):
        me = self.me
        for n, d in enumerate(self.ROUNDS):
            for k, (dc, dt) in enumerate(GROUP):
                place = lax.rem(me.t + dt + d, 4)
                cp = remote(
                    self.src.at[lax.rem(me.c + dc, 2) * 4 + place],
                    self.dst.at[place, me.piece],
                    self.ss.at[n * 7 + k], self.rs.at[n * 7 + k], me.group(dc, dt), "spread",
                )
                cp.start()
                self.sent.append(cp)
            place = lax.rem(me.t + d, 4)
            self.dst[place, me.piece] = self.src[me.c * 4 + place]

    def wait(self, n):
        me = self.me
        place = lax.rem(me.t + self.ROUNDS[n], 4)
        for k, (dc, dt) in enumerate(GROUP):
            v = self.dst.at[place, me.group_piece((2 - dc) % 2, (4 - dt) % 4)]
            remote(
                v, v, self.ss.at[n * 7 + k], self.rs.at[n * 7 + k], me.sibling(), "spread"
            ).wait_recv()

    def drain(self):
        for cp in self.sent:
            cp.wait_send()


class Collect:
    def __init__(self, me, src, dst, ss, rs):
        self.me, self.src, self.dst, self.ss, self.rs = me, src, dst, ss, rs
        self.sent = []

    def start(self, n):
        me = self.me
        place = lax.rem(me.t + Spread.ROUNDS[n], 4)
        piece = me.c * 4 + place
        for k, (dc, dt) in enumerate(GROUP):
            cp = remote(
                self.src(n, place, me.group_piece(dc, dt)), self.dst.at[piece, me.t],
                self.ss.at[n * 7 + k], self.rs.at[n * 7 + k], me.group(dc, dt), "collect",
            )
            cp.start()
            self.sent.append(cp)
        self.dst[piece, me.t] = self.src(n, place, me.piece)[...]

    def wait(self):
        me = self.me
        for n in range(4):
            for k, (dc, dt) in enumerate(GROUP):
                c = lax.rem(me.c + dc, 2)
                maker = lax.rem(me.t + 4 - dt, 4)
                v = self.dst.at[c * 4 + lax.rem(maker + Spread.ROUNDS[n], 4), maker]
                remote(
                    v, v, self.ss.at[n * 7 + k], self.rs.at[n * 7 + k], me.sibling(), "collect"
                ).wait_recv()

    def drain(self):
        for cp in self.sent:
            cp.wait_send()


class RingReduce:
    def __init__(self, me, left, right, opposite, landing, ss, rs, tag):
        self.me, self.left, self.right, self.opposite = me, left, right, opposite
        self.landing, self.ss, self.rs, self.tag = landing, ss, rs, tag
        self.sent = []

    def _send(self, src, row, k, d):
        cp = remote(
            src, self.landing(row, 128), self.ss.at[k], self.rs.at[k], self.me.x(d), self.tag
        )
        cp.start()
        self.sent.append(cp)

    def _arrived(self, row, k):
        v = self.landing(row, 128)
        remote(v, v, self.ss.at[k], self.rs.at[k], self.me.x(1), self.tag).wait_recv()

    def over(self):
        self._send(self.opposite(0, 128), 512, 0, 1)
        self._send(self.opposite(128, 128), 640, 1, -1)

    def to_right(self):
        self._send(self.right(128, 128), 128, 2, 1)

    def to_left(self):
        self._send(self.left(0, 128), 256, 3, -1)

    def relay(self):
        for k, view, r, row, d in ((0, self.right, 0, 0, 1), (1, self.left, 128, 384, -1)):
            self._arrived(512 + 128 * k, k)
            v = view(r, 128)
            passed = self.landing(512 + 128 * k, 128)[...]
            v[...] = (v[...].astype(F32) + passed.astype(F32)).astype(BF)
            self._send(v, row, 4 + k, d)

    def wait(self):
        for row, k in ((128, 2), (256, 3), (0, 4), (384, 5)):
            self._arrived(row, k)

    def total(self, own, s):
        return (
            own.astype(F32)
            + self.landing(s * 128, 128)[...].astype(F32)
            + self.landing(256 + s * 128, 128)[...].astype(F32)
        )

    def drain(self):
        for cp in self.sent:
            cp.wait_send()


class Reduce32:
    tag = None

    def __init__(self, me, mine, theirs, landing, ss, rs, free, relay=False):
        self.relay = relay
        self.me, self.mine, self.theirs, self.landing = me, mine, theirs, landing
        self.ss, self.rs, self.free = ss, rs, free
        self.sent, self.crossing, self.arrays = [], [], []
        self.pair = 1 - lax.div(me.a1, 2)
        mate = me.a1 + 1 - 2 * lax.rem(me.a1, 2)
        self.order = (self.pair * 2, self.pair * 2 + 1, mate, me.a1)

    def _send(self, src, dst, k, dev):
        cp = remote(src, dst, self.ss.at[k], self.rs.at[k], dev, self.tag)
        cp.start()
        self.sent.append(cp)
        return cp

    def across(self, group):
        cp = self._send(
            self.theirs(group * 192, 192), self.landing(group * 192, 192), group,
            self.me.sibling(),
        )
        self.crossing.append(cp)

    def across_array(self, n, src, dst):
        self.arrays.append(self._send(src, dst, n, self.me.sibling()))
        self.crossing.append(self.arrays[-1])

    def release(self):
        for cp in self.crossing:
            cp.wait_send()
            self.sent.remove(cp)
        for d in (1, 2, 3):
            for dev in (self.me.at(d, 0), self.me.at(0, d)):
                pl.semaphore_signal(self.free, inc=1, device_id=dev, device_id_type=MESH)

    def first(self):
        me = self.me
        pl.semaphore_wait(self.free, 6)
        self.one = []
        for cp in self.arrays:
            cp.wait_recv()
        for group in self.order:
            m, there = self.mine(group * 192, 192), self.landing(group * 192, 192)
            if not self.arrays:
                remote(
                    m, there, self.ss.at[group], self.rs.at[group], me.sibling(), self.tag
                ).wait_recv()
            m[...] = (m[...].astype(F32) + there[...].astype(F32)).astype(BF)
            if not self.relay and len(self.one) < 3:
                d = lax.rem(group - me.a1 + 4, 4)
                dst = self.theirs((d - 1) * 192, 192)
                self.one.append(self._send(m, dst, 3 + d, me.at(d, 0)))
        if self.relay:
            up, down = (lax.rem(me.a1 + d, 4) * 192 for d in (1, 3))
            over = lax.rem(me.a1 + 2, 4) * 192
            for src, row, k, d in (
                (over, 384, 4, 1), (over + 96, 480, 5, 3), (up + 96, 96, 6, 1), (down, 192, 7, 3),
            ):
                self._send(self.mine(src, 96), self.theirs(row, 96), k, me.at(d, 0))

    def _half_arrived(self, row, k):
        v = self.theirs(row, 96)
        remote(v, v, self.ss.at[k], self.rs.at[k], self.me.sibling(), self.tag).wait_recv()

    def pass_on(self):
        me = self.me
        for n, d, half, row in ((0, 1, 0, 0), (1, 3, 96, 288)):
            self._half_arrived(384 + 96 * n, 4 + n)
            m = self.mine(lax.rem(me.a1 + d, 4) * 192 + half, 96)
            passed = self.theirs(384 + 96 * n, 96)[...]
            m[...] = (m[...].astype(F32) + passed.astype(F32)).astype(BF)
            self._send(m, self.theirs(row, 96), 8 + n, me.at(d, 0))

    def second(self):
        me = self.me
        m = self.mine(me.a1 * 192, 192)
        if self.relay:
            for row, k in ((96, 6), (192, 7), (0, 8), (288, 9)):
                self._half_arrived(row, k)
        else:
            for k in range(3):
                v = self.theirs(k * 192, 192)
                remote(
                    v, v, self.ss.at[4 + k], self.rs.at[4 + k], me.sibling(), self.tag
                ).wait_recv()
        total = m[...].astype(F32)
        for k in range(2 if self.relay else 3):
            total = total + self.theirs(k * 192, 192)[...].astype(F32)
        m[...] = total.astype(BF)
        self.two = []
        for k, d in enumerate((1, 3, 2)):
            src = self.mine(me.a1 * 192 + lax.rem(me.a2 + d, 4) * 48, 48)
            self.two.append(self._send(src, self.theirs(576 + k * 48, 48), 10 + k, me.at(0, d)))

    def last(self):
        me = self.me
        for cp in self.two:
            cp.wait_recv()
        total = self.mine(me.a1 * 192 + me.a2 * 48, 48)[...].astype(F32)
        for k in range(3):
            total = total + self.theirs(576 + k * 48, 48)[...].astype(F32)
        return total

    def drain(self):
        for cp in self.sent:
            cp.wait_send()


def layer_kernel(
    wq, wk, wv, wo_in, wg, wu, wd, seg, bk_in, rb, g1_in, g2_in, stage,
    xt_h, ct_h, feat_h, heads_h, outs_h,
    small_o, ga_o, gf_o, lo_h, gi_h, wall_o,
    xt, ct, lo_o, gi_o,
    pool, feat, r1, own, wf, hgu, zbuf, qkv, dr, kv, acc, prob, skew, cqs, wo, wop,
    obuf, spread_in, collect_in, xs, das, sx, rx, sm, rm, aw,
    g1, g2, g2p, bk,
    lsem, ssx, rsx, sg, rg, sf, rf, sc, rc, sxr, rxr, sq, rq, so, ro, sd, rd, st, rt,
    sdo, rdo, sdq, rdq, srf, rrf, sra, rra, sxs, rxs, sms, rms, credit,
):
    me = Place()
    core, t = me.core, me.t
    WALL, RECV, OUT = 2048, 2048, 2816

    def local(src, dst, i):
        cp = pltpu.make_async_copy(src, dst, lsem.at[i])
        cp.start()
        return cp

    load_xt = local(xt_h, xt, 4)
    load_feat = local(feat_h, feat, 0)
    load_ct = local(ct_h, ct, 5)

    def pack():
        aw[...] = jnp.zeros_like(aw)
        shard = [w[...].astype(F32) for w in (wq, wk, wv, wo_in)] + [jnp.zeros((4, D), F32)]
        aw[:, 0:D] = jnp.concatenate(shard, axis=0).astype(BF)
        for g, g_in in ((g1, g1_in), (g2, g2_in)):
            g[...] = jnp.zeros_like(g)
            g[:, 0:D] = g_in[...].astype(F32).reshape(1, D)
        bk[...] = jnp.zeros_like(bk)
        bk[:, 1:2048] = bk_in[...].reshape(1, 2047)

    greet(me.all_partners(), pack)
    load_heads = local(heads_h, r1, 1)
    load_outs = local(outs_h, das, 2)

    xsend = []
    for k, d in enumerate((1, 3, 2)):
        cp = remote(
            aw, sx.at[pl.ds(pl.multiple_of(t * 16, 16), 16)], ssx.at[k], rsx.at[k], me.x(d), "xst"
        )
        cp.start()
        xsend.append(cp)
    sx[pl.ds(pl.multiple_of(t * 16, 16), 16), :] = aw[...]

    load_xt.wait()
    for s in range(2):
        rows = rows_of(xt, s)
        xs[pl.ds(s * 128, 128), :] = (rows * norm_rows(rows) * g1[...]).astype(BF)
    for cp in xsend:
        cp.wait()

    def wall_block(slot):
        return pool.at[pl.ds(pl.multiple_of(WALL + slot * 48, 16), 48), :]

    wall_block(me.slot())[...] = dot(stage[...], sx[...]).astype(BF)
    gw = Gather32(me, wall_block, sg, rg)
    gw.first()

    def part_rows(base):
        return lambda i, r, n: pool.at[pl.ds(pl.multiple_of(base + i * ROWS + r, 128), n)]

    gx = RingGather(me, part_rows(1024), sxr, rxr)
    gc = RingGather(me, part_rows(0), sc, rc)
    load_feat.wait()
    load_ct.wait()
    for ref, part in ((xt, part_rows(1024)), (ct, part_rows(0))):
        for s in range(2):
            part(t, s * 128, 128)[...] = dot(rows_of(ref, s).astype(BF), feat[...]).astype(BF)
        if ref is xt:
            gx.first()
    gw.second()

    def chunk_rows(base, slot):
        return pl.ds(pl.multiple_of(base + slot * ROWS, ROWS), ROWS)

    def wf_rows(row, n):
        return wf.at[:, pl.ds(pl.multiple_of(row, 16), n), :]

    def wf_block(slot):
        return wf_rows(slot * 48, 48)

    for n, w in enumerate((wg, wu, wd)):
        wf[n, pl.ds(pl.multiple_of(me.slot() * 48, 16), 48), :] = jnp.concatenate(
            [w[...].astype(F32), jnp.zeros((2, FS), F32)], axis=0
        ).astype(BF)
    gf = Gather32(me, wf_block, sf, rf, True)
    gf.first()

    whole = t + lax.div(t + 1, 2)
    shared = 1 + 3 * lax.div(t, 2)
    half = lax.rem(t, 2)
    onehot = lax.broadcasted_iota(jnp.int32, (32, 2048), 0) == bk[...]
    lane = lax.broadcasted_iota(jnp.int32, (32, 128), 1)
    by_bucket = jnp.concatenate(
        [jnp.transpose(jnp.pad(rb[...].astype(F32), ((0, 122), (0, 96))))], axis=0
    )[0:32]
    for n, head in ((0, whole), (1, shared)):
        column = jnp.sum(jnp.where(lane == head, by_bucket, 0.0), axis=1, keepdims=True)
        line = jnp.sum(jnp.where(onehot, column, 0.0), axis=0, keepdims=True)
        skew[n] = pltpu.roll(
            jnp.broadcast_to(line, (128, 2048)), 0, 1, stride=1, stride_axis=0
        )
    ids = seg[pl.ds(me.c, 1), :].astype(F32)
    place = lax.broadcasted_iota(jnp.int32, (1, LEN), 1).astype(F32)
    ids = jnp.where(ids == 0.0, -1.0 - place, ids)
    for p in range(8):
        cqs[p : p + 1, :] = ids[:, p * 128 : (p + 1) * 128]

    gw.third()
    for k in (0, 1):
        gx.arrived(k)
        gx.relay(k)
    gw.fourth()
    gw.last()

    gf.second()

    load_heads.wait()
    y = jnp.concatenate(
        [
            dot(xs[0:256, :], pool[pl.ds(WALL + n * 512, 512), :], NT).astype(BF)
            for n in range(3)
        ],
        axis=1,
    )
    for j in range(4):
        z = dot(y, r1[:, pl.ds(j * 384, 384)]).astype(BF)
        for s in range(2):
            zbuf[s * 4 + j] = z[s * 128 : (s + 1) * 128]
    eq = Exchange(me, zbuf, qkv, sq, rq)
    eq.start(0)
    eq.start(1)
    store_wall = local(pool.at[pl.ds(WALL, DP)], wall_o, 3)
    load_outs.wait()
    wo[...] = dot(das[...], pool[pl.ds(WALL, DP), :]).astype(BF)
    wop[...] = dot(wo[...], feat[...]).astype(BF)
    gain = jnp.broadcast_to(g2[...], (16, DP)).astype(BF)
    g2p[...] = dot(gain, feat[...])[0:1]
    def unpack(parts):
        for p in range(8):
            for n in parts:
                kv[n, pl.ds(p * 128, 128), :] = qkv[p, :, 64 + n * 64 : 128 + n * 64]

    eq.wait(0)
    gc.first()
    unpack((0, 1, 2))

    def attend(n, block, p, q):
        start = pl.multiple_of(LEN - p * 128, 128)
        scores = dot(q, kv[2 * n], NT) + skew[n, :, pl.ds(start, LEN)]
        same = jnp.transpose(jnp.broadcast_to(cqs[pl.ds(p, 1), :], (128, 128)))[:, 0:1] == ids
        scores = jnp.where(same, scores, -1e30)
        e = jnp.exp(scores - jnp.max(scores, axis=1, keepdims=True))
        probs = (e * (1.0 / jnp.sum(e, axis=1, keepdims=True))).astype(BF)
        prob[block] = probs
        return dot(probs, kv[2 * n + 1]).astype(BF)

    def whole_step(p, _):
        o = attend(0, p, p, qkv[p, :, 0:64])
        obuf[p, :, 0:64] = o
        obuf[p, :, 64:128] = jnp.zeros((128, 64), BF)
        return 0

    lax.fori_loop(0, 8, whole_step, 0)
    eq.wait(1)
    unpack((3,))
    gf.third()

    def shared_step(i, _):
        p = half * 4 + i
        obuf[p, :, 64:128] = attend(1, 8 + i, p, qkv[p, :, 320:384])
        return 0

    lax.fori_loop(0, 4, shared_step, 0)
    gw.drain()
    store_wall.wait()
    spread = Spread(me, obuf, spread_in, so, ro)
    spread.start()
    gf.fourth()
    gx.opposite()
    gx.drain()
    gf.last()
    gf.drain()

    def collect_out(n, place, target):
        return spread_in.at[place, target] if n else obuf.at[target]

    collect = Collect(me, collect_out, collect_in, sdo, rdo)

    def attended(slot, s):
        return jnp.concatenate([spread_in[slot, s * 4 + j] for j in range(4)], axis=1)

    gain_back = jnp.where(g2p[...] > 0.0, 1.0 / jnp.maximum(g2p[...], 0.25), 0.0)

    def chunk(n, dpart, opart):
        slot = lax.rem(t + Spread.ROUNDS[n], 4)
        spread.wait(n)
        rows = chunk_rows(0, slot)
        xrows = chunk_rows(1024, slot)
        h1 = pool[xrows, :].astype(F32) + dot(
            jnp.concatenate([attended(slot, s) for s in range(2)], axis=0), wop[...]
        )
        r2 = norm_rows(h1)
        pool[xrows, :] = (h1 * r2 * g2p[...]).astype(BF)
        x = pool[xrows, :]
        dy = pool[rows, :]
        for n0, nw in ((0, 256), (256, 256), (512, 256), (768, 128)):
            cols = slice(n0, n0 + nw)
            g = dot(x, wf[0, :, cols])
            u = dot(x, wf[1, :, cols])
            dh = dot(dy, wf[2, :, cols])
            sq_g = g * g
            th = jnp.tanh(GELU_C * g * (1.0 + 0.044715 * sq_g))
            up = 0.5 * (1.0 + th)
            gelu = g * up
            slope = up + 0.5 * g * (1.0 - th * th) * (GELU_C * (1.0 + 0.134145 * sq_g))
            hgu[2, rows, cols] = (gelu * u).astype(BF)
            hgu[0, rows, cols] = (dh * u * slope).astype(BF)
            hgu[1, rows, cols] = (dh * gelu).astype(BF)
        dx = dot(hgu[0, rows, :], wf[0], NT) + dot(hgu[1, rows, :], wf[1], NT)
        dpart[...] = dx.astype(BF)
        x = pool[xrows, :].astype(F32)
        mean = jnp.sum(dx * x, axis=1, keepdims=True) * (1.0 / D)
        d = r2 * (dx * g2p[...] - x * (gain_back * mean))
        if n == 0:
            d = d + pool[rows, :].astype(F32)
        do = dot(d.astype(BF), wop[...], NT).astype(BF)
        if n == 0:
            spread.drain()
        for s in range(2):
            for j in range(4):
                block = do[s * 128 : (s + 1) * 128, j * 128 : (j + 1) * 128]
                collect_out(n, slot, s * 4 + j)[...] = block
        collect.start(n)
        opart[...] = dot(hgu[2, rows, :], wf[2], NT).astype(BF)

    def rows_at(ref, base):
        return lambda r, n: ref.at[pl.ds(base + r, n)]

    sum_dx = RingReduce(
        me, rows_at(r1, 0), rows_at(r1, 256), rows_at(r1, 512), rows_at(pool, RECV),
        sd, rd, "dx",
    )
    chunk(0, own.at[0], own.at[1])
    for k in (0, 1):
        gc.arrived(k)
        gc.relay(k)
    chunk(1, r1.at[pl.ds(0, ROWS)], r1.at[pl.ds(768, ROWS)])
    sum_dx.to_left()
    chunk(2, r1.at[pl.ds(256, ROWS)], r1.at[pl.ds(1024, ROWS)])
    sum_dx.to_right()
    gc.opposite()
    chunk(3, r1.at[pl.ds(512, ROWS)], own.at[2])
    sum_dx.over()
    gc.drain()

    mine_row, their_row = core * 768, (1 - core) * 768
    rf32 = Reduce32(
        me, lambda r, n: wf_rows(mine_row + r, n), lambda r, n: wf_rows(their_row + r, n),
        lambda r, n: hgu.at[:, pl.ds(pl.multiple_of(r, 16), n), :], srf, rrf, credit.at[1],
        True,
    )
    for n, ws in ((0, (2,)), (1, (0, 1))):
        for m in range(6):
            cols = slice(m * 256, m * 256 + 256)
            term = jnp.concatenate([hgu[i] for i in ws], axis=1)
            grad = dot(pool[n * 1024 : n * 1024 + 1024, cols], term, TN).astype(BF)
            for k, i in enumerate(ws):
                wf[i, cols, :] = grad[:, k * FS : k * FS + FS]
        pl.semaphore_signal(credit.at[0], inc=1, device_id=me.sibling(), device_id_type=MESH)
        pl.semaphore_wait(credit.at[0], 1)
        for i in ws:
            rf32.across_array(
                i, wf.at[i, pl.ds(pl.multiple_of(their_row, 16), 768)], hgu.at[i, pl.ds(0, 768)]
            )

    acc[...] = jnp.zeros_like(acc)
    skew[...] = jnp.zeros_like(skew)
    eq.drain()
    sum_dx.relay()
    pool[1536:2048, :] = r1[768:1280, :]
    sum_out = RingReduce(
        me, rows_at(pool, 1536), rows_at(pool, 1792), lambda r, n: own.at[2, pl.ds(r, n)],
        rows_at(pool, OUT), st, rt, "out",
    )
    collect.wait()
    for p in range(8):
        do = collect_in[p, 0].astype(F32)
        for k in (1, 2, 3):
            do = do + collect_in[p, k].astype(F32)
        collect_in[p, 0] = do.astype(BF)

    def attend_back(n, block, p, q, do):
        start = pl.multiple_of(LEN - p * 128, 128)
        pb = prob[block]
        probs = pb.astype(F32)
        dp = dot(do, kv[2 * n + 1], NT)
        delta = jnp.sum(dp * probs, axis=1, keepdims=True)
        ds = (probs * (dp - delta)).astype(BF)
        cols = pl.ds(start, LEN)
        skew[n, :, cols] = skew[n, :, cols] + ds.astype(F32)
        acc[2 * n] = acc[2 * n] + dot(q, ds, TN)
        acc[2 * n + 1] = acc[2 * n + 1] + dot(do, pb, TN)
        return dot(ds, kv[2 * n]).astype(BF)

    def whole_back(p, _):
        zbuf[p, :, 0:64] = attend_back(0, p, p, qkv[p, :, 0:64], collect_in[p, 0, :, 0:64])
        return 0

    def shared_back(i, _):
        p = half * 4 + i
        zbuf[p, :, 320:384] = attend_back(1, 8 + i, p, qkv[p, :, 320:384], collect_in[p, 0, :, 64:128])
        return 0

    def key_grads(n):
        grad = jnp.transpose(acc[n]).astype(BF)
        for p in range(8):
            zbuf[p, :, 64 + n * 64 : 128 + n * 64] = grad[p * 128 : (p + 1) * 128]

    zbuf[:, :, 320:384] = jnp.zeros((8, 128, 64), BF)
    lax.fori_loop(0, 4, shared_back, 0)
    key_grads(2)
    key_grads(3)
    ez = Exchange(me, zbuf, dr, sdq, rdq)
    ez.start(1)
    lax.fori_loop(0, 8, whole_back, 0)
    key_grads(0)
    key_grads(1)
    ez.start(0)
    rf32.release()
    rf32.first()

    sum_dx.wait()
    sum_dx.drain()
    load_heads = local(heads_h, r1, 1)
    att = jnp.concatenate([attended(t, s) for s in range(2)], axis=0)
    das[pl.ds(256, 256), :] = dot(att, das[...]).astype(BF)
    gain2 = jnp.zeros((1, DP), F32)
    for s in range(2):
        rows = pl.ds(s * 128, 128)
        dxn2 = dot(sum_dx.total(own[0, rows, :], s).astype(BF), feat[...], NT)
        h1 = rows_of(xt, s) + dot(attended(t, s), wo[...])
        lo_o[s] = jnp.transpose(h1)[0:D]
        r2 = norm_rows(h1)
        n2 = h1 * r2
        gain2 = gain2 + jnp.sum(dxn2 * n2, axis=0, keepdims=True)
        e2 = dxn2 * g2[...]
        mean = jnp.sum(e2 * n2, axis=1, keepdims=True) * (1.0 / D)
        d = rows_of(ct, s) + r2 * (e2 - n2 * mean)
        gi_o[s] = jnp.transpose(d)[0:D]
        xs[pl.ds(256 + s * 128, 128), :] = d.astype(BF)
    pl.semaphore_signal(credit.at[2], inc=1, device_id=me.sibling(), device_id_type=MESH)

    row = lax.broadcasted_iota(jnp.int32, (128, 2048), 0)
    bias = jnp.zeros((32, 128), F32)
    for n, head in ((0, whole), (1, shared)):
        tilted = skew[n]
        for b in range(7):
            moved = pltpu.roll(tilted, 2048 - (1 << b), 1)
            tilted = jnp.where(lax.rem(lax.div(row, 1 << b), 2) == 1, moved, tilted)
        line = jnp.sum(tilted, axis=0, keepdims=True)
        column = jnp.sum(jnp.where(onehot, line, 0.0), axis=1, keepdims=True)
        bias = bias + jnp.where(lane == head, column, 0.0)
    bias_rows = jnp.transpose(jnp.concatenate([bias, jnp.zeros((96, 128), F32)], axis=0))

    load_heads.wait()
    rf32.pass_on()
    ez.wait(0)
    ez.wait(1)
    for s in range(2):
        d = jnp.concatenate([dr[s * 4 + j] for j in range(4)], axis=1)
        das[pl.ds(s * 128, 128), :] = dot(d, r1[...], NT).astype(BF)
    load_wall = local(wall_o, r1, 3)
    sum_out.over()
    ra32 = Reduce32(
        me,
        lambda r, n: pool.at[pl.ds(pl.multiple_of(mine_row + r, 16), n), :],
        lambda r, n: pool.at[pl.ds(pl.multiple_of(their_row + r, 16), n), :],
        lambda r, n: pool.at[pl.ds(pl.multiple_of(RECV + r, 16), n), :],
        sra, rra, credit.at[3],
    )
    pl.semaphore_wait(credit.at[2], 1)
    for base, out in ((their_row, True), (mine_row, False)):
        for n in range(2):
            pair = lax.rem(ra32.pair + n, 2)
            rows = pl.ds(pl.multiple_of(base + pair * 384, 128), 384)
            pool[rows, :] = dot(das[:, rows], xs[...], TN).astype(BF)
            if out:
                for group in ra32.order[2 * n : 2 * n + 2]:
                    ra32.across(group)
    ra32.release()
    sum_out.to_right()
    sum_out.to_left()

    load_wall.wait()
    gain1 = jnp.zeros((1, DP), F32)
    for s in range(2):
        rows = pl.ds(s * 128, 128)
        dxn = dot(das[rows, :], r1[...])
        x = rows_of(xt, s)
        r1x = norm_rows(x)
        n1 = x * r1x
        gain1 = gain1 + jnp.sum(dxn * n1, axis=0, keepdims=True)
        e1 = dxn * g1[...]
        mean = jnp.sum(e1 * n1, axis=1, keepdims=True) * (1.0 / D)
        gi_o[s] = gi_o[s] + jnp.transpose(r1x * (e1 - n1 * mean))[0:D]
    store_gi = local(gi_o, gi_h, 5)
    sm[0, 0:1, :] = gain1
    sm[0, 1:2, :] = gain2
    sm[0, 2:8, :] = jnp.zeros((6, DP), F32)
    sm[0, 2:8, 0:128] = bias_rows[0:6]

    small_sent = []

    def small(n, devs):
        cps = []
        for k, dev in enumerate(devs):
            i = n * 3 + k
            cp = remote(sm.at[n], rm.at[i], sms.at[i], rms.at[i], dev, "small")
            cp.start()
            cps.append(cp)
        small_sent.extend(cps)
        return cps

    def gather_small(n, cps):
        total = sm[n]
        for k, cp in enumerate(cps):
            cp.wait_recv()
            total = total + rm[n * 3 + k]
        sm[n + 1] = total

    c = small(0, [me.x(d) for d in (1, 2, 3)])
    ra32.first()
    sum_out.relay()
    gather_small(0, c)
    c = small(1, [me.at(d, 0) for d in (1, 2, 3)])
    rf32.second()
    ra32.second()
    gather_small(1, c)
    c = small(2, [me.at(0, d) for d in (1, 2, 3)])
    gf_o[...] = rf32.last()

    sum_out.wait()
    for s in range(2):
        rows = pl.ds(s * 128, 128)
        total = sum_out.total(own[1, rows, :], s).astype(BF)
        lo_o[s] = lo_o[s] + jnp.transpose(dot(total, feat[...], NT))[0:D]
    store_lo = local(lo_o, lo_h, 4)

    mine = ra32.last().astype(BF)
    sx[...] = dot(stage[...], mine, TN).astype(BF)
    gather_small(2, c)
    c = small(3, [me.sibling()])
    last = []
    for k, d in enumerate((1, 3, 2)):
        rows = pl.ds(pl.multiple_of(lax.rem(t + d, 4) * 16, 16), 16)
        cp = remote(sx.at[rows], rx.at[k], sxs.at[k], rxs.at[k], me.x(d), "sx")
        cp.start()
        last.append(cp)
    gather_small(3, c)
    small_o[...] = sm[4]
    total = sx[pl.ds(pl.multiple_of(t * 16, 16), 16), :].astype(F32)
    for k, cp in enumerate(last):
        cp.wait_recv()
        total = total + rx[k].astype(F32)
    ga_o[...] = total
    for cp in last + small_sent:
        cp.wait_send()
    store_lo.wait()
    store_gi.wait()
    for g in (rf32, ra32, ez, collect, sum_out):
        g.drain()


VM = pl.BlockSpec(memory_space=pltpu.VMEM)
HB = pl.BlockSpec(memory_space=pl.ANY)
DMA = pltpu.SemaphoreType.DMA


def sds(shape, dtype=BF):
    return jax.ShapeDtypeStruct(shape, dtype)


def layer(*args):
    V = pltpu.VMEM
    return pl.pallas_call(
        layer_kernel,
        name="layer",
        out_shape=(
            sds((8, DP), F32), sds((16, DP), F32), sds((3, 48, FS), F32),
            sds((2, D, 128), F32), sds((2, D, 128), F32), sds((DP, DP)),
        ),
        in_specs=[VM] * 13 + [HB] * 5,
        out_specs=[VM] * 3 + [HB] * 3,
        scratch_shapes=[
            V((2, D, 128), BF), V((2, D, 128), BF), V((2, D, 128), F32), V((2, D, 128), F32),
            V((14 * ROWS, DP), BF), V((DP, DP), BF), V((DP, DP), BF), V((3, ROWS, DP), BF),
            V((3, DP, FS), BF), V((3, 4 * ROWS, FS), BF), V((8, 128, 384), BF),
            V((8, 128, 384), BF), V((8, 128, 384), BF), V((4, LEN, 64), BF), V((4, 64, LEN), F32),
            V((12, 128, LEN), BF), V((2, 128, 2048), F32), V((8, 128), F32), V((512, DP), BF),
            V((512, DP), BF), V((8, 128, 128), BF), V((4, 8, 128, 128), BF),
            V((8, 4, 128, 128), BF), V((512, DP), BF), V((512, DP), BF), V((64, DP), BF),
            V((3, 16, DP), BF), V((5, 8, DP), F32), V((10, 8, DP), F32), V((16, DP), BF),
            V((1, DP), F32), V((1, DP), F32), V((1, DP), F32), V((1, 2048), jnp.int32),
            DMA((6,)), DMA((3,)), DMA((3,)), DMA((31,)), DMA((32,)), DMA((31,)), DMA((32,)),
            DMA((4,)), DMA((4,)), DMA((4,)), DMA((4,)), DMA((14,)), DMA((14,)), DMA((28,)),
            DMA((28,)), DMA((6,)), DMA((6,)), DMA((6,)), DMA((6,)), DMA((28,)), DMA((28,)),
            DMA((14,)), DMA((14,)), DMA((13,)), DMA((13,)), DMA((13,)), DMA((13,)), DMA((3,)),
            DMA((3,)), DMA((10,)), DMA((10,)), pltpu.SemaphoreType.REGULAR((4,)),
        ],
        compiler_params=pltpu.CompilerParams(
            collective_id=0, has_side_effects=True, vmem_limit_bytes=64 * 2**20 - 2**17
        ),
    )(*args)


def finish_kernel(small_h, ga_h, gf_h, lo_h, gi_h, *rest):
    outs, (small, ga, gf, hold), hand, (sem_in, sem_out) = rest[:12], rest[12:16], rest[16:26], rest[26:]
    steps = [(n, s, r) for n in range(2) for s in range(2) for r in range(4)]

    def rows(refs, i):
        n, s, r = steps[i]
        return refs[n].at[s, pl.ds(r * 368, 368)]

    arriving = [pltpu.make_async_copy(rows((lo_h, gi_h), i), hold.at[i], sem_in.at[i]) for i in range(16)]
    parts = [
        pltpu.make_async_copy(src, dst, sem_in.at[16 + i])
        for i, (src, dst) in enumerate(((small_h, small), (ga_h, ga), (gf_h, gf)))
    ]
    leaving = [pltpu.make_async_copy(hold.at[i], rows(outs, i), sem_out.at[i]) for i in range(16)]
    packed = [
        pltpu.make_async_copy(hand[i], outs[2 + i], sem_out.at[16 + i]) for i in range(10)
    ]
    for cp in parts + arriving:
        cp.start()
    for cp in parts:
        cp.wait()
    s1, s2, sb, q, k, v, o, g, u, d = hand
    s1[...] = small[0:1, 0:D].reshape(D)
    s2[...] = small[1:2, 0:D].reshape(D)
    sb[...] = small[2:8, 0:32]
    for n, ref in enumerate((q, k, v, o)):
        ref[...] = ga[3 * n : 3 * n + 3, 0:D]
    for n, ref in enumerate((g, u, d)):
        ref[...] = gf[n, 0:46]
    for cp in packed:
        cp.start()
    for i in range(16):
        arriving[i].wait()
        leaving[i].start()
    for cp in packed + leaving:
        cp.wait()


def finish(*args):
    V = pltpu.VMEM
    shapes = ((D,),) * 2 + ((6, 32),) + ((3, D),) * 4 + ((46, FS),) * 3
    return pl.pallas_call(
        finish_kernel,
        name="finish",
        out_shape=(sds((2, D, 128), F32),) * 2 + tuple(sds(s, F32) for s in shapes),
        in_specs=[HB] * 5,
        out_specs=[HB] * 12,
        scratch_shapes=[
            V((8, DP), F32), V((16, DP), F32), V((3, 48, FS), F32), V((16, 368, 128), F32),
            *(V(s, F32) for s in shapes), DMA((19,)), DMA((26,)),
        ],
        compiler_params=pltpu.CompilerParams(vmem_limit_bytes=60 * 2**20),
    )(*args)


def per_device(
    inputs, cotangent, segment_ids, buckets, norm_gain_1, norm_gain_2, relative_bias,
    query_weight, key_weight, value_weight, output_weight, gate_weight, up_weight, down_weight,
):
    stage, feat, heads, outs = make_constants()
    stored = layer(
        query_weight.T, key_weight.T, value_weight.T, output_weight,
        gate_weight, up_weight, down_weight.T,
        segment_ids, buckets, relative_bias.T, norm_gain_1, norm_gain_2, stage,
        jnp.transpose(inputs, (0, 2, 1)), jnp.transpose(cotangent, (0, 2, 1)), feat, heads, outs,
    )
    lo, gi, gain1, gain2, bias, q, k, v, o, gate, up, down = finish(*stored[:5])
    return (
        jnp.transpose(lo, (0, 2, 1)), jnp.transpose(gi, (0, 2, 1)), gain1, gain2, bias.T,
        q.T, k.T, v.T, o, gate, up, down.T,
    )


def solution(mesh):
    every = ("fsdp", "ctx", "tp")
    rows = P("fsdp", ("ctx", "tp"), None)
    wide = P(("fsdp", "ctx"), "tp")
    attn = (P(None, every), P(None, every), P(None, every), P(every, None))
    ffn = (wide, wide, P("tp", ("fsdp", "ctx")))
    return jax.shard_map(
        per_device,
        mesh=mesh,
        in_specs=(rows, rows, P("fsdp", None), P(), P(), P(), P()) + attn + ffn,
        out_specs=(rows, rows, P(), P(), P()) + attn + ffn,
        check_vma=False,
    )
```

```python
import functools
import numpy as np
import jax
import jax.numpy as jnp
from jax import lax
from jax.experimental import pallas as pl
from jax.experimental.pallas import tpu as pltpu
from jax.sharding import PartitionSpec as P

D = 1472
DP = 1536
FS = 896
LEN = 1024
PIECE = 128
ROWS = 256
EPS = 1e-6
MESH = pl.DeviceIdType.MESH
BF = jnp.bfloat16
F32 = jnp.float32
NT = (((1,), (1,)), ((), ()))
NN = (((1,), (0,)), ((), ()))
TN = (((0,), (0,)), ((), ()))
GELU_C = 0.7978845608028654
WHOLE_HEAD = (0, 2, 3, 5)
SHARED_HEAD = (1, 1, 4, 4)


def dot(left, right, dims=NN):
    return lax.dot_general(left, right, dims, preferred_element_type=F32)


def block_slot(block):
    f, c = divmod(block, 2)
    y, zh, core = f // 4, (f // 2) % 2, f % 2
    z = zh * 2 + c
    return core * 16 + (y * 4 + z if core == 0 else z * 4 + y)


def make_constants():
    feat = np.zeros((DP, DP), np.float32)
    for r in range(D):
        feat[r, block_slot(r // 46) * 48 + r % 46] = 1
    stage = np.zeros((48, 64), np.float32)
    for w in range(4):
        for t in range(4):
            for i in range(3):
                stage[w * 12 + t * 3 + i, t * 16 + w * 3 + i] = 1

    def gathered(w, col):
        return block_slot(col // 12) * 48 + w * 12 + col % 12

    heads = np.zeros((DP, DP), np.float32)
    outs = np.zeros((DP, 512), np.float32)
    for j in range(4):
        hw, hs = WHOLE_HEAD[j], SHARED_HEAD[j]
        for part, (w, h) in enumerate(
            ((0, hw), (1, hw), (2, hw), (1, hs), (2, hs), (0, hs))
        ):
            for e in range(64):
                heads[gathered(w, h * 64 + e), j * 384 + part * 64 + e] = 1
        for part, h in enumerate((hw, hs)):
            for e in range(64):
                outs[gathered(3, h * 64 + e), j * 128 + part * 64 + e] = 1
    return tuple(a.astype(jnp.bfloat16) for a in (stage, feat, heads, outs.T))


class Place:
    def __init__(self):
        self.f = lax.axis_index("fsdp")
        self.c = lax.axis_index("ctx")
        self.t = lax.axis_index("tp")
        y = lax.div(self.f, 4)
        self.core = lax.rem(self.f, 2)
        z = lax.rem(lax.div(self.f, 2), 2) * 2 + self.c
        self.a1 = y + self.core * (z - y)
        self.a2 = z + self.core * (y - z)
        self.piece = self.c * 4 + self.t

    def at(self, da1, da2, dcore=0):
        core = lax.rem(self.core + dcore, 2)
        if dcore:
            y = self.a1 + self.core * (self.a2 - self.a1)
            z = self.a2 + self.core * (self.a1 - self.a2)
        else:
            b1 = lax.rem(self.a1 + da1, 4)
            b2 = lax.rem(self.a2 + da2, 4)
            y = b1 + core * (b2 - b1)
            z = b2 + core * (b1 - b2)
        return (y * 4 + lax.div(z, 2) * 2 + core, lax.rem(z, 2), self.t)

    def sibling(self):
        return self.at(0, 0, 1)

    def x(self, d):
        return (self.f, self.c, lax.rem(self.t + d + 4, 4))

    def group(self, dc, dt):
        return (self.f, lax.rem(self.c + dc, 2), lax.rem(self.t + dt, 4))

    def group_piece(self, dc, dt):
        return lax.rem(self.c + dc, 2) * 4 + lax.rem(self.t + dt, 4)

    def slot(self, da1=0, da2=0):
        return (
            self.core * 16 + lax.rem(self.a1 + da1, 4) * 4 + lax.rem(self.a2 + da2, 4)
        )

    def all_partners(self):
        out = [self.sibling()]
        for d in (1, 2, 3):
            out += [self.at(d, 0), self.at(0, d), self.x(d), self.group(1, d)]
        return out


GROUP = tuple((dc, dt) for dc in (0, 1) for dt in range(4) if (dc, dt) != (0, 0))


def greet(partners, meanwhile):
    bar = pltpu.get_barrier_semaphore()
    for p in partners:
        pl.semaphore_signal(bar, inc=1, device_id=p, device_id_type=MESH)
    meanwhile()
    pl.semaphore_wait(bar, len(partners))


def remote(src, dst, ss, rs, dev, tag=None):
    return pltpu.make_async_remote_copy(
        src_ref=src, dst_ref=dst, send_sem=ss, recv_sem=rs, device_id=dev,
        device_id_type=MESH,
    )


class Gather32:
    tag = None

    def __init__(self, me, view, ss, rs, relay=False):
        self.me, self.view, self.ss, self.rs = me, view, ss, rs
        self.relay, self.reach = relay, (1, 3) if relay else (1, 3, 2)
        self.sent = []

    def _send(self, slot, dev):
        k = len(self.sent)
        cp = remote(self.view(slot), self.view(slot), self.ss.at[k], self.rs.at[slot], dev, self.tag)
        cp.start()
        self.sent.append(cp)

    def _arrived(self, slot):
        v = self.view(slot)
        remote(v, v, self.ss.at[0], self.rs.at[slot], self.me.sibling(), self.tag).wait_recv()

    def first(self):
        me = self.me
        for d in (1, 3, 2):
            self._send(me.slot(), me.at(0, d))
        for d in self.reach:
            self._send(me.slot(), me.at(d, 0))
        self._send(me.slot(), me.sibling())

    def second(self):
        me = self.me
        for d in (1, 3, 2):
            s = me.slot(0, d)
            self._arrived(s)
            for e in self.reach:
                self._send(s, me.at(e, 0))
            self._send(s, me.sibling())

    def third(self):
        me = self.me
        for d in range(4):
            for e in (1, 3):
                s = me.slot(e, d)
                self._arrived(s)
                if self.relay and (d < 2) == (e == 3):
                    self._send(s, me.at(4 - e, 0))
                self._send(s, me.sibling())

    def fourth(self):
        me = self.me
        for d in range(4):
            s = me.slot(2, d)
            self._arrived(s)
            self._send(s, me.sibling())

    def last(self):
        me = self.me
        base = (1 - me.core) * 16
        for k in range(16):
            self._arrived(base + k)

    def drain(self):
        for cp in self.sent:
            cp.wait_send()


class RingGather:
    tag = None

    def __init__(self, me, buf, ss, rs):
        self.me, self.buf, self.ss, self.rs = me, buf, ss, rs
        self.sent = []

    def slot(self, d):
        return lax.rem(self.me.t + d + 4, 4)

    def _send(self, v, k, d):
        cp = remote(v, v, self.ss.at[k], self.rs.at[k], self.me.x(d), self.tag)
        cp.start()
        self.sent.append(cp)

    def _arrived(self, v, k):
        remote(v, v, self.ss.at[k], self.rs.at[k], self.me.x(1), self.tag).wait_recv()

    def first(self):
        own = self.buf(self.me.t, 0, ROWS)
        self._send(own, 0, 1)
        self._send(own, 1, -1)

    def arrived(self, k):
        self._arrived(self.buf(self.slot(2 * k - 1), 0, ROWS), k)

    def relay(self, k):
        self._send(self.buf(self.slot(2 * k - 1), k * 128, 128), 2 + k, 1 - 2 * k)

    def opposite(self):
        for k in (0, 1):
            self._arrived(self.buf(self.slot(2), k * 128, 128), 2 + k)

    def drain(self):
        for cp in self.sent:
            cp.wait_send()


class Exchange:
    tag = None
    LANES = ((0, 256), (256, 128))

    def __init__(self, me, src, dst, ss, rs):
        self.me, self.src, self.dst, self.ss, self.rs = me, src, dst, ss, rs
        self.sent = []

    def start(self, part):
        me = self.me
        lanes = pl.ds(*self.LANES[part])
        for k, (dc, dt) in enumerate(GROUP):
            cp = remote(
                self.src.at[me.group_piece(dc, dt), :, lanes], self.dst.at[me.piece, :, lanes],
                self.ss.at[part * 7 + k], self.rs.at[part * 7 + k], me.group(dc, dt), self.tag,
            )
            cp.start()
            self.sent.append(cp)
        self.dst[me.piece, :, lanes] = self.src[me.piece, :, lanes]

    def wait(self, part):
        me = self.me
        lanes = pl.ds(*self.LANES[part])
        for k, (dc, dt) in enumerate(GROUP):
            v = self.dst.at[me.group_piece((2 - dc) % 2, (4 - dt) % 4), :, lanes]
            remote(
                v, v, self.ss.at[part * 7 + k], self.rs.at[part * 7 + k], me.sibling(), self.tag
            ).wait_recv()

    def drain(self):
        for cp in self.sent:
            cp.wait_send()


def norm_rows(rows):
    return lax.rsqrt(jnp.sum(rows * rows, axis=1, keepdims=True) * (1.0 / D) + EPS)


def rows_of(ref, s):
    v = ref[s].astype(F32)
    v = jnp.concatenate([v, jnp.zeros((DP - D, PIECE), F32)], axis=0)
    return jnp.transpose(v)


class Spread:
    ROUNDS = (0, 3, 1, 2)

    def __init__(self, me, src, dst, ss, rs):
        self.me, self.src, self.dst, self.ss, self.rs = me, src, dst, ss, rs
        self.sent = []

    def start(self):
        me = self.me
        for n, d in enumerate(self.ROUNDS):
            for k, (dc, dt) in enumerate(GROUP):
                place = lax.rem(me.t + dt + d, 4)
                cp = remote(
                    self.src.at[lax.rem(me.c + dc, 2) * 4 + place],
                    self.dst.at[place, me.piece],
                    self.ss.at[n * 7 + k], self.rs.at[n * 7 + k], me.group(dc, dt), "spread",
                )
                cp.start()
                self.sent.append(cp)
            place = lax.rem(me.t + d, 4)
            self.dst[place, me.piece] = self.src[me.c * 4 + place]

    def wait(self, n):
        me = self.me
        place = lax.rem(me.t + self.ROUNDS[n], 4)
        for k, (dc, dt) in enumerate(GROUP):
            v = self.dst.at[place, me.group_piece((2 - dc) % 2, (4 - dt) % 4)]
            remote(
                v, v, self.ss.at[n * 7 + k], self.rs.at[n * 7 + k], me.sibling(), "spread"
            ).wait_recv()

    def drain(self):
        for cp in self.sent:
            cp.wait_send()


class Collect:
    def __init__(self, me, src, dst, ss, rs):
        self.me, self.src, self.dst, self.ss, self.rs = me, src, dst, ss, rs
        self.sent = []

    def start(self, n):
        me = self.me
        place = lax.rem(me.t + Spread.ROUNDS[n], 4)
        piece = me.c * 4 + place
        for k, (dc, dt) in enumerate(GROUP):
            cp = remote(
                self.src(n, place, me.group_piece(dc, dt)), self.dst.at[piece, me.t],
                self.ss.at[n * 7 + k], self.rs.at[n * 7 + k], me.group(dc, dt), "collect",
            )
            cp.start()
            self.sent.append(cp)
        self.dst[piece, me.t] = self.src(n, place, me.piece)[...]

    def wait(self):
        me = self.me
        for n in range(4):
            for k, (dc, dt) in enumerate(GROUP):
                c = lax.rem(me.c + dc, 2)
                maker = lax.rem(me.t + 4 - dt, 4)
                v = self.dst.at[c * 4 + lax.rem(maker + Spread.ROUNDS[n], 4), maker]
                remote(
                    v, v, self.ss.at[n * 7 + k], self.rs.at[n * 7 + k], me.sibling(), "collect"
                ).wait_recv()

    def drain(self):
        for cp in self.sent:
            cp.wait_send()


class RingReduce:
    def __init__(self, me, left, right, opposite, landing, ss, rs, tag):
        self.me, self.left, self.right, self.opposite = me, left, right, opposite
        self.landing, self.ss, self.rs, self.tag = landing, ss, rs, tag
        self.sent = []

    def _send(self, src, row, k, d):
        cp = remote(
            src, self.landing(row, 128), self.ss.at[k], self.rs.at[k], self.me.x(d), self.tag
        )
        cp.start()
        self.sent.append(cp)

    def _arrived(self, row, k):
        v = self.landing(row, 128)
        remote(v, v, self.ss.at[k], self.rs.at[k], self.me.x(1), self.tag).wait_recv()

    def over(self):
        self._send(self.opposite(0, 128), 512, 0, 1)
        self._send(self.opposite(128, 128), 640, 1, -1)

    def to_right(self):
        self._send(self.right(128, 128), 128, 2, 1)

    def to_left(self):
        self._send(self.left(0, 128), 256, 3, -1)

    def relay(self):
        for k, view, r, row, d in ((0, self.right, 0, 0, 1), (1, self.left, 128, 384, -1)):
            self._arrived(512 + 128 * k, k)
            v = view(r, 128)
            passed = self.landing(512 + 128 * k, 128)[...]
            v[...] = (v[...].astype(F32) + passed.astype(F32)).astype(BF)
            self._send(v, row, 4 + k, d)

    def wait(self):
        for row, k in ((128, 2), (256, 3), (0, 4), (384, 5)):
            self._arrived(row, k)

    def total(self, own, s):
        return (
            own.astype(F32)
            + self.landing(s * 128, 128)[...].astype(F32)
            + self.landing(256 + s * 128, 128)[...].astype(F32)
        )

    def drain(self):
        for cp in self.sent:
            cp.wait_send()


class Reduce32:
    tag = None

    def __init__(self, me, mine, theirs, landing, ss, rs, free, relay=False):
        self.relay = relay
        self.me, self.mine, self.theirs, self.landing = me, mine, theirs, landing
        self.ss, self.rs, self.free = ss, rs, free
        self.sent, self.crossing, self.arrays = [], [], []
        self.pair = 1 - lax.div(me.a1, 2)
        mate = me.a1 + 1 - 2 * lax.rem(me.a1, 2)
        self.order = (self.pair * 2, self.pair * 2 + 1, mate, me.a1)

    def _send(self, src, dst, k, dev):
        cp = remote(src, dst, self.ss.at[k], self.rs.at[k], dev, self.tag)
        cp.start()
        self.sent.append(cp)
        return cp

    def across(self, group):
        cp = self._send(
            self.theirs(group * 192, 192), self.landing(group * 192, 192), group,
            self.me.sibling(),
        )
        self.crossing.append(cp)

    def across_array(self, n, src, dst):
        self.arrays.append(self._send(src, dst, n, self.me.sibling()))
        self.crossing.append(self.arrays[-1])

    def release(self):
        for cp in self.crossing:
            cp.wait_send()
            self.sent.remove(cp)
        for d in (1, 2, 3):
            for dev in (self.me.at(d, 0), self.me.at(0, d)):
                pl.semaphore_signal(self.free, inc=1, device_id=dev, device_id_type=MESH)

    def first(self):
        me = self.me
        pl.semaphore_wait(self.free, 6)
        self.one = []
        for cp in self.arrays:
            cp.wait_recv()
        for group in self.order:
            m, there = self.mine(group * 192, 192), self.landing(group * 192, 192)
            if not self.arrays:
                remote(
                    m, there, self.ss.at[group], self.rs.at[group], me.sibling(), self.tag
                ).wait_recv()
            m[...] = (m[...].astype(F32) + there[...].astype(F32)).astype(BF)
            if not self.relay and len(self.one) < 3:
                d = lax.rem(group - me.a1 + 4, 4)
                dst = self.theirs((d - 1) * 192, 192)
                self.one.append(self._send(m, dst, 3 + d, me.at(d, 0)))
        if self.relay:
            up, down = (lax.rem(me.a1 + d, 4) * 192 for d in (1, 3))
            over = lax.rem(me.a1 + 2, 4) * 192
            for src, row, k, d in (
                (over, 384, 4, 1), (over + 96, 480, 5, 3), (up + 96, 96, 6, 1), (down, 192, 7, 3),
            ):
                self._send(self.mine(src, 96), self.theirs(row, 96), k, me.at(d, 0))

    def _half_arrived(self, row, k):
        v = self.theirs(row, 96)
        remote(v, v, self.ss.at[k], self.rs.at[k], self.me.sibling(), self.tag).wait_recv()

    def pass_on(self):
        me = self.me
        for n, d, half, row in ((0, 1, 0, 0), (1, 3, 96, 288)):
            self._half_arrived(384 + 96 * n, 4 + n)
            m = self.mine(lax.rem(me.a1 + d, 4) * 192 + half, 96)
            passed = self.theirs(384 + 96 * n, 96)[...]
            m[...] = (m[...].astype(F32) + passed.astype(F32)).astype(BF)
            self._send(m, self.theirs(row, 96), 8 + n, me.at(d, 0))

    def second(self):
        me = self.me
        m = self.mine(me.a1 * 192, 192)
        if self.relay:
            for row, k in ((96, 6), (192, 7), (0, 8), (288, 9)):
                self._half_arrived(row, k)
        else:
            for k in range(3):
                v = self.theirs(k * 192, 192)
                remote(
                    v, v, self.ss.at[4 + k], self.rs.at[4 + k], me.sibling(), self.tag
                ).wait_recv()
        total = m[...].astype(F32)
        for k in range(2 if self.relay else 3):
            total = total + self.theirs(k * 192, 192)[...].astype(F32)
        m[...] = total.astype(BF)
        self.two = []
        for k, d in enumerate((1, 3, 2)):
            src = self.mine(me.a1 * 192 + lax.rem(me.a2 + d, 4) * 48, 48)
            self.two.append(self._send(src, self.theirs(576 + k * 48, 48), 10 + k, me.at(0, d)))

    def last(self):
        me = self.me
        for cp in self.two:
            cp.wait_recv()
        total = self.mine(me.a1 * 192 + me.a2 * 48, 48)[...].astype(F32)
        for k in range(3):
            total = total + self.theirs(576 + k * 48, 48)[...].astype(F32)
        return total

    def drain(self):
        for cp in self.sent:
            cp.wait_send()


def layer_kernel(
    wq, wk, wv, wo_in, wg, wu, wd, seg, bk_in, rb, g1_in, g2_in, stage,
    xt_h, ct_h, feat_h, heads_h, outs_h,
    small_o, ga_o, gf_o, lo_h, gi_h, wall_o,
    xt, ct, lo_o, gi_o,
    pool, feat, r1, own, wf, hgu, zbuf, qkv, dr, kv, acc, prob, skew, cqs, wo, wop,
    obuf, spread_in, collect_in, xs, das, sx, rx, sm, rm, aw,
    g1, g2, g2p, bk,
    lsem, ssx, rsx, sg, rg, sf, rf, sc, rc, sxr, rxr, sq, rq, so, ro, sd, rd, st, rt,
    sdo, rdo, sdq, rdq, srf, rrf, sra, rra, sxs, rxs, sms, rms, credit,
):
    me = Place()
    core, t = me.core, me.t
    WALL, RECV, OUT = 2048, 2048, 2816

    def local(src, dst, i):
        cp = pltpu.make_async_copy(src, dst, lsem.at[i])
        cp.start()
        return cp

    load_xt = local(xt_h, xt, 4)
    load_feat = local(feat_h, feat, 0)
    load_ct = local(ct_h, ct, 5)

    def pack():
        aw[...] = jnp.zeros_like(aw)
        shard = [w[...].astype(F32) for w in (wq, wk, wv, wo_in)] + [jnp.zeros((4, D), F32)]
        aw[:, 0:D] = jnp.concatenate(shard, axis=0).astype(BF)
        for g, g_in in ((g1, g1_in), (g2, g2_in)):
            g[...] = jnp.zeros_like(g)
            g[:, 0:D] = g_in[...].astype(F32).reshape(1, D)
        bk[...] = jnp.zeros_like(bk)
        bk[:, 1:2048] = bk_in[...].reshape(1, 2047)

    greet(me.all_partners(), pack)
    load_heads = local(heads_h, r1, 1)
    load_outs = local(outs_h, das, 2)

    xsend = []
    for k, d in enumerate((1, 3, 2)):
        cp = remote(
            aw, sx.at[pl.ds(pl.multiple_of(t * 16, 16), 16)], ssx.at[k], rsx.at[k], me.x(d), "xst"
        )
        cp.start()
        xsend.append(cp)
    sx[pl.ds(pl.multiple_of(t * 16, 16), 16), :] = aw[...]

    load_xt.wait()
    for s in range(2):
        rows = rows_of(xt, s)
        xs[pl.ds(s * 128, 128), :] = (rows * norm_rows(rows) * g1[...]).astype(BF)
    for cp in xsend:
        cp.wait()

    def wall_block(slot):
        return pool.at[pl.ds(pl.multiple_of(WALL + slot * 48, 16), 48), :]

    wall_block(me.slot())[...] = dot(stage[...], sx[...]).astype(BF)
    gw = Gather32(me, wall_block, sg, rg)
    gw.first()

    def part_rows(base):
        return lambda i, r, n: pool.at[pl.ds(pl.multiple_of(base + i * ROWS + r, 128), n)]

    gx = RingGather(me, part_rows(1024), sxr, rxr)
    gc = RingGather(me, part_rows(0), sc, rc)
    load_feat.wait()
    load_ct.wait()
    for ref, part in ((xt, part_rows(1024)), (ct, part_rows(0))):
        for s in range(2):
            part(t, s * 128, 128)[...] = dot(rows_of(ref, s).astype(BF), feat[...]).astype(BF)
        if ref is xt:
            gx.first()
    gw.second()

    def chunk_rows(base, slot):
        return pl.ds(pl.multiple_of(base + slot * ROWS, ROWS), ROWS)

    def wf_rows(row, n):
        return wf.at[:, pl.ds(pl.multiple_of(row, 16), n), :]

    def wf_block(slot):
        return wf_rows(slot * 48, 48)

    for n, w in enumerate((wg, wu, wd)):
        wf[n, pl.ds(pl.multiple_of(me.slot() * 48, 16), 48), :] = jnp.concatenate(
            [w[...].astype(F32), jnp.zeros((2, FS), F32)], axis=0
        ).astype(BF)
    gf = Gather32(me, wf_block, sf, rf, True)
    gf.first()

    whole = t + lax.div(t + 1, 2)
    shared = 1 + 3 * lax.div(t, 2)
    half = lax.rem(t, 2)
    onehot = lax.broadcasted_iota(jnp.int32, (32, 2048), 0) == bk[...]
    lane = lax.broadcasted_iota(jnp.int32, (32, 128), 1)
    by_bucket = jnp.concatenate(
        [jnp.transpose(jnp.pad(rb[...].astype(F32), ((0, 122), (0, 96))))], axis=0
    )[0:32]
    for n, head in ((0, whole), (1, shared)):
        column = jnp.sum(jnp.where(lane == head, by_bucket, 0.0), axis=1, keepdims=True)
        line = jnp.sum(jnp.where(onehot, column, 0.0), axis=0, keepdims=True)
        skew[n] = pltpu.roll(
            jnp.broadcast_to(line, (128, 2048)), 0, 1, stride=1, stride_axis=0
        )
    ids = seg[pl.ds(me.c, 1), :].astype(F32)
    place = lax.broadcasted_iota(jnp.int32, (1, LEN), 1).astype(F32)
    ids = jnp.where(ids == 0.0, -1.0 - place, ids)
    for p in range(8):
        cqs[p : p + 1, :] = ids[:, p * 128 : (p + 1) * 128]

    gw.third()
    for k in (0, 1):
        gx.arrived(k)
        gx.relay(k)
    gw.fourth()
    gw.last()

    gf.second()

    load_heads.wait()
    y = jnp.concatenate(
        [
            dot(xs[0:256, :], pool[pl.ds(WALL + n * 512, 512), :], NT).astype(BF)
            for n in range(3)
        ],
        axis=1,
    )
    for j in range(4):
        z = dot(y, r1[:, pl.ds(j * 384, 384)]).astype(BF)
        for s in range(2):
            zbuf[s * 4 + j] = z[s * 128 : (s + 1) * 128]
    eq = Exchange(me, zbuf, qkv, sq, rq)
    eq.start(0)
    eq.start(1)
    store_wall = local(pool.at[pl.ds(WALL, DP)], wall_o, 3)
    load_outs.wait()
    wo[...] = dot(das[...], pool[pl.ds(WALL, DP), :]).astype(BF)
    wop[...] = dot(wo[...], feat[...]).astype(BF)
    gain = jnp.broadcast_to(g2[...], (16, DP)).astype(BF)
    g2p[...] = dot(gain, feat[...])[0:1]
    def unpack(parts):
        for p in range(8):
            for n in parts:
                kv[n, pl.ds(p * 128, 128), :] = qkv[p, :, 64 + n * 64 : 128 + n * 64]

    eq.wait(0)
    gc.first()
    unpack((0, 1, 2))

    def attend(n, block, p, q):
        start = pl.multiple_of(LEN - p * 128, 128)
        scores = dot(q, kv[2 * n], NT) + skew[n, :, pl.ds(start, LEN)]
        same = jnp.transpose(jnp.broadcast_to(cqs[pl.ds(p, 1), :], (128, 128)))[:, 0:1] == ids
        scores = jnp.where(same, scores, -1e30)
        e = jnp.exp(scores - jnp.max(scores, axis=1, keepdims=True))
        probs = (e * (1.0 / jnp.sum(e, axis=1, keepdims=True))).astype(BF)
        prob[block] = probs
        return dot(probs, kv[2 * n + 1]).astype(BF)

    def whole_step(p, _):
        o = attend(0, p, p, qkv[p, :, 0:64])
        obuf[p, :, 0:64] = o
        obuf[p, :, 64:128] = jnp.zeros((128, 64), BF)
        return 0

    lax.fori_loop(0, 8, whole_step, 0)
    eq.wait(1)
    unpack((3,))
    gf.third()

    def shared_step(i, _):
        p = half * 4 + i
        obuf[p, :, 64:128] = attend(1, 8 + i, p, qkv[p, :, 320:384])
        return 0

    lax.fori_loop(0, 4, shared_step, 0)
    gw.drain()
    store_wall.wait()
    spread = Spread(me, obuf, spread_in, so, ro)
    spread.start()
    gf.fourth()
    gx.opposite()
    gx.drain()
    gf.last()
    gf.drain()

    def collect_out(n, place, target):
        return spread_in.at[place, target] if n else obuf.at[target]

    collect = Collect(me, collect_out, collect_in, sdo, rdo)

    def attended(slot, s):
        return jnp.concatenate([spread_in[slot, s * 4 + j] for j in range(4)], axis=1)

    gain_back = jnp.where(g2p[...] > 0.0, 1.0 / jnp.maximum(g2p[...], 0.25), 0.0)

    def chunk(n, dpart, opart):
        slot = lax.rem(t + Spread.ROUNDS[n], 4)
        spread.wait(n)
        rows = chunk_rows(0, slot)
        xrows = chunk_rows(1024, slot)
        h1 = pool[xrows, :].astype(F32) + dot(
            jnp.concatenate([attended(slot, s) for s in range(2)], axis=0), wop[...]
        )
        r2 = norm_rows(h1)
        pool[xrows, :] = (h1 * r2 * g2p[...]).astype(BF)
        x = pool[xrows, :]
        dy = pool[rows, :]
        for n0, nw in ((0, 256), (256, 256), (512, 256), (768, 128)):
            cols = slice(n0, n0 + nw)
            g = dot(x, wf[0, :, cols])
            u = dot(x, wf[1, :, cols])
            dh = dot(dy, wf[2, :, cols])
            sq_g = g * g
            th = jnp.tanh(GELU_C * g * (1.0 + 0.044715 * sq_g))
            up = 0.5 * (1.0 + th)
            gelu = g * up
            slope = up + 0.5 * g * (1.0 - th * th) * (GELU_C * (1.0 + 0.134145 * sq_g))
            hgu[2, rows, cols] = (gelu * u).astype(BF)
            hgu[0, rows, cols] = (dh * u * slope).astype(BF)
            hgu[1, rows, cols] = (dh * gelu).astype(BF)
        dx = dot(hgu[0, rows, :], wf[0], NT) + dot(hgu[1, rows, :], wf[1], NT)
        dpart[...] = dx.astype(BF)
        x = pool[xrows, :].astype(F32)
        mean = jnp.sum(dx * x, axis=1, keepdims=True) * (1.0 / D)
        d = r2 * (dx * g2p[...] - x * (gain_back * mean))
        if n == 0:
            d = d + pool[rows, :].astype(F32)
        do = dot(d.astype(BF), wop[...], NT).astype(BF)
        if n == 0:
            spread.drain()
        for s in range(2):
            for j in range(4):
                block = do[s * 128 : (s + 1) * 128, j * 128 : (j + 1) * 128]
                collect_out(n, slot, s * 4 + j)[...] = block
        collect.start(n)
        opart[...] = dot(hgu[2, rows, :], wf[2], NT).astype(BF)

    def rows_at(ref, base):
        return lambda r, n: ref.at[pl.ds(base + r, n)]

    sum_dx = RingReduce(
        me, rows_at(r1, 0), rows_at(r1, 256), rows_at(r1, 512), rows_at(pool, RECV),
        sd, rd, "dx",
    )
    chunk(0, own.at[0], own.at[1])
    for k in (0, 1):
        gc.arrived(k)
        gc.relay(k)
    chunk(1, r1.at[pl.ds(0, ROWS)], r1.at[pl.ds(768, ROWS)])
    sum_dx.to_left()
    chunk(2, r1.at[pl.ds(256, ROWS)], r1.at[pl.ds(1024, ROWS)])
    sum_dx.to_right()
    gc.opposite()
    chunk(3, r1.at[pl.ds(512, ROWS)], own.at[2])
    sum_dx.over()
    gc.drain()

    mine_row, their_row = core * 768, (1 - core) * 768
    rf32 = Reduce32(
        me, lambda r, n: wf_rows(mine_row + r, n), lambda r, n: wf_rows(their_row + r, n),
        lambda r, n: hgu.at[:, pl.ds(pl.multiple_of(r, 16), n), :], srf, rrf, credit.at[1],
        True,
    )
    for n, ws in ((0, (2,)), (1, (0, 1))):
        for m in range(6):
            cols = slice(m * 256, m * 256 + 256)
            term = jnp.concatenate([hgu[i] for i in ws], axis=1)
            grad = dot(pool[n * 1024 : n * 1024 + 1024, cols], term, TN).astype(BF)
            for k, i in enumerate(ws):
                wf[i, cols, :] = grad[:, k * FS : k * FS + FS]
        pl.semaphore_signal(credit.at[0], inc=1, device_id=me.sibling(), device_id_type=MESH)
        pl.semaphore_wait(credit.at[0], 1)
        for i in ws:
            rf32.across_array(
                i, wf.at[i, pl.ds(pl.multiple_of(their_row, 16), 768)], hgu.at[i, pl.ds(0, 768)]
            )

    acc[...] = jnp.zeros_like(acc)
    skew[...] = jnp.zeros_like(skew)
    eq.drain()
    pool[1536:2048, :] = r1[768:1280, :]
    sum_out = RingReduce(
        me, rows_at(pool, 1536), rows_at(pool, 1792), lambda r, n: own.at[2, pl.ds(r, n)],
        rows_at(pool, OUT), st, rt, "out",
    )
    collect.wait()
    for p in range(8):
        do = collect_in[p, 0].astype(F32)
        for k in (1, 2, 3):
            do = do + collect_in[p, k].astype(F32)
        collect_in[p, 0] = do.astype(BF)

    def attend_back(n, block, p, q, do):
        start = pl.multiple_of(LEN - p * 128, 128)
        pb = prob[block]
        probs = pb.astype(F32)
        dp = dot(do, kv[2 * n + 1], NT)
        delta = jnp.sum(dp * probs, axis=1, keepdims=True)
        ds = (probs * (dp - delta)).astype(BF)
        cols = pl.ds(start, LEN)
        skew[n, :, cols] = skew[n, :, cols] + ds.astype(F32)
        acc[2 * n] = acc[2 * n] + dot(q, ds, TN)
        acc[2 * n + 1] = acc[2 * n + 1] + dot(do, pb, TN)
        return dot(ds, kv[2 * n]).astype(BF)

    def whole_back(p, _):
        zbuf[p, :, 0:64] = attend_back(0, p, p, qkv[p, :, 0:64], collect_in[p, 0, :, 0:64])
        return 0

    def shared_back(i, _):
        p = half * 4 + i
        zbuf[p, :, 320:384] = attend_back(1, 8 + i, p, qkv[p, :, 320:384], collect_in[p, 0, :, 64:128])
        return 0

    def key_grads(n):
        grad = jnp.transpose(acc[n]).astype(BF)
        for p in range(8):
            zbuf[p, :, 64 + n * 64 : 128 + n * 64] = grad[p * 128 : (p + 1) * 128]

    zbuf[:, :, 320:384] = jnp.zeros((8, 128, 64), BF)
    lax.fori_loop(0, 4, shared_back, 0)
    sum_dx.relay()
    key_grads(2)
    key_grads(3)
    ez = Exchange(me, zbuf, dr, sdq, rdq)
    ez.start(1)
    lax.fori_loop(0, 8, whole_back, 0)
    key_grads(0)
    key_grads(1)
    ez.start(0)
    rf32.release()
    rf32.first()

    sum_dx.wait()
    sum_dx.drain()
    load_heads = local(heads_h, r1, 1)
    att = jnp.concatenate([attended(t, s) for s in range(2)], axis=0)
    das[pl.ds(256, 256), :] = dot(att, das[...]).astype(BF)
    gain2 = jnp.zeros((1, DP), F32)
    for s in range(2):
        rows = pl.ds(s * 128, 128)
        dxn2 = dot(sum_dx.total(own[0, rows, :], s).astype(BF), feat[...], NT)
        h1 = rows_of(xt, s) + dot(attended(t, s), wo[...])
        lo_o[s] = jnp.transpose(h1)[0:D]
        r2 = norm_rows(h1)
        n2 = h1 * r2
        gain2 = gain2 + jnp.sum(dxn2 * n2, axis=0, keepdims=True)
        e2 = dxn2 * g2[...]
        mean = jnp.sum(e2 * n2, axis=1, keepdims=True) * (1.0 / D)
        d = rows_of(ct, s) + r2 * (e2 - n2 * mean)
        gi_o[s] = jnp.transpose(d)[0:D]
        xs[pl.ds(256 + s * 128, 128), :] = d.astype(BF)
    pl.semaphore_signal(credit.at[2], inc=1, device_id=me.sibling(), device_id_type=MESH)

    row = lax.broadcasted_iota(jnp.int32, (128, 2048), 0)
    bias = jnp.zeros((32, 128), F32)
    for n, head in ((0, whole), (1, shared)):
        tilted = skew[n]
        for b in range(7):
            moved = pltpu.roll(tilted, 2048 - (1 << b), 1)
            tilted = jnp.where(lax.rem(lax.div(row, 1 << b), 2) == 1, moved, tilted)
        line = jnp.sum(tilted, axis=0, keepdims=True)
        column = jnp.sum(jnp.where(onehot, line, 0.0), axis=1, keepdims=True)
        bias = bias + jnp.where(lane == head, column, 0.0)
    bias_rows = jnp.transpose(jnp.concatenate([bias, jnp.zeros((96, 128), F32)], axis=0))

    load_heads.wait()
    rf32.pass_on()
    ez.wait(0)
    ez.wait(1)
    for s in range(2):
        d = jnp.concatenate([dr[s * 4 + j] for j in range(4)], axis=1)
        das[pl.ds(s * 128, 128), :] = dot(d, r1[...], NT).astype(BF)
    load_wall = local(wall_o, r1, 3)
    sum_out.over()
    ra32 = Reduce32(
        me,
        lambda r, n: pool.at[pl.ds(pl.multiple_of(mine_row + r, 16), n), :],
        lambda r, n: pool.at[pl.ds(pl.multiple_of(their_row + r, 16), n), :],
        lambda r, n: pool.at[pl.ds(pl.multiple_of(RECV + r, 16), n), :],
        sra, rra, credit.at[3],
    )
    pl.semaphore_wait(credit.at[2], 1)
    for base, out in ((their_row, True), (mine_row, False)):
        for n in range(2):
            pair = lax.rem(ra32.pair + n, 2)
            rows = pl.ds(pl.multiple_of(base + pair * 384, 128), 384)
            pool[rows, :] = dot(das[:, rows], xs[...], TN).astype(BF)
            if out:
                for group in ra32.order[2 * n : 2 * n + 2]:
                    ra32.across(group)
    ra32.release()
    sum_out.to_right()
    sum_out.to_left()

    load_wall.wait()
    gain1 = jnp.zeros((1, DP), F32)
    for s in range(2):
        rows = pl.ds(s * 128, 128)
        dxn = dot(das[rows, :], r1[...])
        x = rows_of(xt, s)
        r1x = norm_rows(x)
        n1 = x * r1x
        gain1 = gain1 + jnp.sum(dxn * n1, axis=0, keepdims=True)
        e1 = dxn * g1[...]
        mean = jnp.sum(e1 * n1, axis=1, keepdims=True) * (1.0 / D)
        gi_o[s] = gi_o[s] + jnp.transpose(r1x * (e1 - n1 * mean))[0:D]
    store_gi = local(gi_o, gi_h, 5)
    sm[0, 0:1, :] = gain1
    sm[0, 1:2, :] = gain2
    sm[0, 2:8, :] = jnp.zeros((6, DP), F32)
    sm[0, 2:8, 0:128] = bias_rows[0:6]

    small_sent = []

    def small(n, devs):
        cps = []
        for k, dev in enumerate(devs):
            i = n * 3 + k
            cp = remote(sm.at[n], rm.at[i], sms.at[i], rms.at[i], dev, "small")
            cp.start()
            cps.append(cp)
        small_sent.extend(cps)
        return cps

    def gather_small(n, cps):
        total = sm[n]
        for k, cp in enumerate(cps):
            cp.wait_recv()
            total = total + rm[n * 3 + k]
        sm[n + 1] = total

    c = small(0, [me.x(d) for d in (1, 2, 3)])
    ra32.first()
    sum_out.relay()
    gather_small(0, c)
    c = small(1, [me.at(d, 0) for d in (1, 2, 3)])
    rf32.second()
    ra32.second()
    gather_small(1, c)
    c = small(2, [me.at(0, d) for d in (1, 2, 3)])
    gf_o[...] = rf32.last()

    sum_out.wait()
    for s in range(2):
        rows = pl.ds(s * 128, 128)
        total = sum_out.total(own[1, rows, :], s).astype(BF)
        lo_o[s] = lo_o[s] + jnp.transpose(dot(total, feat[...], NT))[0:D]
    store_lo = local(lo_o, lo_h, 4)

    mine = ra32.last().astype(BF)
    sx[...] = dot(stage[...], mine, TN).astype(BF)
    gather_small(2, c)
    c = small(3, [me.sibling()])
    last = []
    for k, d in enumerate((1, 3, 2)):
        rows = pl.ds(pl.multiple_of(lax.rem(t + d, 4) * 16, 16), 16)
        cp = remote(sx.at[rows], rx.at[k], sxs.at[k], rxs.at[k], me.x(d), "sx")
        cp.start()
        last.append(cp)
    gather_small(3, c)
    small_o[...] = sm[4]
    total = sx[pl.ds(pl.multiple_of(t * 16, 16), 16), :].astype(F32)
    for k, cp in enumerate(last):
        cp.wait_recv()
        total = total + rx[k].astype(F32)
    ga_o[...] = total
    for cp in last + small_sent:
        cp.wait_send()
    store_lo.wait()
    store_gi.wait()
    for g in (rf32, ra32, ez, collect, sum_out):
        g.drain()


VM = pl.BlockSpec(memory_space=pltpu.VMEM)
HB = pl.BlockSpec(memory_space=pl.ANY)
DMA = pltpu.SemaphoreType.DMA


def sds(shape, dtype=BF):
    return jax.ShapeDtypeStruct(shape, dtype)


def layer(*args):
    V = pltpu.VMEM
    return pl.pallas_call(
        layer_kernel,
        name="layer",
        out_shape=(
            sds((8, DP), F32), sds((16, DP), F32), sds((3, 48, FS), F32),
            sds((2, D, 128), F32), sds((2, D, 128), F32), sds((DP, DP)),
        ),
        in_specs=[VM] * 13 + [HB] * 5,
        out_specs=[VM] * 3 + [HB] * 3,
        scratch_shapes=[
            V((2, D, 128), BF), V((2, D, 128), BF), V((2, D, 128), F32), V((2, D, 128), F32),
            V((14 * ROWS, DP), BF), V((DP, DP), BF), V((DP, DP), BF), V((3, ROWS, DP), BF),
            V((3, DP, FS), BF), V((3, 4 * ROWS, FS), BF), V((8, 128, 384), BF),
            V((8, 128, 384), BF), V((8, 128, 384), BF), V((4, LEN, 64), BF), V((4, 64, LEN), F32),
            V((12, 128, LEN), BF), V((2, 128, 2048), F32), V((8, 128), F32), V((512, DP), BF),
            V((512, DP), BF), V((8, 128, 128), BF), V((4, 8, 128, 128), BF),
            V((8, 4, 128, 128), BF), V((512, DP), BF), V((512, DP), BF), V((64, DP), BF),
            V((3, 16, DP), BF), V((5, 8, DP), F32), V((10, 8, DP), F32), V((16, DP), BF),
            V((1, DP), F32), V((1, DP), F32), V((1, DP), F32), V((1, 2048), jnp.int32),
            DMA((6,)), DMA((3,)), DMA((3,)), DMA((31,)), DMA((32,)), DMA((31,)), DMA((32,)),
            DMA((4,)), DMA((4,)), DMA((4,)), DMA((4,)), DMA((14,)), DMA((14,)), DMA((28,)),
            DMA((28,)), DMA((6,)), DMA((6,)), DMA((6,)), DMA((6,)), DMA((28,)), DMA((28,)),
            DMA((14,)), DMA((14,)), DMA((13,)), DMA((13,)), DMA((13,)), DMA((13,)), DMA((3,)),
            DMA((3,)), DMA((10,)), DMA((10,)), pltpu.SemaphoreType.REGULAR((4,)),
        ],
        compiler_params=pltpu.CompilerParams(
            collective_id=0, has_side_effects=True, vmem_limit_bytes=64 * 2**20 - 2**17
        ),
    )(*args)


def finish_kernel(small_h, ga_h, gf_h, lo_h, gi_h, *rest):
    outs, (small, ga, gf, hold), hand, (sem_in, sem_out) = rest[:12], rest[12:16], rest[16:26], rest[26:]
    steps = [(n, s, r) for n in range(2) for s in range(2) for r in range(4)]

    def rows(refs, i):
        n, s, r = steps[i]
        return refs[n].at[s, pl.ds(r * 368, 368)]

    arriving = [pltpu.make_async_copy(rows((lo_h, gi_h), i), hold.at[i], sem_in.at[i]) for i in range(16)]
    parts = [
        pltpu.make_async_copy(src, dst, sem_in.at[16 + i])
        for i, (src, dst) in enumerate(((small_h, small), (ga_h, ga), (gf_h, gf)))
    ]
    leaving = [pltpu.make_async_copy(hold.at[i], rows(outs, i), sem_out.at[i]) for i in range(16)]
    packed = [
        pltpu.make_async_copy(hand[i], outs[2 + i], sem_out.at[16 + i]) for i in range(10)
    ]
    for cp in parts + arriving:
        cp.start()
    for cp in parts:
        cp.wait()
    s1, s2, sb, q, k, v, o, g, u, d = hand
    s1[...] = small[0:1, 0:D].reshape(D)
    s2[...] = small[1:2, 0:D].reshape(D)
    sb[...] = small[2:8, 0:32]
    for n, ref in enumerate((q, k, v, o)):
        ref[...] = ga[3 * n : 3 * n + 3, 0:D]
    for n, ref in enumerate((g, u, d)):
        ref[...] = gf[n, 0:46]
    for cp in packed:
        cp.start()
    for i in range(16):
        arriving[i].wait()
        leaving[i].start()
    for cp in packed + leaving:
        cp.wait()


def finish(*args):
    V = pltpu.VMEM
    shapes = ((D,),) * 2 + ((6, 32),) + ((3, D),) * 4 + ((46, FS),) * 3
    return pl.pallas_call(
        finish_kernel,
        name="finish",
        out_shape=(sds((2, D, 128), F32),) * 2 + tuple(sds(s, F32) for s in shapes),
        in_specs=[HB] * 5,
        out_specs=[HB] * 12,
        scratch_shapes=[
            V((8, DP), F32), V((16, DP), F32), V((3, 48, FS), F32), V((16, 368, 128), F32),
            *(V(s, F32) for s in shapes), DMA((19,)), DMA((26,)),
        ],
        compiler_params=pltpu.CompilerParams(vmem_limit_bytes=60 * 2**20),
    )(*args)


def per_device(
    inputs, cotangent, segment_ids, buckets, norm_gain_1, norm_gain_2, relative_bias,
    query_weight, key_weight, value_weight, output_weight, gate_weight, up_weight, down_weight,
):
    stage, feat, heads, outs = make_constants()
    stored = layer(
        query_weight.T, key_weight.T, value_weight.T, output_weight,
        gate_weight, up_weight, down_weight.T,
        segment_ids, buckets, relative_bias.T, norm_gain_1, norm_gain_2, stage,
        jnp.transpose(inputs, (0, 2, 1)), jnp.transpose(cotangent, (0, 2, 1)), feat, heads, outs,
    )
    lo, gi, gain1, gain2, bias, q, k, v, o, gate, up, down = finish(*stored[:5])
    return (
        jnp.transpose(lo, (0, 2, 1)), jnp.transpose(gi, (0, 2, 1)), gain1, gain2, bias.T,
        q.T, k.T, v.T, o, gate, up, down.T,
    )


def solution(mesh):
    every = ("fsdp", "ctx", "tp")
    rows = P("fsdp", ("ctx", "tp"), None)
    wide = P(("fsdp", "ctx"), "tp")
    attn = (P(None, every), P(None, every), P(None, every), P(every, None))
    ffn = (wide, wide, P("tp", ("fsdp", "ctx")))
    return jax.shard_map(
        per_device,
        mesh=mesh,
        in_specs=(rows, rows, P("fsdp", None), P(), P(), P(), P()) + attn + ffn,
        out_specs=(rows, rows, P(), P(), P()) + attn + ffn,
        check_vma=False,
    )
```
